256 devices in a mesh: frame: 32 (over z, y_hi, core), patch: 8 (over x, y_lo).
Axes of the slice: x: 4, y: 4 (y_hi: 2, y_lo: 2; y = y_hi * 2 + y_lo), z: 8, core: 2. Of those that a mesh axis runs over, the one named last changes fastest.
Arguments:
- stream: bfloat16 [64, 880, 1024], P('frame', 'patch'), may hold values from -6 to 6
- spatial_out: bfloat16 [64, 880, 512], P('frame', 'patch'), may hold values from -6 to 6
- spatial_qkv: bfloat16 [64, 880, 1536], P('frame', 'patch'), may hold values from -6 to 6
- upstream: bfloat16 [64, 880, 1024], P('frame', 'patch'), may hold values from -6 to 6
- proj_spatial: bfloat16 [512, 1024], replicated, may hold values from -0.25 to 0.25
- qkv_temporal: bfloat16 [1024, 3072], replicated, may hold values from -0.75 to 0.75
- proj_temporal: bfloat16 [1024, 1024], replicated, may hold values from -0.1875 to 0.1875
- mod_weight: bfloat16 [256, 1024], replicated, may hold values from -0.25 to 0.25
- noise_steps: int32 [64], P('frame'), may hold values from 0 to 999
- positions: int32 [64], replicated, may hold values from 0 to 63, each once
- memory: int32 [64, 4], replicated, may hold values from 0 to 63
Outputs:
- grad_stream: bfloat16 [64, 880, 1024], P('frame', 'patch')
- grad_spatial_qkv: bfloat16 [64, 880, 1536], P('frame', 'patch')
- grad_proj_spatial: float32 [512, 1024], P('frame', 'patch')
- grad_qkv_temporal: float32 [1024, 3072], P('frame', 'patch')
- grad_proj_temporal: float32 [1024, 1024], P('frame', 'patch')
The draws below stay inside these ranges and needn't reach their ends.
All inputs are finite; a program needn't handle non-finite values.
Results may differ from the reference program's by a relative error of at most 0.027.
Values may be sent and summed in bfloat16 or wider, within the bound.
A program may use at most 128 MiB of HBM per device.

```python
import jax
import jax.numpy as jnp
from jax import lax

D = 1024
H = 16
E = 64
HS = 8
P_SIZE = 880
M = 4
TE = 256
F = 64


def draw_spatial_qkv(key, part):
    key = jax.random.fold_in(key, 11)
    full_shape = (F, P_SIZE, 3, HS, E)
    values = jnp.clip(jax.random.normal(key, full_shape, jnp.float32), -6.0, 6.0)
    return values.reshape(F, P_SIZE, 3 * HS * E).astype(jnp.bfloat16)


def draw_qkv_temporal(key, part):
    key = jax.random.fold_in(key, 23)
    full_shape = (D, 3, H, E)
    values = jnp.clip(jax.random.normal(key, full_shape, jnp.float32), -6.0, 6.0) * D ** (-0.5)
    return values.reshape(D, 3 * H * E).astype(jnp.bfloat16)


def touch_ends(array, rng, low, largest):
    index_at = [jax.random.randint(jax.random.fold_in(rng, axis), (), 0, length) for axis, length in enumerate(array.shape)]
    widest = array.shape.index(max(array.shape))
    next_to = index_at[:widest] + [(index_at[widest] + 1) % array.shape[widest]] + index_at[widest + 1:]
    return array.at[tuple(index_at)].set(low).at[tuple(next_to)].set(largest)


def block_scale(own_key, dims, split, smallest, top_value):
    loudness, own = 1.0, jax.random.fold_in(own_key, 6)
    for axis_at, shards_of in split:
        steps = jnp.exp(jax.random.uniform(jax.random.fold_in(own, axis_at), (shards_of,), jnp.float32, smallest / len(split), top_value / len(split)))
        loudness = loudness * jnp.repeat(steps, dims[axis_at] // shards_of).reshape([-1 if axis == axis_at else 1 for axis in range(len(dims))])
    return loudness


def bell_draw(rng, dims, width, most, pieces=(), held_as=jnp.bfloat16):
    loudness = block_scale(rng, dims, pieces, -0.22, 0.18) if pieces else 1.0
    values = jax.random.normal(rng, dims, jnp.float32) * width * loudness
    return jnp.minimum(jnp.maximum(values, -most), most).astype(held_as)


def setup_inputs(seed: int = 0) -> dict:
    keys = jax.random.split(jax.random.key(seed), 12)
    stream = bell_draw(keys[0], (F, P_SIZE, D), 1.0, 6.0, ((0, 32), (1, 8)))
    spatial_out = bell_draw(keys[1], (F, P_SIZE, HS * E), 1.0, 6.0, ((0, 32), (1, 8)))
    spatial_qkv = draw_spatial_qkv(jax.random.fold_in(keys[11], 71), 0)
    upstream = bell_draw(keys[3], (F, P_SIZE, D), 1.0, 6.0, ((0, 32), (1, 8)))
    proj_spatial = bell_draw(keys[4], (HS * E, D), (HS * E) ** -0.5, 0.25)
    qkv_temporal = draw_qkv_temporal(jax.random.fold_in(keys[11], 71), 0)
    proj_temporal = bell_draw(keys[6], (D, D), D ** -0.5, 0.1875)
    mod_weight = bell_draw(keys[7], (TE, D), (2 * TE) ** -0.5, 0.25)
    noise_steps = touch_ends(jax.random.randint(keys[8], (F,), 0, 1000), jax.random.fold_in(keys[8], 1), 0, 999).astype(jnp.int32)
    positions = jax.random.permutation(keys[9], F).astype(jnp.int32)
    memory = touch_ends(jax.random.randint(keys[10], (F, M), 0, F), jax.random.fold_in(keys[10], 1), 0, F - 1).astype(jnp.int32)
    return dict(stream=stream, spatial_out=spatial_out, spatial_qkv=spatial_qkv, upstream=upstream, proj_spatial=proj_spatial, qkv_temporal=qkv_temporal, proj_temporal=proj_temporal, mod_weight=mod_weight, noise_steps=noise_steps, positions=positions, memory=memory)


def frame_embedding(noise_steps, embed_width):
    half_width = embed_width // 2
    counter = jnp.arange(half_width, dtype=jnp.float32)
    frequency = jnp.exp(-jnp.log(10000.0) * counter / half_width)
    angles = noise_steps.astype(jnp.float32)[:, None] * frequency[None, :]
    return jnp.concatenate([jnp.cos(angles), jnp.sin(angles)], axis=1)

def visible_frames(positions, memory):
    frame_total = positions.shape[0]
    earlier = positions[None, :] <= positions[:, None]
    frame_ids = jnp.arange(frame_total, dtype=jnp.int32)
    recalled = jnp.any(memory[:, :, None] == frame_ids[None, None, :], axis=1)
    return jnp.logical_or(earlier, recalled)

def attend_grad(query_matrix_rows, key_matrix_rows, value_matrix_rows, gradient_rows, allowed, logit_scale):
    query_broad = query_matrix_rows.astype(jnp.float32)
    key_broad = key_matrix_rows.astype(jnp.float32)
    value_broad = value_matrix_rows.astype(jnp.float32)
    gradient_broad = gradient_rows.astype(jnp.float32)
    logit_scores = jnp.einsum('hud,hzd->huz', query_broad, key_broad) * logit_scale
    if allowed is not None:
        logit_scores = jnp.where(allowed, logit_scores, -1e+30)
    row_max = lax.optimization_barrier(jnp.max(logit_scores, axis=-1, keepdims=True))
    lifted = jnp.exp(logit_scores - row_max)
    attn_probs = lifted / lax.optimization_barrier(jnp.sum(lifted, axis=-1, keepdims=True))
    probability_narrow = attn_probs.astype(jnp.bfloat16)
    probability_broad = probability_narrow.astype(jnp.float32)
    final_answer = jnp.einsum('rtl,rlp->rtp', probability_broad, value_broad).astype(jnp.bfloat16)
    probability_gradient = jnp.einsum('hud,hzd->huz', gradient_broad, value_broad)
    center = lax.optimization_barrier(jnp.sum(attn_probs * probability_gradient, axis=-1, keepdims=True))
    score_gradient = (attn_probs * (probability_gradient - center) * logit_scale).astype(jnp.bfloat16)
    score_broad = score_gradient.astype(jnp.float32)
    query_gradient = jnp.einsum('rtl,rlp->rtp', score_broad, key_broad).astype(jnp.bfloat16)
    key_gradient = jnp.einsum('pfd,pfn->pdn', score_broad, query_broad).astype(jnp.bfloat16)
    value_gradient = jnp.einsum('pfd,pfn->pdn', probability_broad, gradient_broad).astype(jnp.bfloat16)
    return (final_answer, query_gradient, key_gradient, value_gradient)

def reference(stream, spatial_out, spatial_qkv, upstream, proj_spatial, qkv_temporal, proj_temporal, mod_weight, noise_steps, positions, memory):
    logit_scale = E ** (-0.5)
    token_total = F * P_SIZE
    embedding = frame_embedding(noise_steps, TE).astype(jnp.bfloat16)
    frame_gain = 1.0 + jnp.dot(embedding, mod_weight, preferred_element_type=jnp.float32)
    stream_wide = stream.astype(jnp.float32)
    inverse = lax.rsqrt(lax.optimization_barrier(jnp.mean(stream_wide * stream_wide, axis=-1, keepdims=True)) + 1e-06)
    normed = (stream_wide * inverse * frame_gain[:, None, :]).astype(jnp.bfloat16)
    normed_rows = normed.reshape(token_total, D)
    upstream_rows = upstream.reshape(token_total, D)
    projected = jnp.dot(normed_rows, qkv_temporal, preferred_element_type=jnp.float32).astype(jnp.bfloat16)
    projected = projected.reshape(F, P_SIZE, 3, H, E)
    grad_out_t = jnp.dot(upstream_rows, proj_temporal.T, preferred_element_type=jnp.float32).astype(jnp.bfloat16)
    grad_out_t = grad_out_t.reshape(F, P_SIZE, H, E)
    allowed = visible_frames(positions, memory)

    def by_head(tensor):
        return jnp.transpose(tensor, (2, 1, 0, 3))

    def temporal_head(items):
        return attend_grad(items[0], items[1], items[2], items[3], allowed, logit_scale)
    temporal = lax.map(temporal_head, (by_head(projected[:, :, 0]), by_head(projected[:, :, 1]), by_head(projected[:, :, 2]), by_head(grad_out_t)))
    temporal_o = by_head(temporal[0]).reshape(token_total, D)
    grad_qkv_rows = jnp.stack([by_head(temporal[1]), by_head(temporal[2]), by_head(temporal[3])], axis=2).reshape(token_total, 3 * D)
    grad_proj_temporal = jnp.dot(temporal_o.T, upstream_rows, preferred_element_type=jnp.float32)
    grad_qkv_temporal = jnp.dot(normed_rows.T, grad_qkv_rows, preferred_element_type=jnp.float32)
    grad_normed = jnp.dot(grad_qkv_rows, qkv_temporal.T, preferred_element_type=jnp.float32).reshape(F, P_SIZE, D)
    scaled = grad_normed * frame_gain[:, None, :]
    inner_mean = lax.optimization_barrier(jnp.mean(stream_wide * scaled, axis=-1, keepdims=True))
    grad_stream = (upstream.astype(jnp.float32) + inverse * scaled - stream_wide * inverse ** 3 * inner_mean).astype(jnp.bfloat16)
    stream_rows = grad_stream.reshape(token_total, D)
    grad_out_s = jnp.dot(stream_rows, proj_spatial.T, preferred_element_type=jnp.float32).astype(jnp.bfloat16)
    grad_out_s = grad_out_s.reshape(F, P_SIZE, HS, E)
    grad_proj_spatial = jnp.dot(spatial_out.reshape(token_total, HS * E).T, stream_rows, preferred_element_type=jnp.float32)
    split_qkv = spatial_qkv.reshape(F, P_SIZE, 3, HS, E)

    def frame_heads(tensor):
        return jnp.transpose(tensor, (0, 2, 1, 3))

    def spatial_frame(items):
        outcome = attend_grad(items[0], items[1], items[2], items[3], None, logit_scale)
        return jnp.stack([outcome[1], outcome[2], outcome[3]], axis=0)
    spatial = lax.map(spatial_frame, (frame_heads(split_qkv[:, :, 0]), frame_heads(split_qkv[:, :, 1]), frame_heads(split_qkv[:, :, 2]), frame_heads(grad_out_s)))
    grad_spatial_qkv = jnp.transpose(spatial, (0, 3, 1, 2, 4)).reshape(F, P_SIZE, 3 * HS * E)
    return (grad_stream, grad_spatial_qkv, grad_proj_spatial, grad_qkv_temporal, grad_proj_temporal)
```

```python
import functools

import jax
import jax.numpy as jnp
from jax import lax
from jax.experimental import pallas as pl
from jax.experimental.pallas import tpu as pltpu
from jax.sharding import PartitionSpec as P

MESH = pl.DeviceIdType.MESH
F32 = jnp.float32
BF16 = jnp.bfloat16
D = 1024
E = 64
F = 64
NF = 32
NP = 8
TOK = 110
PAD = 112
SLOT = 4
BUSY = 28
ROWS = F * SLOT
SP = NP * PAD
SCALE = E ** (-0.5)
NEG = -1e30
VLIMIT = 56 * 1024 * 1024


def frame_embedding(noise_steps, embed_width):
    half_width = embed_width // 2
    counter = jnp.arange(half_width, dtype=jnp.float32)
    frequency = jnp.exp(-jnp.log(10000.0) * counter / half_width)
    angles = noise_steps.astype(jnp.float32)[:, None] * frequency[None, :]
    return jnp.concatenate([jnp.cos(angles), jnp.sin(angles)], axis=1)


def visible_frames(positions, memory):
    frame_total = positions.shape[0]
    earlier = positions[None, :] <= positions[:, None]
    frame_ids = jnp.arange(frame_total, dtype=jnp.int32)
    recalled = jnp.any(memory[:, :, None] == frame_ids[None, None, :], axis=1)
    return jnp.logical_or(earlier, recalled)


def rcopy(src, dst, ssem, rsem, f, p):
    return pltpu.make_async_remote_copy(
        src_ref=src, dst_ref=dst, send_sem=ssem, recv_sem=rsem, device_id=(f, p), device_id_type=MESH
    )


def barrier(me_f, me_p, frame, patch):
    sem = pltpu.get_barrier_semaphore()
    count = 0
    if frame:

        def greet(k, _):
            pl.semaphore_signal(sem, inc=1, device_id=(lax.rem(me_f + k, NF), me_p), device_id_type=MESH)
            return 0

        lax.fori_loop(1, NF, greet, 0)
        count += NF - 1
    if patch:

        def greet_p(k, _):
            pl.semaphore_signal(sem, inc=1, device_id=(me_f, lax.rem(me_p + k, NP)), device_id_type=MESH)
            return 0

        lax.fori_loop(1, NP, greet_p, 0)
        count += NP - 1
    pl.semaphore_wait(sem, count)


def low_rows():
    return lax.broadcasted_iota(jnp.int32, (8, D), 0) < 4


def swap_halves(a, b, low):
    return jnp.where(low, a, pltpu.roll(b, 4, 0)), jnp.where(low, pltpu.roll(a, 4, 0), b)


def swap_lanes(a, b):
    low = lax.broadcasted_iota(jnp.int32, a.shape, 1) < E
    return jnp.where(low, a, pltpu.roll(b, E, 1)), jnp.where(low, pltpu.roll(a, E, 1), b)


def forward_kernel(
    stream, upstream, gain, sqkv, recv, recv_s, nbuf, ubuf, send, send_s, ssem, rsem, ssem_s, rsem_s, lsem
):
    me_f, me_p = lax.axis_index("frame"), lax.axis_index("patch")
    for f in range(2):
        x = stream[f].astype(F32)
        inverse = lax.rsqrt(jnp.mean(x * x, axis=-1, keepdims=True) + 1e-06)
        nbuf[f, 104:128] = jnp.zeros((24, D), F32)
        ubuf[f, 104:128] = jnp.zeros((24, D), F32)
        nbuf[f, 0:TOK] = x * inverse * gain[f : f + 1]
        ubuf[f, 0:TOK] = upstream[f].astype(F32)

    low = low_rows()

    def pack(i, _):
        rows = pl.ds(pl.multiple_of(i * 8, 8), 8)
        n0, n1 = swap_halves(nbuf[0, rows], nbuf[1, rows], low)
        u0, u1 = swap_halves(ubuf[0, rows], ubuf[1, rows], low)
        send[2 * i] = jnp.concatenate([n0, u0], axis=0).astype(BF16)
        send[2 * i + 1] = jnp.concatenate([n1, u1], axis=0).astype(BF16)
        return 0

    lax.fori_loop(0, BUSY // 2, pack, 0)

    @pl.when(me_f >= BUSY)
    def _():
        recv[...] = jnp.zeros(recv.shape, BF16)

    barrier(me_f, me_p, True, True)

    def copy_to(k):
        d = lax.rem(me_f + k, NF)
        return d, rcopy(send.at[d], recv.at[me_f], ssem.at[k], rsem.at[k], d, me_p)

    def start(k, _):
        d, copy = copy_to(k)

        @pl.when(d < BUSY)
        def _():
            copy.start()

        return 0

    lax.fori_loop(1, NF, start, 0)
    local = pltpu.make_async_copy(send.at[me_f], recv.at[me_f], lsem.at[0])

    @pl.when(me_f < BUSY)
    def _():
        local.start()

    send_s[:, :, 96:PAD] = jnp.zeros((NP, 3, 16, 128), BF16)
    for j in range(4):
        v = []
        for f in range(2):
            a = sqkv[f, :, 128 * j : 128 * j + 128].astype(F32)
            b = sqkv[f, :, 512 + 128 * j : 640 + 128 * j].astype(F32)
            m0, m1 = swap_lanes(a, b)
            send_s[2 * j, f, 0:TOK] = m0.astype(BF16)
            send_s[2 * j + 1, f, 0:TOK] = m1.astype(BF16)
            v.append(sqkv[f, :, 1024 + 128 * j : 1152 + 128 * j].astype(F32))
        m0, m1 = swap_lanes(v[0], v[1])
        send_s[2 * j, 2, 0:TOK] = m0.astype(BF16)
        send_s[2 * j + 1, 2, 0:TOK] = m1.astype(BF16)

    def copy_s(k):
        d = lax.rem(me_p + k, NP)
        return rcopy(send_s.at[d], recv_s.at[me_p], ssem_s.at[k], rsem_s.at[k], me_f, d)

    def start_s(k, _):
        copy_s(k).start()
        return 0

    lax.fori_loop(1, NP, start_s, 0)
    recv_s[me_p] = send_s[me_p]

    @pl.when(me_f < BUSY)
    def _():
        local.wait()

    def finish(k, _):
        d, copy = copy_to(k)

        @pl.when(d < BUSY)
        def _():
            copy.wait_send()

        @pl.when(me_f < BUSY)
        def _():
            copy.wait_recv()

        return 0

    lax.fori_loop(1, NF, finish, 0)

    def finish_s(k, _):
        copy_s(k).wait()
        return 0

    lax.fori_loop(1, NP, finish_s, 0)


def dot(a, b, da, db):
    return lax.dot_general(a, b, (((da,), (db,)), ((), ())), preferred_element_type=F32)


def temporal_kernel(recv, wqkv, wp, bias, term_a, term_b, gn, nv, uv, nt, proj, g, o, dqkv, ot):
    x = recv[...].astype(F32)
    nv[...] = x[:, 0:8].reshape(ROWS, D).astype(BF16)
    uv[...] = x[:, 8:16].reshape(ROWS, D).astype(BF16)
    nt[...] = nv[...].T

    def project(c, _):
        cols = pl.ds(pl.multiple_of(c * 512, 512), 512)
        proj[:, cols] = dot(nv[...], wqkv[:, cols], 1, 0).astype(BF16)
        return 0

    lax.fori_loop(0, 6, project, 0)

    def project_g(c, _):
        cols = pl.ds(pl.multiple_of(c * 512, 512), 512)
        g[:, cols] = dot(uv[...], wp[cols, :], 1, 1).astype(BF16)
        return 0

    lax.fori_loop(0, 2, project_g, 0)
    low = lax.broadcasted_iota(jnp.int32, (ROWS, 128), 1) < E

    def pair(j, _):
        def cols(base):
            return pl.ds(pl.multiple_of(base + j * 128, 128), 128)

        qp, kp, vp, gp = proj[:, cols(0)], proj[:, cols(D)], proj[:, cols(2 * D)], g[:, cols(0)]
        parts = []
        for half in range(2):
            mine = low if half == 0 else jnp.logical_not(low)
            zero = jnp.zeros_like(qp)
            kh = jnp.where(mine, kp, zero)
            vh = jnp.where(mine, vp, zero)
            st = dot(kh, qp, 1, 1) * SCALE + bias[...]
            e = jnp.exp(st - jnp.max(st, axis=0, keepdims=True))
            p = e / jnp.sum(e, axis=0, keepdims=True)
            pb = p.astype(BF16)
            dp = dot(vh, gp, 1, 1)
            ds = (p * (dp - jnp.sum(p * dp, axis=0, keepdims=True)) * SCALE).astype(BF16)
            parts.append(
                (dot(pb, vp, 0, 0), dot(ds, kp, 0, 0), dot(ds, qp, 1, 0), dot(pb, gp, 1, 0))
            )
        out = [jnp.where(low, a, b).astype(BF16) for a, b in zip(*parts)]
        o[:, cols(0)] = out[0]
        dqkv[:, cols(0)] = out[1]
        dqkv[:, cols(D)] = out[2]
        dqkv[:, cols(2 * D)] = out[3]
        return 0

    lax.fori_loop(0, 8, pair, 0)
    back = dot(dqkv[...], wqkv[...], 1, 1).reshape(NF, 8, D)
    gn[...] = jnp.concatenate([back[:, :, 0:512], back[:, :, 512:1024]], axis=1).astype(BF16)
    ot[...] = o[...].T

    def weights(p, _):
        r = dot(nt[...], dqkv[:, pl.ds(pl.multiple_of(p * 384, 128), 384)], 1, 0)
        r = r.reshape(16, 2, 32, 384)
        term_a[:, :, p, :, 0:384] = r[:, :, 0:16].astype(BF16)
        term_b[:, :, p, :, 0:384] = r[:, :, 16:32].astype(BF16)
        s = dot(ot[...], uv[:, pl.ds(pl.multiple_of(p * 128, 128), 128)], 1, 0)
        s = s.reshape(16, 2, 32, 128)
        term_a[:, :, p, :, 384:512] = s[:, :, 0:16].astype(BF16)
        term_b[:, :, p, :, 384:512] = s[:, :, 16:32].astype(BF16)
        return 0

    lax.fori_loop(0, NP, weights, 0)


def back_kernel(
    gn, stream, upstream, gain, wps, so, gs_out, recv_g, term_p,
    recv, sbuf, sopad, send_g, ssem, rsem, ssem_g, rsem_g, lsem,
):
    me_f, me_p = lax.axis_index("frame"), lax.axis_index("patch")
    barrier(me_f, me_p, True, True)

    def copy_to(k):
        d = lax.rem(me_f + k, NF)
        return rcopy(gn.at[d], recv.at[me_f], ssem.at[k], rsem.at[k], d, me_p)

    def start(k, _):
        copy_to(k).start()
        return 0

    local = pltpu.make_async_copy(gn.at[me_f], recv.at[me_f], lsem.at[0])

    @pl.when(me_f < BUSY)
    def _():
        lax.fori_loop(1, NF, start, 0)
        local.start()

    for f in range(2):
        sopad[f, 96:PAD] = jnp.zeros((16, 512), BF16)
        sopad[f, 0:TOK] = so[f]

    def land(k, _):
        @pl.when(lax.rem(me_f + NF - k, NF) < BUSY)
        def _():
            copy_to(k).wait_recv()

        return 0

    lax.fori_loop(1, NF, land, 0)

    @pl.when(me_f < BUSY)
    def _():
        local.wait()

    low = low_rows()

    def unpack(i, _):
        rows = pl.ds(pl.multiple_of(i * 8, 8), 8)
        x = recv[2 * i].astype(F32)
        y = recv[2 * i + 1].astype(F32)
        x = jnp.concatenate([x[0:8], x[8:16]], axis=1)
        y = jnp.concatenate([y[0:8], y[8:16]], axis=1)
        sbuf[0, rows], sbuf[1, rows] = swap_halves(x, y, low)
        return 0

    lax.fori_loop(0, BUSY // 2, unpack, 0)
    for f in range(2):
        x = stream[f].astype(F32)
        inverse = lax.rsqrt(jnp.mean(x * x, axis=-1, keepdims=True) + 1e-06)
        scaled = sbuf[f, 0:TOK] * gain[f : f + 1]
        inner = jnp.mean(x * scaled, axis=-1, keepdims=True)
        out = upstream[f].astype(F32) + inverse * scaled - x * (inverse * inverse * inverse) * inner
        gs_out[f] = out.astype(BF16)
        sbuf[f, 104:PAD] = jnp.zeros((8, D), F32)
        sbuf[f, 0:TOK] = out
    gs = sbuf[...].reshape(2 * PAD, D).astype(BF16)
    gos = dot(gs, wps[...], 1, 1)
    for j in range(4):
        cols = slice(128 * j, 128 * j + 128)
        m0, m1 = swap_lanes(gos[0:PAD, cols], gos[PAD : 2 * PAD, cols])
        send_g[2 * j] = m0.astype(BF16)
        send_g[2 * j + 1] = m1.astype(BF16)

    def copy_g(k):
        d = lax.rem(me_p + k, NP)
        return rcopy(send_g.at[d], recv_g.at[me_p], ssem_g.at[k], rsem_g.at[k], me_f, d)

    def start_g(k, _):
        copy_g(k).start()
        return 0

    lax.fori_loop(1, NP, start_g, 0)
    recv_g[me_p] = send_g[me_p]
    tp = dot(sopad[...].reshape(2 * PAD, 512), gs, 0, 0)
    for p in range(NP):
        term_p[:, :, p] = tp[:, 128 * p : 128 * p + 128].reshape(16, 2, 16, 128).astype(BF16)

    def gone(k, _):
        copy_to(k).wait_send()
        return 0

    @pl.when(me_f < BUSY)
    def _():
        lax.fori_loop(1, NF, gone, 0)

    def finish_g(k, _):
        copy_g(k).wait()
        return 0

    lax.fori_loop(1, NP, finish_g, 0)


def spatial_kernel(qkv, gg, out, kq, vz, acc_k, acc_q, acc_v, send, recv, ssem, rsem):
    me_f, me_p = lax.axis_index("frame"), lax.axis_index("patch")
    barrier(me_f, me_p, False, True)
    low = lax.broadcasted_iota(jnp.int32, (SP, 128), 1) < E
    dead = lax.rem(lax.broadcasted_iota(jnp.int32, (SP, 128), 0), PAD) >= TOK
    bias = jnp.where(dead, NEG, 0.0).astype(F32)
    vv = qkv[:, 2].reshape(SP, 128).astype(F32)
    for f in range(2):
        x = qkv[:, f].reshape(SP, 128).astype(F32)
        kq[...] = jnp.where(low, pltpu.roll(x, E, 1), 0.0).astype(BF16)
        vz[...] = jnp.where(low if f == 0 else jnp.logical_not(low), vv, 0.0).astype(BF16)
        acc_k[...] = jnp.zeros((SP, 128), F32)
        acc_v[f] = jnp.zeros((SP, 128), F32)
        qk = x.astype(BF16)
        g_all = gg[...].reshape(SP, 128)
        for b in range(SP // 128):
            rows = slice(b * 128, b * 128 + 128)
            q_rows, g_rows = qk[rows], g_all[rows]
            st = dot(kq[...], q_rows, 1, 1) * SCALE + bias
            e = jnp.exp(st - jnp.max(st, axis=0, keepdims=True))
            p = e / jnp.sum(e, axis=0, keepdims=True)
            dp = dot(vz[...], g_rows, 1, 1)
            ds = (p * (dp - jnp.sum(p * dp, axis=0, keepdims=True)) * SCALE).astype(BF16)
            acc_v[f] += dot(p.astype(BF16), g_rows, 1, 0)
            acc_k[...] += dot(ds, q_rows, 1, 0)
            acc_q[rows] = dot(ds, qk, 0, 0)
        send[:, f] = jnp.where(low, acc_k[...], acc_q[...]).astype(BF16).reshape(NP, PAD, 128)
    send[:, 2] = jnp.where(low, acc_v[0], acc_v[1]).astype(BF16).reshape(NP, PAD, 128)

    def copy_to(k):
        d = lax.rem(me_p + k, NP)
        return rcopy(send.at[d], recv.at[me_p], ssem.at[k], rsem.at[k], me_f, d)

    def start(k, _):
        copy_to(k).start()
        return 0

    lax.fori_loop(1, NP, start, 0)
    recv[me_p] = send[me_p]

    def finish(k, _):
        copy_to(k).wait()
        return 0

    lax.fori_loop(1, NP, finish, 0)
    for j in range(4):
        c = 128 * j
        for f in range(2):
            k, q = swap_lanes(recv[2 * j, f].astype(F32), recv[2 * j + 1, f].astype(F32))
            out[f, :, c : c + 128] = q[0:TOK].astype(BF16)
            out[f, :, 512 + c : 640 + c] = k[0:TOK].astype(BF16)
        v0, v1 = swap_lanes(recv[2 * j, 2].astype(F32), recv[2 * j + 1, 2].astype(F32))
        out[0, :, 1024 + c : 1152 + c] = v0[0:TOK].astype(BF16)
        out[1, :, 1024 + c : 1152 + c] = v1[0:TOK].astype(BF16)


def place():
    me_f, me_p = lax.axis_index("frame"), lax.axis_index("patch")
    z, y_hi, core = me_f // 4, lax.rem(me_f // 2, 2), lax.rem(me_f, 2)
    x, y_lo = me_p // 2, lax.rem(me_p, 2)
    return z, y_hi, core, x, y_lo


def device(z, y, core, x):
    return z * 4 + (y // 2) * 2 + core, x * 2 + lax.rem(y, 2)


def sum_barrier():
    z, y_hi, core, x, y_lo = place()
    y = y_hi * 2 + y_lo
    sem = pltpu.get_barrier_semaphore()

    def greet(f, p):
        pl.semaphore_signal(sem, inc=1, device_id=(f, p), device_id_type=MESH)

    greet(*device(z, y, 1 - core, x))
    for k in range(1, 4):
        greet(*device(z, y, core, lax.rem(x + k, 4)))
        greet(*device(z, lax.rem(y + k, 4), core, x))
    for k in range(1, 8):
        greet(*device(lax.rem(z + k, 8), y, core, x))
    pl.semaphore_wait(sem, 14)


class Sum:
    def __init__(self, term, bufs, sems, x_first):
        self.term, self.x_first = term, x_first
        self.r0, self.t1, self.r1, self.t2, self.r2, self.t3, self.r3 = bufs
        self.ssem, self.rsem = sems
        self.z, self.y_hi, self.core, self.x, self.y_lo = place()
        self.y = self.y_hi * 2 + self.y_lo
        self.cols = term.shape[-1]

    def copies(self, stage):
        out = []
        if stage == 0:
            dst = device(self.z, self.y, 1 - self.core, self.x)
            return [rcopy(self.term.at[:, 1 - self.core], self.r0, self.ssem.at[0], self.rsem.at[0], *dst)]
        n = 8 if stage == 3 else 4
        first = {1: 1, 2: 4, 3: 7}[stage]
        for k in range(1, n):
            along_x = (stage == 1) == self.x_first
            if stage == 3:
                to = lax.rem(self.z + k, 8)
                src, dst, where = self.t3.at[to], self.r3.at[k - 1], device(to, self.y, self.core, self.x)
            elif along_x:
                to = lax.rem(self.x + k, 4)
                where = device(self.z, self.y, self.core, to)
                if stage == 1:
                    src, dst = self.t1.at[:, :, to], self.r1.at[k - 1]
                else:
                    src, dst = self.t2.at[:, to], self.r2.at[k - 1]
            else:
                to = lax.rem(self.y + k, 4)
                where = device(self.z, to, self.core, self.x)
                if stage == 1:
                    src, dst = self.t1.at[:, to // 2, :, lax.rem(to, 2)], self.r1.at[k - 1]
                else:
                    src, dst = self.t2.at[:, to // 2, lax.rem(to, 2)], self.r2.at[k - 1]
            s = first + k - 1
            out.append(rcopy(src, dst, self.ssem.at[s], self.rsem.at[s], *where))
        return out

    def start(self, stage):
        for c in self.copies(stage):
            c.start()

    def land(self, stage):
        for c in self.copies(stage):
            c.wait_recv()

    def gone(self):
        for stage in range(4):
            for c in self.copies(stage):
                c.wait_send()

    def add0(self):
        shape = (4, 2, 16, self.cols)

        def body(i, _):
            total = self.term[i, self.core].astype(F32) + self.r0[i].astype(F32)
            self.t1[i // 2, lax.rem(i, 2)] = total.astype(BF16).reshape(shape)
            return 0

        lax.fori_loop(0, 16, body, 0)

    def add1(self):
        def body(i, _):
            if self.x_first:
                total = self.t1[i, :, self.x].astype(F32)
            else:
                total = self.t1[i, self.y_hi, :, self.y_lo].astype(F32)
            for k in range(3):
                total = total + self.r1[k, i].astype(F32)
            self.t2[i] = total.astype(BF16)
            return 0

        lax.fori_loop(0, 8, body, 0)

    def add2(self):
        def body(i, _):
            if self.x_first:
                total = self.t2[i, self.y_hi, self.y_lo].astype(F32)
            else:
                total = self.t2[i, self.x].astype(F32)
            for k in range(3):
                total = total + self.r2[k, i].astype(F32)
            self.t3[i] = total.astype(BF16)
            return 0

        lax.fori_loop(0, 8, body, 0)

    def add3(self):
        total = self.t3[self.z].astype(F32)
        for k in range(7):
            total = total + self.r3[k].astype(F32)
        return total


def sum_scratch(cols, x_first):
    mid = (2, 2) if x_first else (4,)
    return [
        pltpu.VMEM((16, NP, 16, cols), BF16),
        pltpu.VMEM((8, 2, 4, 2, 16, cols), BF16),
        pltpu.VMEM((3, 8) + mid + (16, cols), BF16),
        pltpu.VMEM((8,) + mid + (16, cols), BF16),
        pltpu.VMEM((3, 8, 16, cols), BF16),
        pltpu.VMEM((8, 16, cols), BF16),
        pltpu.VMEM((7, 16, cols), BF16),
        pltpu.SemaphoreType.DMA((14,)),
        pltpu.SemaphoreType.DMA((14,)),
    ]


def sum_kernel(term_a, term_b, term_p, out_q, out_t, out_s, *scratch):
    sums = [
        Sum(term, scratch[9 * i : 9 * i + 7], scratch[9 * i + 7 : 9 * i + 9], x_first)
        for i, (term, x_first) in enumerate(((term_a, True), (term_b, False), (term_p, True)))
    ]
    sum_barrier()
    for s in sums:
        s.start(0)
    for s in sums:
        s.land(0)
        s.add0()
        s.start(1)
    for s in sums:
        s.land(1)
        s.add1()
        s.start(2)
    for s in sums:
        s.land(2)
        s.add2()
        s.start(3)
    for i, s in enumerate(sums):
        s.land(3)
        total = s.add3()
        if i < 2:
            out_q[16 * i : 16 * i + 16] = total[:, 0:384]
            out_t[16 * i : 16 * i + 16] = total[:, 384:512]
        else:
            out_s[...] = total
    for s in sums:
        s.gone()


def call(kernel, outs, scratch, collective_id=None):
    vmem = pl.BlockSpec(memory_space=pltpu.VMEM)
    params = dict(vmem_limit_bytes=VLIMIT)
    if collective_id is not None:
        params.update(collective_id=collective_id, has_side_effects=True)

    def run(*args):
        return pl.pallas_call(
            kernel,
            out_shape=[jax.ShapeDtypeStruct(s, t) for s, t in outs],
            in_specs=[vmem] * len(args),
            out_specs=[vmem] * len(outs),
            scratch_shapes=scratch,
            compiler_params=pltpu.CompilerParams(**params),
        )(*args)

    return run


def shards(
    stream,
    spatial_out,
    spatial_qkv,
    upstream,
    proj_spatial,
    qkv_temporal,
    proj_temporal,
    mod_weight,
    noise_steps,
    positions,
    memory,
):
    dma = pltpu.SemaphoreType.DMA
    embedding = frame_embedding(noise_steps, mod_weight.shape[0]).astype(BF16)
    gain = 1.0 + jnp.dot(embedding, mod_weight, preferred_element_type=F32)
    allowed = visible_frames(positions, memory)
    spread = jnp.repeat(jnp.repeat(allowed.T, SLOT, axis=0), SLOT, axis=1)
    slot = jnp.arange(ROWS, dtype=jnp.int32) % SLOT
    bias = jnp.where(jnp.logical_and(spread, slot[:, None] == slot[None, :]), 0.0, NEG).astype(F32)

    recv, recv_s = call(
        forward_kernel,
        [((NF, 16, D), BF16), ((NP, 3, PAD, 128), BF16)],
        [
            pltpu.VMEM((2, 128, D), F32),
            pltpu.VMEM((2, 128, D), F32),
            pltpu.VMEM((NF, 16, D), BF16),
            pltpu.VMEM((NP, 3, PAD, 128), BF16),
            dma((NF,)),
            dma((NF,)),
            dma((NP,)),
            dma((NP,)),
            dma((1,)),
        ],
        0,
    )(stream, upstream, gain, spatial_qkv)

    term_a, term_b, gn = call(
        temporal_kernel,
        [((16, 2, NP, 16, 512), BF16), ((16, 2, NP, 16, 512), BF16), ((NF, 16, 512), BF16)],
        [
            pltpu.VMEM((ROWS, D), BF16),
            pltpu.VMEM((ROWS, D), BF16),
            pltpu.VMEM((D, ROWS), BF16),
            pltpu.VMEM((ROWS, 3 * D), BF16),
            pltpu.VMEM((ROWS, D), BF16),
            pltpu.VMEM((ROWS, D), BF16),
            pltpu.VMEM((ROWS, 3 * D), BF16),
            pltpu.VMEM((D, ROWS), BF16),
        ],
    )(recv, qkv_temporal, proj_temporal, bias)

    grad_stream, recv_g, term_p = call(
        back_kernel,
        [((2, TOK, D), BF16), ((NP, PAD, 128), BF16), ((16, 2, NP, 16, 128), BF16)],
        [
            pltpu.VMEM((NF, 16, 512), BF16),
            pltpu.VMEM((2, PAD, D), F32),
            pltpu.VMEM((2, PAD, 512), BF16),
            pltpu.VMEM((NP, PAD, 128), BF16),
            dma((NF,)),
            dma((NF,)),
            dma((NP,)),
            dma((NP,)),
            dma((1,)),
        ],
        1,
    )(gn, stream, upstream, gain, proj_spatial, spatial_out)

    (grad_spatial_qkv,) = call(
        spatial_kernel,
        [((2, TOK, 1536), BF16)],
        [
            pltpu.VMEM((SP, 128), BF16),
            pltpu.VMEM((SP, 128), BF16),
            pltpu.VMEM((SP, 128), F32),
            pltpu.VMEM((SP, 128), F32),
            pltpu.VMEM((2, SP, 128), F32),
            pltpu.VMEM((NP, 3, PAD, 128), BF16),
            pltpu.VMEM((NP, 3, PAD, 128), BF16),
            dma((NP,)),
            dma((NP,)),
        ],
        2,
    )(recv_s, recv_g)

    grad_q, grad_t, grad_s = call(
        sum_kernel,
        [((32, 384), F32), ((32, 128), F32), ((16, 128), F32)],
        sum_scratch(512, True) + sum_scratch(512, False) + sum_scratch(128, True),
        3,
    )(term_a, term_b, term_p)
    return (grad_stream, grad_spatial_qkv, grad_s, grad_q, grad_t)


def solution(mesh):
    in_specs = (
        P("frame", "patch", None),
        P("frame", "patch", None),
        P("frame", "patch", None),
        P("frame", "patch", None),
        P(),
        P(),
        P(),
        P(),
        P("frame"),
        P(),
        P(),
    )
    out_specs = (
        P("frame", "patch", None),
        P("frame", "patch", None),
        P("frame", "patch"),
        P("frame", "patch"),
        P("frame", "patch"),
    )
    return jax.shard_map(shards, mesh=mesh, in_specs=in_specs, out_specs=out_specs, check_vma=False)
```

```python
import functools

import jax
import jax.numpy as jnp
from jax import lax
from jax.experimental import pallas as pl
from jax.experimental.pallas import tpu as pltpu
from jax.sharding import PartitionSpec as P

MESH = pl.DeviceIdType.MESH
F32 = jnp.float32
BF16 = jnp.bfloat16
D = 1024
E = 64
F = 64
NF = 32
NP = 8
TOK = 110
PAD = 112
SLOT = 4
BUSY = 28
ROWS = F * SLOT
SP = NP * PAD
SCALE = E ** (-0.5)
NEG = -1e30
VLIMIT = 61 * 1024 * 1024


def frame_embedding(noise_steps, embed_width):
    half_width = embed_width // 2
    counter = jnp.arange(half_width, dtype=jnp.float32)
    frequency = jnp.exp(-jnp.log(10000.0) * counter / half_width)
    angles = noise_steps.astype(jnp.float32)[:, None] * frequency[None, :]
    return jnp.concatenate([jnp.cos(angles), jnp.sin(angles)], axis=1)


def visible_frames(positions, memory):
    frame_total = positions.shape[0]
    earlier = positions[None, :] <= positions[:, None]
    frame_ids = jnp.arange(frame_total, dtype=jnp.int32)
    recalled = jnp.any(memory[:, :, None] == frame_ids[None, None, :], axis=1)
    return jnp.logical_or(earlier, recalled)


def rcopy(src, dst, ssem, rsem, f, p):
    return pltpu.make_async_remote_copy(
        src_ref=src, dst_ref=dst, send_sem=ssem, recv_sem=rsem, device_id=(f, p), device_id_type=MESH
    )


def low_rows():
    return lax.broadcasted_iota(jnp.int32, (8, D), 0) < 4


def swap_halves(a, b, low):
    return jnp.where(low, a, pltpu.roll(b, 4, 0)), jnp.where(low, pltpu.roll(a, 4, 0), b)


def swap_lanes(a, b):
    low = lax.broadcasted_iota(jnp.int32, a.shape, 1) < E
    return jnp.where(low, a, pltpu.roll(b, E, 1)), jnp.where(low, pltpu.roll(a, E, 1), b)


def dot(a, b, da, db):
    return lax.dot_general(a, b, (((da,), (db,)), ((), ())), preferred_element_type=F32)


def place():
    me_f, me_p = lax.axis_index("frame"), lax.axis_index("patch")
    z, y_hi, core = me_f // 4, lax.rem(me_f // 2, 2), lax.rem(me_f, 2)
    x, y_lo = me_p // 2, lax.rem(me_p, 2)
    return z, y_hi, core, x, y_lo


def device(z, y, core, x):
    return z * 4 + (y // 2) * 2 + core, x * 2 + lax.rem(y, 2)


def barrier():
    me_f, me_p = lax.axis_index("frame"), lax.axis_index("patch")
    z, y_hi, core, x, y_lo = place()
    y = y_hi * 2 + y_lo
    sem = pltpu.get_barrier_semaphore()

    def greet(f, p):
        pl.semaphore_signal(sem, inc=1, device_id=(f, p), device_id_type=MESH)

    def frames(k, _):
        greet(lax.rem(me_f + k, NF), me_p)
        return 0

    lax.fori_loop(1, NF, frames, 0)

    def patches(k, _):
        greet(me_f, lax.rem(me_p + k, NP))
        return 0

    lax.fori_loop(1, NP, patches, 0)
    greet(*device(z, lax.rem(y + 1, 4), core, x))
    greet(*device(z, lax.rem(y + 3, 4), core, x))
    pl.semaphore_wait(sem, NF + NP)


class Exchange:
    def __init__(self, src, dst, sems, along_frame, sends=None, takes=None):
        self.src, self.dst, (self.ssem, self.rsem) = src, dst, sems
        self.along_frame, self.sends, self.takes = along_frame, sends, takes
        self.me_f, self.me_p = lax.axis_index("frame"), lax.axis_index("patch")
        self.n = NF if along_frame else NP
        self.me = self.me_f if along_frame else self.me_p

    def copy(self, k):
        to = lax.rem(self.me + k, self.n)
        where = (to, self.me_p) if self.along_frame else (self.me_f, to)
        return rcopy(self.src.at[to], self.dst.at[self.me], self.ssem.at[k], self.rsem.at[k], *where)

    def each(self, act, wanted):
        def body(k, _):
            if wanted is None:
                act(self.copy(k))
            else:

                @pl.when(wanted(k))
                def _():
                    act(self.copy(k))

            return 0

        lax.fori_loop(1, self.n, body, 0)

    def start(self):
        self.each(lambda c: c.start(), self.sends)

    def land(self):
        self.each(lambda c: c.wait_recv(), self.takes)

    def gone(self):
        self.each(lambda c: c.wait_send(), self.sends)


class Sum:
    def __init__(self, term, bufs, x_first):
        self.term, self.x_first = term, x_first
        (self.r0, self.t2, self.t3, self.in1, self.up1, self.full1, self.in2, self.up2, self.full2, self.r3,
         self.ssem, self.rsem) = bufs
        self.z, self.y_hi, self.core, self.x, self.y_lo = place()
        self.y = self.y_hi * 2 + self.y_lo
        self.cols = term.shape[-1]

    def chunk(self, stage, j):
        if stage == 1:
            if self.x_first:
                return self.term.at[:, :, self.core, j]
            return self.term.at[:, j // 2, self.core, :, lax.rem(j, 2)]
        if self.x_first:
            return self.t2.at[:, j // 2, lax.rem(j, 2)]
        return self.t2.at[:, j]

    def ring(self, stage):
        if (stage == 1) == self.x_first:
            return self.x, lambda j: device(self.z, self.y, self.core, j)
        return self.y, lambda j: device(self.z, j, self.core, self.x)

    def core_copy(self, x, y_lo):
        other = 1 - self.core
        s = x * 2 + y_lo
        return rcopy(
            self.term.at[:, :, other, x, y_lo], self.r0.at[:, :, x, y_lo], self.ssem.at[s], self.rsem.at[s],
            *device(self.z, self.y, other, self.x),
        )

    def core_add(self, x, y_lo):
        self.core_copy(x, y_lo).wait_recv()

        def body(z, _):
            mine = self.term[z, :, self.core, x, y_lo].astype(F32)
            self.term[z, :, self.core, x, y_lo] = (mine + self.r0[z, :, x, y_lo].astype(F32)).astype(BF16)
            return 0

        lax.fori_loop(0, 8, body, 0)

    def first(self, stage):
        me, at = self.ring(stage)
        far = lax.rem(me + 2, 4)
        into = self.in1 if stage == 1 else self.in2
        s = 8 if stage == 1 else 12
        return [
            rcopy(
                self.chunk(stage, far).at[4 * h : 4 * h + 4], into.at[h], self.ssem.at[s + h], self.rsem.at[s + h],
                *at(lax.rem(me + (1, 3)[h], 4)),
            )
            for h in range(2)
        ]

    def second(self, stage):
        me, at = self.ring(stage)
        up = self.up1 if stage == 1 else self.up2
        full = self.full1 if stage == 1 else self.full2
        s = 10 if stage == 1 else 14
        return [
            rcopy(up.at[h], full.at[h], self.ssem.at[s + h], self.rsem.at[s + h], *at(lax.rem(me + (1, 3)[h], 4)))
            for h in range(2)
        ]

    def relay(self, stage):
        me, _ = self.ring(stage)
        into = self.in1 if stage == 1 else self.in2
        up = self.up1 if stage == 1 else self.up2
        firsts, seconds = self.first(stage), self.second(stage)
        for h in range(2):
            mine = self.chunk(stage, lax.rem(me + (1, 3)[h], 4))
            firsts[h].wait_recv()

            def body(z, _):
                a = 4 * h + z
                b = 4 * (1 - h) + z
                up[h, a] = (mine[a].astype(F32) + into[h, z].astype(F32)).astype(BF16)
                up[h, b] = mine[b]
                return 0

            lax.fori_loop(0, 4, body, 0)
            seconds[h].start()

    def ring_add(self, stage):
        me, _ = self.ring(stage)
        full = self.full1 if stage == 1 else self.full2
        out = self.t2 if stage == 1 else self.t3
        mine = self.chunk(stage, me)
        for c in self.second(stage):
            c.wait_recv()

        def body(z, _):
            total = mine[z].astype(F32) + full[0, z].astype(F32) + full[1, z].astype(F32)
            out[z] = total.astype(BF16)
            return 0

        lax.fori_loop(0, 8, body, 0)

    def last(self):
        out = []
        for k in range(1, 8):
            to = lax.rem(self.z + k, 8)
            out.append(
                rcopy(
                    self.t3.at[to], self.r3.at[k - 1], self.ssem.at[15 + k], self.rsem.at[15 + k],
                    *device(to, self.y, self.core, self.x),
                )
            )
        return out

    def total(self):
        total = self.t3[self.z].astype(F32)
        for c in self.last():
            c.wait_recv()
        for k in range(7):
            total = total + self.r3[k].astype(F32)
        return total

    def start(self, copies):
        for c in copies:
            c.start()

    def gone(self):
        for x in range(4):
            for y_lo in range(2):
                self.core_copy(x, y_lo).wait_send()
        for c in self.first(1) + self.second(1) + self.first(2) + self.second(2) + self.last():
            c.wait_send()


def sum_scratch(cols, x_first):
    mid = (2, 2) if x_first else (4,)
    tile = (16, cols)
    return [
        pltpu.VMEM((8, 2, 4, 2) + tile, BF16),
        pltpu.VMEM((8,) + mid + tile, BF16),
        pltpu.VMEM((8,) + tile, BF16),
        pltpu.VMEM((2, 4) + mid + tile, BF16),
        pltpu.VMEM((2, 8) + mid + tile, BF16),
        pltpu.VMEM((2, 8) + mid + tile, BF16),
        pltpu.VMEM((2, 4) + tile, BF16),
        pltpu.VMEM((2, 8) + tile, BF16),
        pltpu.VMEM((2, 8) + tile, BF16),
        pltpu.VMEM((7,) + tile, BF16),
        pltpu.SemaphoreType.DMA((23,)),
        pltpu.SemaphoreType.DMA((23,)),
    ]


NSUM = 12


def whole_kernel(
    stream, upstream, so, sqkv, gain, pos, memo, wqkv_hbm, wp_hbm, wps_hbm,
    gs_out, out, out_q, out_t, out_s,
    wqkv, wp, wps, wsem,
    nbuf, ubuf, send, recv, ssem, rsem, lsem,
    send_s, recv_s, ssem_s, rsem_s,
    bias, nv, uv, nt, proj, g, o, dqkv, ot,
    gn, recv_gn, ssem_n, rsem_n,
    sopad, send_g, recv_g, ssem_g, rsem_g,
    kq, probs, send_b, recv_b, ssem_b, rsem_b,
    term_a, term_b, term_p, *sum_bufs,
):
    me_f, me_p = lax.axis_index("frame"), lax.axis_index("patch")
    owner = me_f < BUSY
    loads = [
        pltpu.make_async_copy(wqkv_hbm, wqkv, wsem.at[0]),
        pltpu.make_async_copy(wp_hbm, wp, wsem.at[1]),
        pltpu.make_async_copy(wps_hbm, wps, wsem.at[2]),
    ]
    for c in loads:
        c.start()
    sums = [
        Sum(term, sum_bufs[NSUM * i : NSUM * i + NSUM], x_first)
        for i, (term, x_first) in enumerate(((term_a, True), (term_b, False), (term_p, True)))
    ]
    sum_a, sum_b, sum_p = sums

    for f in range(2):
        x = stream[f].astype(F32)
        inverse = lax.rsqrt(jnp.mean(x * x, axis=-1, keepdims=True) + 1e-06)
        nbuf[f, 104:PAD] = jnp.zeros((8, D), F32)
        ubuf[f, 104:PAD] = jnp.zeros((8, D), F32)
        nbuf[f, 0:TOK] = x * inverse * gain[f : f + 1]
        ubuf[f, 0:TOK] = upstream[f].astype(F32)

    low8 = low_rows()

    def pack(i, _):
        rows = pl.ds(pl.multiple_of(i * 8, 8), 8)
        n0, n1 = swap_halves(nbuf[0, rows], nbuf[1, rows], low8)
        u0, u1 = swap_halves(ubuf[0, rows], ubuf[1, rows], low8)
        send[2 * i] = jnp.concatenate([n0, u0], axis=0).astype(BF16)
        send[2 * i + 1] = jnp.concatenate([n1, u1], axis=0).astype(BF16)
        return 0

    lax.fori_loop(0, BUSY // 2, pack, 0)

    @pl.when(jnp.logical_not(owner))
    def _():
        recv[...] = jnp.zeros(recv.shape, BF16)

    barrier()
    out_x = Exchange(
        send, recv, (ssem, rsem), True, lambda k: lax.rem(me_f + k, NF) < BUSY, lambda k: owner
    )
    out_x.start()
    local = pltpu.make_async_copy(send.at[me_f], recv.at[me_f], lsem.at[0])

    @pl.when(owner)
    def _():
        local.start()

    send_s[:, :, 96:PAD] = jnp.zeros((NP, 3, 16, 128), BF16)
    for j in range(4):
        v = []
        for f in range(2):
            a = sqkv[f, :, 128 * j : 128 * j + 128].astype(F32)
            b = sqkv[f, :, 512 + 128 * j : 640 + 128 * j].astype(F32)
            m0, m1 = swap_lanes(a, b)
            send_s[2 * j, f, 0:TOK] = m0.astype(BF16)
            send_s[2 * j + 1, f, 0:TOK] = m1.astype(BF16)
            v.append(sqkv[f, :, 1024 + 128 * j : 1152 + 128 * j].astype(F32))
        m0, m1 = swap_lanes(v[0], v[1])
        send_s[2 * j, 2, 0:TOK] = m0.astype(BF16)
        send_s[2 * j + 1, 2, 0:TOK] = m1.astype(BF16)
    head_x = Exchange(send_s, recv_s, (ssem_s, rsem_s), False)
    head_x.start()
    recv_s[me_p] = send_s[me_p]
    for f in range(2):
        sopad[f, 96:PAD] = jnp.zeros((16, 512), BF16)
        sopad[f, 0:TOK] = so[f]

    def frame_of(i):
        return (i // 8) * 2 + lax.rem(i, 8) // 4

    table = jnp.concatenate(
        [pos[...].astype(F32), memo[...].astype(F32), jnp.zeros((3, F), F32)], axis=0
    ).astype(BF16)
    at_col = (
        lax.broadcasted_iota(jnp.int32, (F, ROWS), 0) == frame_of(lax.broadcasted_iota(jnp.int32, (F, ROWS), 1))
    )
    at_row = (
        lax.broadcasted_iota(jnp.int32, (ROWS, F), 1) == frame_of(lax.broadcasted_iota(jnp.int32, (ROWS, F), 0))
    )
    asked = dot(table, jnp.where(at_col, 1.0, 0.0).astype(BF16), 1, 0)
    held = dot(jnp.where(at_row, 1.0, 0.0).astype(BF16), table, 1, 1)
    key = lax.broadcasted_iota(jnp.int32, (ROWS, ROWS), 0)
    key_frame = frame_of(key).astype(F32)
    seen = held[:, 0:1] <= asked[0:1]
    for m in range(4):
        seen = jnp.logical_or(seen, key_frame == asked[1 + m : 2 + m])
    same = lax.rem(key, SLOT) == lax.rem(lax.broadcasted_iota(jnp.int32, (ROWS, ROWS), 1), SLOT)
    bias[...] = jnp.where(jnp.logical_and(seen, same), 0.0, NEG).astype(F32)

    head_x.land()
    low = lax.broadcasted_iota(jnp.int32, (SP, 128), 1) < E
    dead = lax.rem(lax.broadcasted_iota(jnp.int32, (SP, 128), 0), PAD) >= TOK
    dead_bias = jnp.where(dead, NEG, 0.0).astype(F32)
    for f in range(2):
        x = recv_s[:, f].reshape(SP, 128).astype(F32)
        kq[...] = jnp.where(low, pltpu.roll(x, E, 1), 0.0).astype(BF16)
        for b in range(SP // 128):
            rows = slice(b * 128, b * 128 + 128)
            st = dot(kq[...], x[rows].astype(BF16), 1, 1) * SCALE + dead_bias
            e = jnp.exp(st - jnp.max(st, axis=0, keepdims=True))
            probs[f, :, rows] = (e / jnp.sum(e, axis=0, keepdims=True)).astype(BF16)

    out_x.land()

    @pl.when(owner)
    def _():
        local.wait()

    for c in loads:
        c.wait()
    x = recv[...].astype(F32)
    nv[...] = x[:, 0:8].reshape(ROWS, D).astype(BF16)
    uv[...] = x[:, 8:16].reshape(ROWS, D).astype(BF16)
    nt[...] = nv[...].T

    def project(c, _):
        cols = pl.ds(pl.multiple_of(c * 512, 512), 512)
        proj[:, cols] = dot(nv[...], wqkv[:, cols], 1, 0).astype(BF16)
        return 0

    lax.fori_loop(0, 6, project, 0)

    def project_g(c, _):
        cols = pl.ds(pl.multiple_of(c * 512, 512), 512)
        g[:, cols] = dot(uv[...], wp[cols, :], 1, 1).astype(BF16)
        return 0

    lax.fori_loop(0, 2, project_g, 0)
    low_t = lax.broadcasted_iota(jnp.int32, (ROWS, 128), 1) < E

    def pair(j, _):
        def cols(base):
            return pl.ds(pl.multiple_of(base + j * 128, 128), 128)

        qp, kp, vp, gp = proj[:, cols(0)], proj[:, cols(D)], proj[:, cols(2 * D)], g[:, cols(0)]
        parts = []
        for half in range(2):
            mine = low_t if half == 0 else jnp.logical_not(low_t)
            zero = jnp.zeros_like(qp)
            kh = jnp.where(mine, kp, zero)
            vh = jnp.where(mine, vp, zero)
            st = dot(kh, qp, 1, 1) * SCALE + bias[...]
            e = jnp.exp(st - jnp.max(st, axis=0, keepdims=True))
            p = e / jnp.sum(e, axis=0, keepdims=True)
            pb = p.astype(BF16)
            dp = dot(vh, gp, 1, 1)
            ds = (p * (dp - jnp.sum(p * dp, axis=0, keepdims=True)) * SCALE).astype(BF16)
            parts.append(
                (dot(pb, vp, 0, 0), dot(ds, kp, 0, 0), dot(ds, qp, 1, 0), dot(pb, gp, 1, 0))
            )
        res = [jnp.where(low_t, a, b).astype(BF16) for a, b in zip(*parts)]
        o[:, cols(0)] = res[0]
        dqkv[:, cols(0)] = res[1]
        dqkv[:, cols(D)] = res[2]
        dqkv[:, cols(2 * D)] = res[3]
        return 0

    lax.fori_loop(0, 8, pair, 0)
    back = dot(dqkv[...], wqkv[...], 1, 1).reshape(NF, 8, D)
    gn[...] = jnp.concatenate([back[:, :, 0:512], back[:, :, 512:1024]], axis=1).astype(BF16)

    back_x = Exchange(
        gn, recv_gn, (ssem_n, rsem_n), True, lambda k: owner, lambda k: lax.rem(me_f + NF - k, NF) < BUSY
    )
    back_x.start()
    local_n = pltpu.make_async_copy(gn.at[me_f], recv_gn.at[me_f], lsem.at[1])

    @pl.when(owner)
    def _():
        local_n.start()

    ot[...] = o[...].T

    def weights(p, _):
        x, y_lo = p // 2, lax.rem(p, 2)
        r = dot(nt[...], dqkv[:, pl.ds(pl.multiple_of(p * 384, 128), 384)], 1, 0)
        r = r.reshape(8, 2, 2, 32, 384)
        s = dot(ot[...], uv[:, pl.ds(pl.multiple_of(p * 128, 128), 128)], 1, 0)
        s = s.reshape(8, 2, 2, 32, 128)
        term_a[:, :, :, x, y_lo, :, 0:384] = r[:, :, :, 0:16].astype(BF16)
        term_a[:, :, :, x, y_lo, :, 384:512] = s[:, :, :, 0:16].astype(BF16)
        sum_a.core_copy(x, y_lo).start()
        term_b[:, :, :, x, y_lo, :, 0:384] = r[:, :, :, 16:32].astype(BF16)
        term_b[:, :, :, x, y_lo, :, 384:512] = s[:, :, :, 16:32].astype(BF16)
        sum_b.core_copy(x, y_lo).start()
        return 0

    lax.fori_loop(0, NP, weights, 0)

    def cores(p, _):
        x, y_lo = p // 2, lax.rem(p, 2)
        sum_a.core_add(x, y_lo)
        sum_b.core_add(x, y_lo)
        return 0

    lax.fori_loop(0, NP, cores, 0)
    for s in (sum_a, sum_b):
        s.start(s.first(1))

    back_x.land()

    @pl.when(owner)
    def _():
        local_n.wait()

    def unpack(i, _):
        rows = pl.ds(pl.multiple_of(i * 8, 8), 8)
        x = recv_gn[2 * i].astype(F32)
        y = recv_gn[2 * i + 1].astype(F32)
        x = jnp.concatenate([x[0:8], x[8:16]], axis=1)
        y = jnp.concatenate([y[0:8], y[8:16]], axis=1)
        nbuf[0, rows], nbuf[1, rows] = swap_halves(x, y, low8)
        return 0

    lax.fori_loop(0, BUSY // 2, unpack, 0)
    for f in range(2):
        x = stream[f].astype(F32)
        inverse = lax.rsqrt(jnp.mean(x * x, axis=-1, keepdims=True) + 1e-06)
        scaled = nbuf[f, 0:TOK] * gain[f : f + 1]
        inner = jnp.mean(x * scaled, axis=-1, keepdims=True)
        res = upstream[f].astype(F32) + inverse * scaled - x * (inverse * inverse * inverse) * inner
        gs_out[f] = res.astype(BF16)
        nbuf[f, 104:PAD] = jnp.zeros((8, D), F32)
        nbuf[f, 0:TOK] = res
    gs = nbuf[...].reshape(2 * PAD, D).astype(BF16)
    gos = dot(gs, wps[...], 1, 1)
    for j in range(4):
        cols = slice(128 * j, 128 * j + 128)
        m0, m1 = swap_lanes(gos[0:PAD, cols], gos[PAD : 2 * PAD, cols])
        send_g[2 * j] = m0.astype(BF16)
        send_g[2 * j + 1] = m1.astype(BF16)
    cot_x = Exchange(send_g, recv_g, (ssem_g, rsem_g), False)
    cot_x.start()
    recv_g[me_p] = send_g[me_p]
    tp = dot(sopad[...].reshape(2 * PAD, 512), gs, 0, 0)
    for p in range(NP):
        term_p[:, :, :, p // 2, p % 2] = tp[:, 128 * p : 128 * p + 128].reshape(8, 2, 2, 16, 128).astype(BF16)
        sum_p.core_copy(p // 2, p % 2).start()
    for s in (sum_a, sum_b):
        s.relay(1)
    for p in range(NP):
        sum_p.core_add(p // 2, p % 2)
    sum_p.start(sum_p.first(1))

    cot_x.land()
    g_all = recv_g[...].reshape(SP, 128)
    v_all = recv_s[:, 2].reshape(SP, 128).astype(F32)
    dvs = []
    for f in range(2):
        dvs.append(dot(probs[f], g_all, 1, 0))
        qk = recv_s[:, f].reshape(SP, 128)
        kq[...] = jnp.where(low if f == 0 else jnp.logical_not(low), v_all, 0.0).astype(BF16)
        for b in range(SP // 128):
            rows = slice(b * 128, b * 128 + 128)
            p = probs[f, :, rows].astype(F32)
            dp = dot(kq[...], g_all[rows], 1, 1)
            ds = p * (dp - jnp.sum(p * dp, axis=0, keepdims=True)) * SCALE
            probs[f, :, rows] = ds.astype(BF16)
        dk = dot(probs[f], qk, 1, 0)
        dq = dot(probs[f], qk, 0, 0)
        send_b[:, f] = jnp.where(low, dk, dq).astype(BF16).reshape(NP, PAD, 128)
        if f == 0:
            for s in (sum_a, sum_b):
                s.ring_add(1)
                s.start(s.first(2))
            sum_p.relay(1)
    send_b[:, 2] = jnp.where(low, dvs[0], dvs[1]).astype(BF16).reshape(NP, PAD, 128)
    token_x = Exchange(send_b, recv_b, (ssem_b, rsem_b), False)
    token_x.start()
    recv_b[me_p] = send_b[me_p]
    for s in (sum_a, sum_b):
        s.relay(2)
    sum_p.ring_add(1)
    sum_p.start(sum_p.first(2))
    for s in (sum_a, sum_b):
        s.ring_add(2)
        s.start(s.last())
    sum_p.relay(2)
    sum_p.ring_add(2)
    sum_p.start(sum_p.last())

    token_x.land()
    for j in range(4):
        c = 128 * j
        for f in range(2):
            k, q = swap_lanes(recv_b[2 * j, f].astype(F32), recv_b[2 * j + 1, f].astype(F32))
            out[f, :, c : c + 128] = q[0:TOK].astype(BF16)
            out[f, :, 512 + c : 640 + c] = k[0:TOK].astype(BF16)
        v0, v1 = swap_lanes(recv_b[2 * j, 2].astype(F32), recv_b[2 * j + 1, 2].astype(F32))
        out[0, :, 1024 + c : 1152 + c] = v0[0:TOK].astype(BF16)
        out[1, :, 1024 + c : 1152 + c] = v1[0:TOK].astype(BF16)
    for i, s in enumerate((sum_a, sum_b)):
        total = s.total()
        out_q[16 * i : 16 * i + 16] = total[:, 0:384]
        out_t[16 * i : 16 * i + 16] = total[:, 384:512]
    out_s[...] = sum_p.total()
    out_x.gone()
    head_x.gone()
    back_x.gone()
    cot_x.gone()
    token_x.gone()
    for s in sums:
        s.gone()


def hand_over(q, t, s, out_q, out_t, out_s):
    out_q[...] = q[...]
    out_t[...] = t[...]
    out_s[...] = s[...]


def shards(
    stream,
    spatial_out,
    spatial_qkv,
    upstream,
    proj_spatial,
    qkv_temporal,
    proj_temporal,
    mod_weight,
    noise_steps,
    positions,
    memory,
):
    embedding = frame_embedding(noise_steps, mod_weight.shape[0]).astype(BF16)
    gain = 1.0 + jnp.dot(embedding, mod_weight, preferred_element_type=F32)
    vmem = pl.BlockSpec(memory_space=pltpu.VMEM)
    hbm = pl.BlockSpec(memory_space=pl.ANY)

    def pair_of(n):
        return [pltpu.SemaphoreType.DMA((n,)), pltpu.SemaphoreType.DMA((n,))]

    small = [((32, 384), F32), ((32, 128), F32), ((16, 128), F32)]
    outs = [((2, TOK, D), BF16), ((2, TOK, 1536), BF16)] + small
    scratch = (
        [
            pltpu.VMEM((D, 3 * D), BF16),
            pltpu.VMEM((D, D), BF16),
            pltpu.VMEM((512, D), BF16),
            pltpu.SemaphoreType.DMA((3,)),
            pltpu.VMEM((2, PAD, D), F32),
            pltpu.VMEM((2, PAD, D), F32),
            pltpu.VMEM((NF, 16, D), BF16),
            pltpu.VMEM((NF, 16, D), BF16),
        ]
        + pair_of(NF)
        + [
            pltpu.SemaphoreType.DMA((2,)),
            pltpu.VMEM((NP, 3, PAD, 128), BF16),
            pltpu.VMEM((NP, 3, PAD, 128), BF16),
        ]
        + pair_of(NP)
        + [
            pltpu.VMEM((ROWS, ROWS), F32),
            pltpu.VMEM((ROWS, D), BF16),
            pltpu.VMEM((ROWS, D), BF16),
            pltpu.VMEM((D, ROWS), BF16),
            pltpu.VMEM((ROWS, 3 * D), BF16),
            pltpu.VMEM((ROWS, D), BF16),
            pltpu.VMEM((ROWS, D), BF16),
            pltpu.VMEM((ROWS, 3 * D), BF16),
            pltpu.VMEM((D, ROWS), BF16),
            pltpu.VMEM((NF, 16, 512), BF16),
            pltpu.VMEM((NF, 16, 512), BF16),
        ]
        + pair_of(NF)
        + [
            pltpu.VMEM((2, PAD, 512), BF16),
            pltpu.VMEM((NP, PAD, 128), BF16),
            pltpu.VMEM((NP, PAD, 128), BF16),
        ]
        + pair_of(NP)
        + [
            pltpu.VMEM((SP, 128), BF16),
            pltpu.VMEM((2, SP, SP), BF16),
            pltpu.VMEM((NP, 3, PAD, 128), BF16),
            pltpu.VMEM((NP, 3, PAD, 128), BF16),
        ]
        + pair_of(NP)
        + [
            pltpu.VMEM((8, 2, 2, 4, 2, 16, 512), BF16),
            pltpu.VMEM((8, 2, 2, 4, 2, 16, 512), BF16),
            pltpu.VMEM((8, 2, 2, 4, 2, 16, 128), BF16),
        ]
        + sum_scratch(512, True)
        + sum_scratch(512, False)
        + sum_scratch(128, True)
    )
    grad_stream, grad_spatial_qkv, *totals = pl.pallas_call(
        whole_kernel,
        out_shape=[jax.ShapeDtypeStruct(s, t) for s, t in outs],
        in_specs=[vmem] * 7 + [hbm] * 3,
        out_specs=[vmem] * 5,
        scratch_shapes=scratch,
        compiler_params=pltpu.CompilerParams(vmem_limit_bytes=VLIMIT, collective_id=0, has_side_effects=True),
    )(
        stream,
        upstream,
        spatial_out,
        spatial_qkv,
        gain,
        positions.reshape(1, F),
        memory.T,
        qkv_temporal,
        proj_temporal,
        proj_spatial,
    )
    grad_q, grad_t, grad_s = pl.pallas_call(
        hand_over,
        out_shape=[jax.ShapeDtypeStruct(s, t) for s, t in small],
        in_specs=[vmem] * 3,
        out_specs=[vmem] * 3,
    )(*totals)
    return (grad_stream, grad_spatial_qkv, grad_s, grad_q, grad_t)


def solution(mesh):
    in_specs = (
        P("frame", "patch", None),
        P("frame", "patch", None),
        P("frame", "patch", None),
        P("frame", "patch", None),
        P(),
        P(),
        P(),
        P(),
        P("frame"),
        P(),
        P(),
    )
    out_specs = (
        P("frame", "patch", None),
        P("frame", "patch", None),
        P("frame", "patch"),
        P("frame", "patch"),
        P("frame", "patch"),
    )
    return jax.shard_map(shards, mesh=mesh, in_specs=in_specs, out_specs=out_specs, check_vma=False)
```

```python
import functools

import jax
import jax.numpy as jnp
from jax import lax
from jax.experimental import pallas as pl
from jax.experimental.pallas import tpu as pltpu
from jax.sharding import PartitionSpec as P

MESH = pl.DeviceIdType.MESH
F32 = jnp.float32
BF16 = jnp.bfloat16
D = 1024
E = 64
F = 64
NF = 32
NP = 8
TOK = 110
PAD = 112
SLOT = 4
BUSY = 28
ROWS = F * SLOT
SP = NP * PAD
SCALE = E ** (-0.5)
NEG = -1e30
VLIMIT = 61 * 1024 * 1024


def rcopy(src, dst, ssem, rsem, f, p):
    return pltpu.make_async_remote_copy(
        src_ref=src, dst_ref=dst, send_sem=ssem, recv_sem=rsem, device_id=(f, p), device_id_type=MESH
    )


def swap_halves(a, b):
    axis = a.ndim - 2
    low = lax.broadcasted_iota(jnp.int32, a.shape, axis) < 4
    return jnp.where(low, a, pltpu.roll(b, 4, axis)), jnp.where(low, pltpu.roll(a, 4, axis), b)


def swap_lanes(a, b):
    low = lax.broadcasted_iota(jnp.int32, a.shape, 1) < E
    return jnp.where(low, a, pltpu.roll(b, E, 1)), jnp.where(low, pltpu.roll(a, E, 1), b)


def dot(a, b, da, db):
    return lax.dot_general(a, b, (((da,), (db,)), ((), ())), preferred_element_type=F32)


def place():
    me_f, me_p = lax.axis_index("frame"), lax.axis_index("patch")
    z, y_hi, core = me_f // 4, lax.rem(me_f // 2, 2), lax.rem(me_f, 2)
    x, y_lo = me_p // 2, lax.rem(me_p, 2)
    return z, y_hi, core, x, y_lo


def device(z, y, core, x):
    return z * 4 + (y // 2) * 2 + core, x * 2 + lax.rem(y, 2)


def barrier():
    me_f, me_p = lax.axis_index("frame"), lax.axis_index("patch")
    z, y_hi, core, x, y_lo = place()
    sem = pltpu.get_barrier_semaphore()

    def greet(f, p):
        pl.semaphore_signal(sem, inc=1, device_id=(f, p), device_id_type=MESH)

    def frames(k, _):
        greet(lax.rem(me_f + k, NF), me_p)
        return 0

    lax.fori_loop(1, NF, frames, 0)

    def patches(k, _):
        greet(me_f, lax.rem(me_p + k, NP))
        return 0

    lax.fori_loop(1, NP, patches, 0)

    def across(k, _):
        greet(*device(z, (1 - y_hi) * 2 + lax.rem(k, 2), core, k // 2))
        return 0

    lax.fori_loop(0, NP, across, 0)
    pl.semaphore_wait(sem, NF - 1 + 2 * NP - 1)


class Exchange:
    def __init__(self, src, dst, sems, along_frame, sends=None, takes=None):
        self.src, self.dst, (self.ssem, self.rsem) = src, dst, sems
        self.along_frame, self.sends, self.takes = along_frame, sends, takes
        self.me_f, self.me_p = lax.axis_index("frame"), lax.axis_index("patch")
        self.me = self.me_f if along_frame else self.me_p
        self.n = NF if along_frame else NP

    def copy(self, to, src, dst):
        where = (to, self.me_p) if self.along_frame else (self.me_f, to)
        return rcopy(src, dst, self.ssem.at[0], self.rsem.at[0], *where)

    def start(self):
        def body(k, _):
            to = lax.rem(self.me + k, self.n)

            def go():
                self.copy(to, self.src.at[to], self.dst.at[self.me]).start()

            if self.sends is None:
                go()
            else:
                pl.when(self.sends[0](to))(go)
            return 0

        lax.fori_loop(1, self.n, body, 0)

    def all_of(self, cases, act):
        for condition, count in cases or [(None, self.n - 1)]:

            def go(count=count):
                to = lax.rem(self.me + 1, self.n)
                act(self.copy(to, self.src.at[0:count], self.dst.at[0:count]))

            if condition is None:
                go()
            else:
                pl.when(condition)(go)

    def land(self):
        self.all_of(self.takes, lambda c: c.wait_recv())

    def gone(self):
        self.all_of(self.sends and self.sends[1], lambda c: c.wait_send())


class Sum:
    def __init__(self, term, bufs, x_first):
        self.term, self.x_first = term, x_first
        (self.r0, self.t2, self.t3, self.in1, self.up1, self.full1, self.in2, self.up2, self.full2, self.r3,
         self.ssem, self.rsem) = bufs
        self.z, self.y_hi, self.core, self.x, self.y_lo = place()
        self.y = self.y_hi * 2 + self.y_lo
        self.cols = term.shape[-1]

    def chunk(self, stage, j):
        if stage == 1:
            if self.x_first:
                return self.term.at[:, :, self.core, j]
            return self.term.at[:, j // 2, self.core, :, lax.rem(j, 2)]
        if self.x_first:
            return self.t2.at[:, j // 2, lax.rem(j, 2)]
        return self.t2.at[:, j]

    def ring(self, stage):
        if (stage == 1) == self.x_first:
            return self.x, lambda j: device(self.z, self.y, self.core, j)
        return self.y, lambda j: device(self.z, j, self.core, self.x)

    def core_copy(self, x, y_lo):
        other = 1 - self.core
        s = x * 2 + y_lo
        return rcopy(
            self.term.at[:, :, other, x, y_lo], self.r0.at[:, :, x, y_lo], self.ssem.at[s], self.rsem.at[s],
            *device(self.z, self.y, other, self.x),
        )

    def core_add(self, x, y_lo):
        self.core_copy(x, y_lo).wait_recv()

        def body(z, _):
            mine = self.term[z, :, self.core, x, y_lo].astype(F32)
            self.term[z, :, self.core, x, y_lo] = (mine + self.r0[z, :, x, y_lo].astype(F32)).astype(BF16)
            return 0

        lax.fori_loop(0, 8, body, 0)

    def first(self, stage):
        me, at = self.ring(stage)
        far = lax.rem(me + 2, 4)
        into = self.in1 if stage == 1 else self.in2
        s = 8 if stage == 1 else 12
        return [
            rcopy(
                self.chunk(stage, far).at[4 * h : 4 * h + 4], into.at[h], self.ssem.at[s + h], self.rsem.at[s + h],
                *at(lax.rem(me + (1, 3)[h], 4)),
            )
            for h in range(2)
        ]

    def second(self, stage):
        me, at = self.ring(stage)
        up = self.up1 if stage == 1 else self.up2
        full = self.full1 if stage == 1 else self.full2
        s = 10 if stage == 1 else 14
        return [
            rcopy(up.at[h], full.at[h], self.ssem.at[s + h], self.rsem.at[s + h], *at(lax.rem(me + (1, 3)[h], 4)))
            for h in range(2)
        ]

    def relay(self, stage):
        me, _ = self.ring(stage)
        into = self.in1 if stage == 1 else self.in2
        up = self.up1 if stage == 1 else self.up2
        firsts, seconds = self.first(stage), self.second(stage)
        for h in range(2):
            mine = self.chunk(stage, lax.rem(me + (1, 3)[h], 4))
            firsts[h].wait_recv()

            def body(z, _):
                a = 4 * h + z
                b = 4 * (1 - h) + z
                up[h, a] = (mine[a].astype(F32) + into[h, z].astype(F32)).astype(BF16)
                up[h, b] = mine[b]
                return 0

            lax.fori_loop(0, 4, body, 0)
            seconds[h].start()

    def ring_add(self, stage):
        me, _ = self.ring(stage)
        full = self.full1 if stage == 1 else self.full2
        out = self.t2 if stage == 1 else self.t3
        mine = self.chunk(stage, me)
        for c in self.second(stage):
            c.wait_recv()

        def body(z, _):
            total = mine[z].astype(F32) + full[0, z].astype(F32) + full[1, z].astype(F32)
            out[z] = total.astype(BF16)
            return 0

        lax.fori_loop(0, 8, body, 0)

    def last(self):
        out = []
        for k in range(1, 8):
            to = lax.rem(self.z + k, 8)
            out.append(
                rcopy(
                    self.t3.at[to], self.r3.at[k - 1], self.ssem.at[15 + k], self.rsem.at[15 + k],
                    *device(to, self.y, self.core, self.x),
                )
            )
        return out

    def total(self):
        total = self.t3[self.z].astype(F32)
        for c in self.last():
            c.wait_recv()
        for k in range(7):
            total = total + self.r3[k].astype(F32)
        return total

    def start(self, copies):
        for c in copies:
            c.start()

    def gone(self):
        for x in range(4):
            for y_lo in range(2):
                self.core_copy(x, y_lo).wait_send()
        for c in self.first(1) + self.second(1) + self.first(2) + self.second(2) + self.last():
            c.wait_send()


class PlaneSum(Sum):
    def __init__(self, term, bufs):
        self.term = term
        self.r0, self.t3, self.inp, self.r3, self.ssem, self.rsem, self.psem, self.qsem = bufs
        self.z, self.y_hi, self.core, self.x, self.y_lo = place()
        self.y = self.y_hi * 2 + self.y_lo

    def plane(self, act):
        def body(k, _):
            to = lax.rem(self.x * 4 + self.y + k, 16)
            x, y = to // 4, lax.rem(to, 4)
            act(
                rcopy(
                    self.term.at[:, y // 2, self.core, x, lax.rem(y, 2)], self.inp.at[k - 1],
                    self.psem.at[k - 1], self.qsem.at[k - 1], *device(self.z, y, self.core, x),
                )
            )
            return 0

        lax.fori_loop(1, 16, body, 0)

    def plane_add(self):
        self.plane(lambda c: c.wait_recv())

        def body(z, _):
            total = self.term[z, self.y_hi, self.core, self.x, self.y_lo].astype(F32)
            for k in range(15):
                total = total + self.inp[k, z].astype(F32)
            self.t3[z] = total.astype(BF16)
            return 0

        lax.fori_loop(0, 8, body, 0)

    def gone(self):
        for x in range(4):
            for y_lo in range(2):
                self.core_copy(x, y_lo).wait_send()
        self.plane(lambda c: c.wait_send())
        for c in self.last():
            c.wait_send()


def sum_scratch(cols, x_first):
    mid = (2, 2) if x_first else (4,)
    tile = (16, cols)
    return [
        pltpu.VMEM((8, 2, 4, 2) + tile, BF16),
        pltpu.VMEM((8,) + mid + tile, BF16),
        pltpu.VMEM((8,) + tile, BF16),
        pltpu.VMEM((2, 4) + mid + tile, BF16),
        pltpu.VMEM((2, 8) + mid + tile, BF16),
        pltpu.VMEM((2, 8) + mid + tile, BF16),
        pltpu.VMEM((2, 4) + tile, BF16),
        pltpu.VMEM((2, 8) + tile, BF16),
        pltpu.VMEM((2, 8) + tile, BF16),
        pltpu.VMEM((7,) + tile, BF16),
        pltpu.SemaphoreType.DMA((23,)),
        pltpu.SemaphoreType.DMA((23,)),
    ]


def plane_scratch(cols):
    tile = (16, cols)
    return [
        pltpu.VMEM((8, 2, 4, 2) + tile, BF16),
        pltpu.VMEM((8,) + tile, BF16),
        pltpu.VMEM((15, 8) + tile, BF16),
        pltpu.VMEM((7,) + tile, BF16),
        pltpu.SemaphoreType.DMA((23,)),
        pltpu.SemaphoreType.DMA((23,)),
        pltpu.SemaphoreType.DMA((15,)),
        pltpu.SemaphoreType.DMA((15,)),
    ]


NSUM = 12
TR = 2 * PAD


def whole_kernel(
    stream, upstream, noise, mod, pos, memo, so_hbm, sqkv_hbm, wqkv_hbm, wp_hbm, wps_hbm,
    gs_out, recv_b0, recv_b1, tot_a, tot_b, tot_p,
    so, sqkv, wqkv, wp, wps, wsem,
    xbuf, ubuf, nbuf, gainbuf, send_n, recv_n, send_u, recv_u, ssem, rsem, ssem_u, rsem_u, lsem,
    send_s, recv_s, ssem_s, rsem_s,
    bias, nv, uv, nt, proj, g, o, dqkv, ot, tprobs,
    gn, recv_gn, ssem_n, rsem_n,
    sopad, gosbuf, send_g, recv_g, ssem_g, rsem_g,
    kq, probs, send_b0, ssem_b0, rsem_b0, send_b1, ssem_b1, rsem_b1,
    term_a, term_b, term_p, *sum_bufs,
):
    me_f, me_p = lax.axis_index("frame"), lax.axis_index("patch")
    owner = me_f < BUSY
    loads = [
        pltpu.make_async_copy(src, dst, wsem.at[i])
        for i, (src, dst) in enumerate(
            ((sqkv_hbm, sqkv), (wqkv_hbm, wqkv), (wp_hbm, wp), (wps_hbm, wps), (so_hbm, so))
        )
    ]
    for c in loads:
        c.start()
    sum_a = Sum(term_a, sum_bufs[0:NSUM], True)
    sum_b = Sum(term_b, sum_bufs[NSUM : 2 * NSUM], False)
    sum_p = PlaneSum(term_p, sum_bufs[2 * NSUM :])

    counter = lax.broadcasted_iota(jnp.int32, (1, 128), 1).astype(F32)
    frequency = jnp.exp(-jnp.log(10000.0) * counter / 128)
    waves = []
    for f in range(2):
        angles = noise[f].astype(F32) * frequency
        waves.append(jnp.concatenate([jnp.cos(angles), jnp.sin(angles)], axis=1))
    embedding = jnp.concatenate(waves * 4, axis=0).astype(BF16)
    gainbuf[...] = 1.0 + dot(embedding, mod[...], 1, 0)

    def gain():
        return jnp.broadcast_to(gainbuf[...].reshape(1, 8, D), (TR // 8, 8, D)).reshape(TR, D)

    def inverse_of(x):
        return lax.rsqrt(jnp.mean(x * x, axis=-1, keepdims=True) + 1e-06)

    xbuf[216:TR] = jnp.zeros((8, D), F32)
    ubuf[216:TR] = jnp.zeros((8, D), F32)
    xbuf[0 : 2 * TOK] = stream[...].astype(F32).reshape(2 * TOK, D)
    ubuf[0 : 2 * TOK] = upstream[...].astype(F32).reshape(2 * TOK, D)
    x = xbuf[...]
    nbuf[...] = x * inverse_of(x) * gain()

    def pack(i, _):
        rows = pl.ds(pl.multiple_of(i * 8, 8), 8)
        for buf, to in ((nbuf, send_n), (ubuf, send_u)):
            part = buf[rows]
            to[i] = jnp.concatenate([part[:, 0:512], part[:, 512:1024]], axis=0).astype(BF16)
        return 0

    lax.fori_loop(0, BUSY, pack, 0)

    @pl.when(jnp.logical_not(owner))
    def _():
        recv_n[...] = jnp.zeros(recv_n.shape, BF16)
        recv_u[...] = jnp.zeros(recv_u.shape, BF16)

    barrier()
    to_owners = [(owner, BUSY - 1), (jnp.logical_not(owner), BUSY)]
    from_all = [(owner, NF - 1)]
    out_n = Exchange(send_n, recv_n, (ssem, rsem), True, (lambda d: d < BUSY, to_owners), from_all)
    out_u = Exchange(send_u, recv_u, (ssem_u, rsem_u), True, (lambda d: d < BUSY, to_owners), from_all)
    out_n.start()
    out_l = [
        pltpu.make_async_copy(send_n.at[me_f], recv_n.at[me_f], lsem.at[0]),
        pltpu.make_async_copy(send_u.at[me_f], recv_u.at[me_f], lsem.at[1]),
    ]

    @pl.when(owner)
    def _():
        out_l[0].start()
        out_l[1].start()

    loads[0].wait()
    send_s[:, :, 96:PAD] = jnp.zeros((NP, 3, 16, 128), BF16)
    for j in range(4):
        v = []
        for f in range(2):
            q0 = sqkv[:, f, 128 * j : 128 * j + 128].astype(F32)
            k0 = sqkv[:, f, 512 + 128 * j : 640 + 128 * j].astype(F32)
            m0, m1 = swap_lanes(q0, k0)
            send_s[2 * j, f, 0:TOK] = m0.astype(BF16)
            send_s[2 * j + 1, f, 0:TOK] = m1.astype(BF16)
            v.append(sqkv[:, f, 1024 + 128 * j : 1152 + 128 * j].astype(F32))
        m0, m1 = swap_lanes(v[0], v[1])
        send_s[2 * j, 2, 0:TOK] = m0.astype(BF16)
        send_s[2 * j + 1, 2, 0:TOK] = m1.astype(BF16)
    recv_s[me_p] = send_s[me_p]
    sopad[208:TR] = jnp.zeros((16, 512), BF16)
    loads[4].wait()
    sopad[0 : 2 * TOK] = so[...].astype(F32).reshape(2 * TOK, 512).astype(BF16)

    table = jnp.concatenate(
        [pos[...].astype(F32), memo[...].astype(F32), jnp.zeros((3, F), F32)], axis=0
    ).astype(BF16)
    frame_col = lax.rem(lax.broadcasted_iota(jnp.int32, (F, 128), 1), F)
    at_col = lax.broadcasted_iota(jnp.int32, (F, 128), 0) == frame_col
    at_row = lax.broadcasted_iota(jnp.int32, (F, F), 0) == lax.broadcasted_iota(jnp.int32, (F, F), 1)
    asked = dot(table, jnp.where(at_col, 1.0, 0.0).astype(BF16), 1, 0)
    held = dot(jnp.where(at_row, 1.0, 0.0).astype(BF16), table, 1, 1)
    key_frame = lax.broadcasted_iota(jnp.int32, (F, 128), 0).astype(F32)
    seen = held[:, 0:1] <= asked[0:1]
    for m in range(4):
        seen = jnp.logical_or(seen, key_frame == asked[1 + m : 2 + m])
    bias[...] = jnp.where(seen, 0.0, NEG).astype(F32)

    i = lax.broadcasted_iota(jnp.int32, (ROWS, ROWS), 1)
    wanted = lax.rem(i // 2, SLOT) * F + (i // 8) * 2 + lax.rem(i, 2)
    order = jnp.where(lax.broadcasted_iota(jnp.int32, (ROWS, ROWS), 0) == wanted, 1.0, 0.0).astype(BF16)

    def arrived(ref):
        x = ref[...].astype(F32)
        x = jnp.concatenate([x[:, 0:8], x[:, 8:16]], axis=2).reshape(ROWS, D).astype(BF16)
        return dot(order, x, 1, 0).astype(BF16)

    out_n.gone()
    out_u.start()
    head_x = Exchange(send_s, recv_s, (ssem_s, rsem_s), False)
    head_x.start()

    out_n.land()

    @pl.when(owner)
    def _():
        out_l[0].wait()

    loads[1].wait()

    nv[...] = arrived(recv_n)
    nt[...] = nv[...].T

    def project(c, _):
        cols = pl.ds(pl.multiple_of(c * 512, 512), 512)
        proj[:, cols] = dot(nv[...], wqkv[:, cols], 1, 0).astype(BF16)
        return 0

    lax.fori_loop(0, 6, project, 0)

    low_t = lax.broadcasted_iota(jnp.int32, (F, 128), 1) < E

    def two_heads(x):
        x = x.astype(F32)
        return jnp.concatenate([jnp.where(low_t, x, 0.0), jnp.where(low_t, 0.0, x)], axis=0).astype(BF16)

    def cols_of(j, base):
        return pl.ds(pl.multiple_of(base + j * 128, 128), 128)

    slots = [slice(F * s, F * s + F) for s in range(SLOT)]

    def temporal_probs(j, _):
        made = []
        for rows in slots:
            k = (proj[rows, cols_of(j, D)].astype(F32) * SCALE).astype(BF16)
            st = dot(k, two_heads(proj[rows, cols_of(j, 0)]), 1, 1) + bias[...]
            e = jnp.exp(st - jnp.max(st, axis=0, keepdims=True))
            made.append((e * (1.0 / jnp.sum(e, axis=0, keepdims=True))).astype(BF16))
        for rows, p in zip(slots, made):
            tprobs[j, rows] = p
        return 0

    lax.fori_loop(0, 8, temporal_probs, 0)

    out_u.land()

    @pl.when(owner)
    def _():
        out_l[1].wait()

    loads[2].wait()

    uv[...] = arrived(recv_u)

    def project_g(c, _):
        cols = pl.ds(pl.multiple_of(c * 512, 512), 512)
        g[:, cols] = dot(uv[...], wp[cols, :], 1, 1).astype(BF16)
        return 0

    lax.fori_loop(0, 2, project_g, 0)

    def pair(j, _):
        held = []
        for rows in slots:
            k, v = proj[rows, cols_of(j, D)], proj[rows, cols_of(j, 2 * D)]
            q, gr = two_heads(proj[rows, cols_of(j, 0)]), two_heads(g[rows, cols_of(j, 0)])
            pb = tprobs[j, rows]
            p = pb.astype(F32)
            dp = dot((v.astype(F32) * SCALE).astype(BF16), gr, 1, 1)
            ds = (p * (dp - jnp.sum(p * dp, axis=0, keepdims=True))).astype(BF16)
            held.append((q, k, v, gr, pb, ds))
        made = [
            (dot(pb, v, 0, 0), dot(ds, k, 0, 0), dot(ds, q, 1, 0), dot(pb, gr, 1, 0))
            for q, k, v, gr, pb, ds in held
        ]
        for rows, (out, dq, dk, dv) in zip(slots, made):
            o[rows, cols_of(j, 0)] = jnp.where(low_t, out[0:F], out[F : 2 * F]).astype(BF16)
            dqkv[rows, cols_of(j, 0)] = jnp.where(low_t, dq[0:F], dq[F : 2 * F]).astype(BF16)
            dqkv[rows, cols_of(j, D)] = dk.astype(BF16)
            dqkv[rows, cols_of(j, 2 * D)] = dv.astype(BF16)
        return 0

    lax.fori_loop(0, 8, pair, 0)

    back = dot(order, dot(dqkv[...], wqkv[...], 1, 1).astype(BF16), 0, 0).reshape(NF, 8, D)
    gn[...] = jnp.concatenate([back[:, :, 0:512], back[:, :, 512:1024]], axis=1).astype(BF16)
    back_x = Exchange(gn, recv_gn, (ssem_n, rsem_n), True, (lambda d: owner, from_all), to_owners)
    back_x.start()
    back_l = pltpu.make_async_copy(gn.at[me_f], recv_gn.at[me_f], lsem.at[2])

    @pl.when(owner)
    def _():
        back_l.start()

    ot[...] = o[...].T
    z, y_hi, core, x, y_lo = place()

    def weights(cx, cy):
        p = cx * 2 + cy
        r = dot(nt[...], dqkv[:, pl.ds(pl.multiple_of(p * 384, 128), 384)], 1, 0)
        r = r.reshape(8, 2, 2, 32, 384)
        s = dot(ot[...], uv[:, pl.ds(pl.multiple_of(p * 128, 128), 128)], 1, 0)
        s = s.reshape(8, 2, 2, 32, 128)
        term_a[:, :, :, cx, cy, :, 0:384] = r[:, :, :, 0:16].astype(BF16)
        term_a[:, :, :, cx, cy, :, 384:512] = s[:, :, :, 0:16].astype(BF16)
        sum_a.core_copy(cx, cy).start()
        term_b[:, :, :, cx, cy, :, 0:384] = r[:, :, :, 16:32].astype(BF16)
        term_b[:, :, :, cx, cy, :, 384:512] = s[:, :, :, 16:32].astype(BF16)
        sum_b.core_copy(cx, cy).start()

    def cores(cx, cy):
        sum_a.core_add(cx, cy)
        sum_b.core_add(cx, cy)

    turns = [(2, 0), (2, 1), (1, 0), (3, 0), (0, 0), (1, 1), (3, 1), (0, 1)]
    turns = [(lax.rem(x + dx, 4), lax.rem(y_lo + dy, 2)) for dx, dy in turns]
    for n, turn in enumerate(turns):
        weights(*turn)
        if n >= 2:
            cores(*turns[n - 2])
        if n == 3:
            sum_a.start(sum_a.first(1))
        if n == 6:
            sum_b.start(sum_b.first(1))
    cores(*turns[-2])
    cores(*turns[-1])

    sum_a.relay(1)

    head_x.land()
    low = lax.broadcasted_iota(jnp.int32, (SP, 128), 1) < E
    dead = lax.rem(lax.broadcasted_iota(jnp.int32, (SP, 128), 0), PAD) >= TOK
    dead_bias = jnp.where(dead, NEG, 0.0).astype(F32)
    for f in range(2):
        x = recv_s[:, f].reshape(SP, 128).astype(F32)
        kq[...] = jnp.where(low, pltpu.roll(x, E, 1) * SCALE, 0.0).astype(BF16)
        for b in range(SP // 128):
            rows = slice(b * 128, b * 128 + 128)
            st = dot(kq[...], x[rows].astype(BF16), 1, 1) + dead_bias
            e = jnp.exp(st - jnp.max(st, axis=0, keepdims=True))
            probs[f, :, rows] = (e * (1.0 / jnp.sum(e, axis=0, keepdims=True))).astype(BF16)
    loads[3].wait()

    back_x.land()

    @pl.when(owner)
    def _():
        back_l.wait()

    came = recv_gn[0:BUSY].astype(F32)
    scaled = jnp.concatenate([came[:, 0:8], came[:, 8:16]], axis=2).reshape(TR, D) * gain()
    x = xbuf[...]
    inverse = inverse_of(x)
    inner = jnp.mean(x * scaled, axis=-1, keepdims=True)
    gs = (ubuf[...] + inverse * scaled - x * (inverse * inverse * inverse) * inner).astype(BF16)
    gs_out[...] = gs
    gos = dot(gs, wps[...], 1, 1)
    for j in range(4):
        gosbuf[j] = gos[:, 128 * j : 128 * j + 128]
    for j in range(4):
        m0, m1 = swap_lanes(gosbuf[j, pl.ds(0, PAD, stride=2)], gosbuf[j, pl.ds(1, PAD, stride=2)])
        send_g[2 * j] = m0.astype(BF16)
        send_g[2 * j + 1] = m1.astype(BF16)
    cot_x = Exchange(send_g, recv_g, (ssem_g, rsem_g), False)
    cot_x.start()
    recv_g[me_p] = send_g[me_p]
    tp = dot(sopad[...], gs, 0, 0)
    for p in range(NP):
        term_p[:, :, :, p // 2, p % 2] = tp[:, 128 * p : 128 * p + 128].reshape(8, 2, 2, 16, 128).astype(BF16)
        sum_p.core_copy(p // 2, p % 2).start()

    sum_b.relay(1)

    for p in range(NP):
        sum_p.core_add(p // 2, p % 2)
    sum_p.plane(lambda c: c.start())

    sum_a.ring_add(1)
    sum_a.start(sum_a.first(2))

    cot_x.land()

    g_all = recv_g[...].reshape(SP, 128)
    v_all = recv_s[:, 2].reshape(SP, 128).astype(F32)

    def spatial(f):
        dv = dot(probs[f], g_all, 1, 0)
        qk = recv_s[:, f].reshape(SP, 128)
        kq[...] = jnp.where(low if f == 0 else jnp.logical_not(low), v_all * SCALE, 0.0).astype(BF16)
        for b in range(SP // 128):
            rows = slice(b * 128, b * 128 + 128)
            p = probs[f, :, rows].astype(F32)
            dp = dot(kq[...], g_all[rows], 1, 1)
            ds = p * (dp - jnp.sum(p * dp, axis=0, keepdims=True))
            probs[f, :, rows] = ds.astype(BF16)
        dk = dot(probs[f], qk, 1, 0)
        dq = dot(probs[f], qk, 0, 0)
        return jnp.where(low, dk, dq).astype(BF16).reshape(NP, PAD, 128), dv

    send_b0[...], dv0 = spatial(0)
    token0 = Exchange(send_b0, recv_b0, (ssem_b0, rsem_b0), False)
    token0.start()
    recv_b0[me_p] = send_b0[me_p]

    sum_b.ring_add(1)
    sum_b.start(sum_b.first(2))

    send_b1[:, 0], dv1 = spatial(1)
    send_b1[:, 1] = jnp.where(low, dv0, dv1).astype(BF16).reshape(NP, PAD, 128)

    sum_a.relay(2)
    token1 = Exchange(send_b1, recv_b1, (ssem_b1, rsem_b1), False)
    token1.start()
    recv_b1[me_p] = send_b1[me_p]
    sum_b.relay(2)

    sum_p.plane_add()
    sum_p.start(sum_p.last())

    for s in (sum_a, sum_b):
        s.ring_add(2)
        s.start(s.last())

    token0.land()
    token1.land()
    tot_a[...] = sum_a.total()
    tot_b[...] = sum_b.total()
    tot_p[...] = sum_p.total()

    for e in (out_u, back_x, head_x, cot_x, token0, token1):
        e.gone()
    for s in (sum_a, sum_b, sum_p):
        s.gone()


def finish_kernel(gs, back0, back1, tot_a, tot_b, tot_p, gs_out, out, out_s, out_q, out_t):
    gs_out[...] = gs[0 : 2 * TOK].astype(F32).reshape(TOK, 2, D).astype(BF16)
    for i, total in enumerate((tot_a, tot_b)):
        out_q[16 * i : 16 * i + 16] = total[:, 0:384]
        out_t[16 * i : 16 * i + 16] = total[:, 384:512]
    out_s[...] = tot_p[...]
    for j in range(4):
        c = 128 * j
        for f in range(2):
            part = back0 if f == 0 else back1.at[:, 0]
            k, q = swap_lanes(part[2 * j].astype(F32), part[2 * j + 1].astype(F32))
            out[:, f, c : c + 128] = q[0:TOK].astype(BF16)
            out[:, f, 512 + c : 640 + c] = k[0:TOK].astype(BF16)
        v = swap_lanes(back1[2 * j, 1].astype(F32), back1[2 * j + 1, 1].astype(F32))
        for f in range(2):
            out[:, f, 1024 + c : 1152 + c] = v[f][0:TOK].astype(BF16)


def shards(
    stream,
    spatial_out,
    spatial_qkv,
    upstream,
    proj_spatial,
    qkv_temporal,
    proj_temporal,
    mod_weight,
    noise_steps,
    positions,
    memory,
):
    vmem = pl.BlockSpec(memory_space=pltpu.VMEM)
    smem = pl.BlockSpec(memory_space=pltpu.SMEM)
    hbm = pl.BlockSpec(memory_space=pl.ANY)

    def arr(*shape, dtype=BF16):
        return pltpu.VMEM(shape, dtype)

    def pair_of(n):
        return [pltpu.SemaphoreType.DMA((n,)), pltpu.SemaphoreType.DMA((n,))]

    def shapes(outs):
        return [jax.ShapeDtypeStruct(s, t) for s, t in outs]

    def by_token(tensor):
        return jnp.transpose(tensor, (1, 0, 2))

    scratch = (
        [
            arr(TOK, 2, 512),
            arr(TOK, 2, 1536),
            arr(D, 3 * D),
            arr(D, D),
            arr(512, D),
            pltpu.SemaphoreType.DMA((5,)),
            arr(TR, D, dtype=F32),
            arr(TR, D, dtype=F32),
            arr(TR, D, dtype=F32),
            arr(8, D, dtype=F32),
            arr(NF, 16, 512),
            arr(NF, 16, 512),
            arr(NF, 16, 512),
            arr(NF, 16, 512),
        ]
        + pair_of(1)
        + pair_of(1)
        + [pltpu.SemaphoreType.DMA((3,)), arr(NP, 3, PAD, 128), arr(NP, 3, PAD, 128)]
        + pair_of(1)
        + [
            arr(F, 128, dtype=F32),
            arr(ROWS, D),
            arr(ROWS, D),
            arr(D, ROWS),
            arr(ROWS, 3 * D),
            arr(ROWS, D),
            arr(ROWS, D),
            arr(ROWS, 3 * D),
            arr(D, ROWS),
            arr(8, ROWS, 128),
            arr(NF, 16, 512),
            arr(NF, 16, 512),
        ]
        + pair_of(1)
        + [arr(TR, 512), arr(4, TR, 128, dtype=F32), arr(NP, PAD, 128), arr(NP, PAD, 128)]
        + pair_of(1)
        + [arr(SP, 128), arr(2, SP, SP), arr(NP, PAD, 128)]
        + pair_of(1)
        + [arr(NP, 2, PAD, 128)]
        + pair_of(1)
        + [arr(8, 2, 2, 4, 2, 16, 512), arr(8, 2, 2, 4, 2, 16, 512), arr(8, 2, 2, 4, 2, 16, 128)]
        + sum_scratch(512, True)
        + sum_scratch(512, False)
        + plane_scratch(128)
    )
    made = pl.pallas_call(
        whole_kernel,
        out_shape=shapes(
            [
                ((TR, D), BF16),
                ((NP, PAD, 128), BF16),
                ((NP, 2, PAD, 128), BF16),
                ((16, 512), F32),
                ((16, 512), F32),
                ((16, 128), F32),
            ]
        ),
        in_specs=[vmem] * 2 + [smem] + [vmem] * 3 + [hbm] * 5,
        out_specs=[vmem] * 6,
        scratch_shapes=scratch,
        compiler_params=pltpu.CompilerParams(vmem_limit_bytes=VLIMIT, collective_id=0, has_side_effects=True),
    )(
        by_token(stream),
        by_token(upstream),
        noise_steps,
        mod_weight,
        positions.reshape(1, F),
        memory.T,
        by_token(spatial_out),
        by_token(spatial_qkv),
        qkv_temporal,
        proj_temporal,
        proj_spatial,
    )
    grad_stream, grad_spatial_qkv, grad_s, grad_q, grad_t = pl.pallas_call(
        finish_kernel,
        out_shape=shapes(
            [
                ((TOK, 2, D), BF16),
                ((TOK, 2, 1536), BF16),
                ((16, 128), F32),
                ((32, 384), F32),
                ((32, 128), F32),
            ]
        ),
        in_specs=[vmem] * 6,
        out_specs=[vmem] * 5,
    )(*made)
    return (by_token(grad_stream), by_token(grad_spatial_qkv), grad_s, grad_q, grad_t)


def solution(mesh):
    in_specs = (
        P("frame", "patch", None),
        P("frame", "patch", None),
        P("frame", "patch", None),
        P("frame", "patch", None),
        P(),
        P(),
        P(),
        P(),
        P("frame"),
        P(),
        P(),
    )
    out_specs = (
        P("frame", "patch", None),
        P("frame", "patch", None),
        P("frame", "patch"),
        P("frame", "patch"),
        P("frame", "patch"),
    )
    return jax.shard_map(shards, mesh=mesh, in_specs=in_specs, out_specs=out_specs, check_vma=False)
```

```python
import functools

import jax
import jax.numpy as jnp
from jax import lax
from jax.experimental import pallas as pl
from jax.experimental.pallas import tpu as pltpu
from jax.sharding import PartitionSpec as P

MESH = pl.DeviceIdType.MESH
F32 = jnp.float32
BF16 = jnp.bfloat16
D = 1024
E = 64
F = 64
NF = 32
NP = 8
TOK = 110
PAD = 112
SLOT = 4
BUSY = 28
ROWS = F * SLOT
SP = NP * PAD
SCALE = E ** (-0.5)
NEG = -1e30
VLIMIT = 61 * 1024 * 1024


def rcopy(src, dst, ssem, rsem, f, p):
    return pltpu.make_async_remote_copy(
        src_ref=src, dst_ref=dst, send_sem=ssem, recv_sem=rsem, device_id=(f, p), device_id_type=MESH
    )


def swap_halves(a, b):
    axis = a.ndim - 2
    low = lax.broadcasted_iota(jnp.int32, a.shape, axis) < 4
    return jnp.where(low, a, pltpu.roll(b, 4, axis)), jnp.where(low, pltpu.roll(a, 4, axis), b)


def swap_lanes(a, b):
    low = lax.broadcasted_iota(jnp.int32, a.shape, 1) < E
    return jnp.where(low, a, pltpu.roll(b, E, 1)), jnp.where(low, pltpu.roll(a, E, 1), b)


def dot(a, b, da, db):
    return lax.dot_general(a, b, (((da,), (db,)), ((), ())), preferred_element_type=F32)


def place():
    me_f, me_p = lax.axis_index("frame"), lax.axis_index("patch")
    z, y_hi, core = me_f // 4, lax.rem(me_f // 2, 2), lax.rem(me_f, 2)
    x, y_lo = me_p // 2, lax.rem(me_p, 2)
    return z, y_hi, core, x, y_lo


def device(z, y, core, x):
    return z * 4 + (y // 2) * 2 + core, x * 2 + lax.rem(y, 2)


def barrier():
    me_f, me_p = lax.axis_index("frame"), lax.axis_index("patch")
    z, y_hi, core, x, y_lo = place()
    sem = pltpu.get_barrier_semaphore()

    def greet(f, p):
        pl.semaphore_signal(sem, inc=1, device_id=(f, p), device_id_type=MESH)

    def frames(k, _):
        greet(lax.rem(me_f + k, NF), me_p)
        return 0

    lax.fori_loop(1, NF, frames, 0)

    def patches(k, _):
        greet(me_f, lax.rem(me_p + k, NP))
        return 0

    lax.fori_loop(1, NP, patches, 0)

    def across(k, _):
        greet(*device(z, (1 - y_hi) * 2 + lax.rem(k, 2), core, k // 2))
        return 0

    lax.fori_loop(0, NP, across, 0)
    pl.semaphore_wait(sem, NF - 1 + 2 * NP - 1)


class Exchange:
    def __init__(self, src, dst, sems, along_frame, sends=None, takes=None):
        self.src, self.dst, (self.ssem, self.rsem) = src, dst, sems
        self.along_frame, self.sends, self.takes = along_frame, sends, takes
        self.me_f, self.me_p = lax.axis_index("frame"), lax.axis_index("patch")
        self.me = self.me_f if along_frame else self.me_p
        self.n = NF if along_frame else NP

    def copy(self, to, src, dst):
        where = (to, self.me_p) if self.along_frame else (self.me_f, to)
        return rcopy(src, dst, self.ssem.at[0], self.rsem.at[0], *where)

    def start(self):
        def body(k, _):
            to = lax.rem(self.me + k, self.n)

            def go():
                self.copy(to, self.src.at[to], self.dst.at[self.me]).start()

            if self.sends is None:
                go()
            else:
                pl.when(self.sends[0](to))(go)
            return 0

        lax.fori_loop(1, self.n, body, 0)

    def all_of(self, cases, act):
        for condition, count in cases or [(None, self.n - 1)]:

            def go(count=count):
                to = lax.rem(self.me + 1, self.n)
                act(self.copy(to, self.src.at[0:count], self.dst.at[0:count]))

            if condition is None:
                go()
            else:
                pl.when(condition)(go)

    def land(self):
        self.all_of(self.takes, lambda c: c.wait_recv())

    def gone(self):
        self.all_of(self.sends and self.sends[1], lambda c: c.wait_send())


class Sum:
    def __init__(self, term, bufs, x_first):
        self.term, self.x_first = term, x_first
        (self.r0, self.t2, self.t3, self.in1, self.up1, self.full1, self.in2, self.up2, self.full2, self.r3,
         self.ssem, self.rsem) = bufs
        self.z, self.y_hi, self.core, self.x, self.y_lo = place()
        self.y = self.y_hi * 2 + self.y_lo
        self.cols = term.shape[-1]

    def chunk(self, stage, j):
        if stage == 1:
            if self.x_first:
                return self.term.at[:, :, self.core, j]
            return self.term.at[:, j // 2, self.core, :, lax.rem(j, 2)]
        if self.x_first:
            return self.t2.at[:, j // 2, lax.rem(j, 2)]
        return self.t2.at[:, j]

    def ring(self, stage):
        if (stage == 1) == self.x_first:
            return self.x, lambda j: device(self.z, self.y, self.core, j)
        return self.y, lambda j: device(self.z, j, self.core, self.x)

    def core_copy(self, x, y_lo):
        other = 1 - self.core
        s = x * 2 + y_lo
        return rcopy(
            self.term.at[:, :, other, x, y_lo], self.r0.at[:, :, x, y_lo], self.ssem.at[s], self.rsem.at[s],
            *device(self.z, self.y, other, self.x),
        )

    def core_add(self, x, y_lo):
        self.core_copy(x, y_lo).wait_recv()

        for z in range(0, 8, 4):
            rows = slice(z, z + 4)
            mine = self.term[rows, :, self.core, x, y_lo].astype(F32)
            self.term[rows, :, self.core, x, y_lo] = (mine + self.r0[rows, :, x, y_lo].astype(F32)).astype(BF16)

    def first(self, stage):
        me, at = self.ring(stage)
        far = lax.rem(me + 2, 4)
        into = self.in1 if stage == 1 else self.in2
        s = 8 if stage == 1 else 14
        return [
            rcopy(
                self.chunk(stage, far).at[4 * h : 4 * h + 4], into.at[h], self.ssem.at[s + h], self.rsem.at[s + h],
                *at(lax.rem(me + (1, 3)[h], 4)),
            )
            for h in range(2)
        ]

    def plain(self, stage):
        me, at = self.ring(stage)
        full = self.full1 if stage == 1 else self.full2
        s = 10 if stage == 1 else 16
        out = []
        for h in range(2):
            to = lax.rem(me + (1, 3)[h], 4)
            rows = slice(4 - 4 * h, 8 - 4 * h)
            out.append(
                rcopy(
                    self.chunk(stage, to).at[rows], full.at[h, rows], self.ssem.at[s + h], self.rsem.at[s + h], *at(to)
                )
            )
        return out

    def second(self, stage):
        me, at = self.ring(stage)
        up = self.up1 if stage == 1 else self.up2
        full = self.full1 if stage == 1 else self.full2
        s = 12 if stage == 1 else 18
        return [
            rcopy(
                up.at[h], full.at[h, 4 * h : 4 * h + 4], self.ssem.at[s + h], self.rsem.at[s + h],
                *at(lax.rem(me + (1, 3)[h], 4)),
            )
            for h in range(2)
        ]

    def relay(self, stage):
        me, _ = self.ring(stage)
        into = self.in1 if stage == 1 else self.in2
        up = self.up1 if stage == 1 else self.up2
        firsts, seconds = self.first(stage), self.second(stage)
        for h in range(2):
            mine = self.chunk(stage, lax.rem(me + (1, 3)[h], 4))
            firsts[h].wait_recv()
            up[h] = (mine[4 * h : 4 * h + 4].astype(F32) + into[h].astype(F32)).astype(BF16)
            seconds[h].start()

    def ring_add(self, stage):
        me, _ = self.ring(stage)
        full = self.full1 if stage == 1 else self.full2
        out = self.t2 if stage == 1 else self.t3
        mine = self.chunk(stage, me)
        for c in self.plain(stage) + self.second(stage):
            c.wait_recv()

        def body(z, _):
            total = mine[z].astype(F32) + full[0, z].astype(F32) + full[1, z].astype(F32)
            out[z] = total.astype(BF16)
            return 0

        lax.fori_loop(0, 8, body, 0)

    def last(self):
        out = []
        for k in range(1, 8):
            to = lax.rem(self.z + k, 8)
            out.append(
                rcopy(
                    self.t3.at[to], self.r3.at[k - 1], self.ssem.at[19 + k], self.rsem.at[19 + k],
                    *device(to, self.y, self.core, self.x),
                )
            )
        return out

    def total(self):
        total = self.t3[self.z].astype(F32)
        for c in self.last():
            c.wait_recv()
        for k in range(7):
            total = total + self.r3[k].astype(F32)
        return total

    def start(self, copies):
        for c in copies:
            c.start()

    def gone(self):
        for x in range(4):
            for y_lo in range(2):
                self.core_copy(x, y_lo).wait_send()
        for stage in (1, 2):
            for c in self.first(stage) + self.plain(stage) + self.second(stage):
                c.wait_send()
        for c in self.last():
            c.wait_send()


class SmallSum(Sum):
    def __init__(self, term, bufs):
        self.term = term
        self.r0, self.zin, self.t3, self.pin, self.ssem, self.rsem, self.psem, self.qsem = bufs
        self.z, self.y_hi, self.core, self.x, self.y_lo = place()
        self.y = self.y_hi * 2 + self.y_lo

    def along_z(self):
        out = []
        for k in range(1, 8):
            to = lax.rem(self.z + k, 8)
            out.append(
                rcopy(
                    self.term.at[to, :, self.core], self.zin.at[k - 1], self.ssem.at[7 + k], self.rsem.at[7 + k],
                    *device(to, self.y, self.core, self.x),
                )
            )
        return out

    def z_add(self):
        total = self.term[self.z, :, self.core].astype(F32)
        for c in self.along_z():
            c.wait_recv()
        for k in range(7):
            total = total + self.zin[k].astype(F32)
        self.t3[...] = total.astype(BF16)

    def plane(self, act):
        def body(k, _):
            to = lax.rem(self.x * 4 + self.y + k, 16)
            x, y = to // 4, lax.rem(to, 4)
            act(
                rcopy(
                    self.t3.at[y // 2, x, lax.rem(y, 2)], self.pin.at[k - 1],
                    self.psem.at[k - 1], self.qsem.at[k - 1], *device(self.z, y, self.core, x),
                )
            )
            return 0

        lax.fori_loop(1, 16, body, 0)

    def total(self):
        total = self.t3[self.y_hi, self.x, self.y_lo].astype(F32)
        self.plane(lambda c: c.wait_recv())
        for k in range(15):
            total = total + self.pin[k].astype(F32)
        return total

    def gone(self):
        for x in range(4):
            for y_lo in range(2):
                self.core_copy(x, y_lo).wait_send()
        for c in self.along_z():
            c.wait_send()
        self.plane(lambda c: c.wait_send())


def sum_scratch(cols, x_first):
    mid = (2, 2) if x_first else (4,)
    tile = (16, cols)
    return [
        pltpu.VMEM((8, 2, 4, 2) + tile, BF16),
        pltpu.VMEM((8,) + mid + tile, BF16),
        pltpu.VMEM((8,) + tile, BF16),
        pltpu.VMEM((2, 4) + mid + tile, BF16),
        pltpu.VMEM((2, 4) + mid + tile, BF16),
        pltpu.VMEM((2, 8) + mid + tile, BF16),
        pltpu.VMEM((2, 4) + tile, BF16),
        pltpu.VMEM((2, 4) + tile, BF16),
        pltpu.VMEM((2, 8) + tile, BF16),
        pltpu.VMEM((7,) + tile, BF16),
        pltpu.SemaphoreType.DMA((27,)),
        pltpu.SemaphoreType.DMA((27,)),
    ]


def small_scratch(cols):
    tile = (16, cols)
    return [
        pltpu.VMEM((8, 2, 4, 2) + tile, BF16),
        pltpu.VMEM((7, 2, 4, 2) + tile, BF16),
        pltpu.VMEM((2, 4, 2) + tile, BF16),
        pltpu.VMEM((15,) + tile, BF16),
        pltpu.SemaphoreType.DMA((15,)),
        pltpu.SemaphoreType.DMA((15,)),
        pltpu.SemaphoreType.DMA((15,)),
        pltpu.SemaphoreType.DMA((15,)),
    ]


NSUM, NSMALL = 12, 8
TR = 2 * PAD


def whole_kernel(
    stream, upstream, noise, mod, pos, memo, so_hbm, sqkv_hbm, wqkv_hbm, wp_hbm, wps_hbm,
    gs_out, recv_b0, recv_b1, tot_a, tot_b, tot_c, tot_p,
    so, sqkv, wqkv, wp, wps, wsem,
    xbuf, ubuf, nbuf, gainbuf, send_n, recv_n, send_u, recv_u, ssem, rsem, ssem_u, rsem_u, lsem,
    send_s, recv_s, ssem_s, rsem_s,
    bias, nv, uv, nt, proj, g, o, dqkv, ot, tprobs,
    gn, recv_gn, ssem_n, rsem_n,
    sopad, gosbuf, send_g, recv_g, ssem_g, rsem_g,
    kq, probs, send_b0, ssem_b0, rsem_b0, send_b1, ssem_b1, rsem_b1,
    term_a, term_b, term_p, term_c, *sum_bufs,
):
    me_f, me_p = lax.axis_index("frame"), lax.axis_index("patch")
    owner = me_f < BUSY
    loads = [
        pltpu.make_async_copy(src, dst, wsem.at[i])
        for i, (src, dst) in enumerate(
            ((sqkv_hbm, sqkv), (wqkv_hbm, wqkv), (wp_hbm, wp), (wps_hbm, wps), (so_hbm, so))
        )
    ]
    for c in loads:
        c.start()
    sum_a = Sum(term_a, sum_bufs[0:NSUM], True)
    sum_b = Sum(term_b, sum_bufs[NSUM : 2 * NSUM], False)
    sum_p = SmallSum(term_p, sum_bufs[2 * NSUM : 2 * NSUM + NSMALL])
    sum_c = SmallSum(term_c, sum_bufs[2 * NSUM + NSMALL :])

    counter = lax.broadcasted_iota(jnp.int32, (1, 128), 1).astype(F32)
    frequency = jnp.exp(-jnp.log(10000.0) * counter / 128)
    waves = []
    for f in range(2):
        angles = noise[f].astype(F32) * frequency
        waves.append(jnp.concatenate([jnp.cos(angles), jnp.sin(angles)], axis=1))
    embedding = jnp.concatenate(waves * 4, axis=0).astype(BF16)
    gainbuf[...] = 1.0 + dot(embedding, mod[...], 1, 0)

    def gain():
        return jnp.broadcast_to(gainbuf[...].reshape(1, 8, D), (TR // 8, 8, D)).reshape(TR, D)

    def inverse_of(x):
        return lax.rsqrt(jnp.mean(x * x, axis=-1, keepdims=True) + 1e-06)

    xbuf[216:TR] = jnp.zeros((8, D), F32)
    ubuf[216:TR] = jnp.zeros((8, D), F32)
    xbuf[0 : 2 * TOK] = stream[...].astype(F32).reshape(2 * TOK, D)
    ubuf[0 : 2 * TOK] = upstream[...].astype(F32).reshape(2 * TOK, D)
    x = xbuf[...]
    nbuf[...] = x * inverse_of(x) * gain()

    def pack(i, _):
        rows = pl.ds(pl.multiple_of(i * 8, 8), 8)
        for buf, to in ((nbuf, send_n), (ubuf, send_u)):
            part = buf[rows]
            to[i] = jnp.concatenate([part[:, 0:512], part[:, 512:1024]], axis=0).astype(BF16)
        return 0

    lax.fori_loop(0, BUSY, pack, 0)

    @pl.when(jnp.logical_not(owner))
    def _():
        recv_n[...] = jnp.zeros(recv_n.shape, BF16)
        recv_u[...] = jnp.zeros(recv_u.shape, BF16)

    barrier()
    to_owners = [(owner, BUSY - 1), (jnp.logical_not(owner), BUSY)]
    from_all = [(owner, NF - 1)]
    out_n = Exchange(send_n, recv_n, (ssem, rsem), True, (lambda d: d < BUSY, to_owners), from_all)
    out_u = Exchange(send_u, recv_u, (ssem_u, rsem_u), True, (lambda d: d < BUSY, to_owners), from_all)
    out_n.start()
    out_l = [
        pltpu.make_async_copy(send_n.at[me_f], recv_n.at[me_f], lsem.at[0]),
        pltpu.make_async_copy(send_u.at[me_f], recv_u.at[me_f], lsem.at[1]),
    ]

    @pl.when(owner)
    def _():
        out_l[0].start()
        out_l[1].start()

    loads[0].wait()
    send_s[:, :, 96:PAD] = jnp.zeros((NP, 3, 16, 128), BF16)
    for j in range(4):
        v = []
        for f in range(2):
            q0 = sqkv[:, f, 128 * j : 128 * j + 128].astype(F32)
            k0 = sqkv[:, f, 512 + 128 * j : 640 + 128 * j].astype(F32)
            m0, m1 = swap_lanes(q0, k0)
            send_s[2 * j, f, 0:TOK] = m0.astype(BF16)
            send_s[2 * j + 1, f, 0:TOK] = m1.astype(BF16)
            v.append(sqkv[:, f, 1024 + 128 * j : 1152 + 128 * j].astype(F32))
        m0, m1 = swap_lanes(v[0], v[1])
        send_s[2 * j, 2, 0:TOK] = m0.astype(BF16)
        send_s[2 * j + 1, 2, 0:TOK] = m1.astype(BF16)
    recv_s[me_p] = send_s[me_p]
    sopad[208:TR] = jnp.zeros((16, 512), BF16)
    loads[4].wait()
    sopad[0 : 2 * TOK] = so[...].astype(F32).reshape(2 * TOK, 512).astype(BF16)

    table = jnp.concatenate(
        [pos[...].astype(F32), memo[...].astype(F32), jnp.zeros((3, F), F32)], axis=0
    ).astype(BF16)
    frame_col = lax.rem(lax.broadcasted_iota(jnp.int32, (F, 128), 1), F)
    at_col = lax.broadcasted_iota(jnp.int32, (F, 128), 0) == frame_col
    at_row = lax.broadcasted_iota(jnp.int32, (F, F), 0) == lax.broadcasted_iota(jnp.int32, (F, F), 1)
    asked = dot(table, jnp.where(at_col, 1.0, 0.0).astype(BF16), 1, 0)
    held = dot(jnp.where(at_row, 1.0, 0.0).astype(BF16), table, 1, 1)
    key_frame = lax.broadcasted_iota(jnp.int32, (F, 128), 0).astype(F32)
    seen = held[:, 0:1] <= asked[0:1]
    for m in range(4):
        seen = jnp.logical_or(seen, key_frame == asked[1 + m : 2 + m])
    bias[...] = jnp.where(seen, 0.0, NEG).astype(F32)

    i = lax.broadcasted_iota(jnp.int32, (ROWS, ROWS), 1)
    wanted = lax.rem(i // 2, SLOT) * F + (i // 8) * 2 + lax.rem(i, 2)
    order = jnp.where(lax.broadcasted_iota(jnp.int32, (ROWS, ROWS), 0) == wanted, 1.0, 0.0).astype(BF16)

    def arrived(ref):
        x = ref[...].astype(F32)
        x = jnp.concatenate([x[:, 0:8], x[:, 8:16]], axis=2).reshape(ROWS, D).astype(BF16)
        return dot(order, x, 1, 0).astype(BF16)

    out_n.gone()
    out_u.start()
    head_x = Exchange(send_s, recv_s, (ssem_s, rsem_s), False)
    head_x.start()

    out_n.land()

    @pl.when(owner)
    def _():
        out_l[0].wait()

    loads[1].wait()

    nv[...] = arrived(recv_n)
    nt[...] = nv[...].T

    def project(c, _):
        cols = pl.ds(pl.multiple_of(c * 512, 512), 512)
        proj[:, cols] = dot(nv[...], wqkv[:, cols], 1, 0).astype(BF16)
        return 0

    lax.fori_loop(0, 6, project, 0)

    low_t = lax.broadcasted_iota(jnp.int32, (F, 128), 1) < E

    def two_heads(x):
        x = x.astype(F32)
        return jnp.concatenate([jnp.where(low_t, x, 0.0), jnp.where(low_t, 0.0, x)], axis=0).astype(BF16)

    def cols_of(j, base):
        return pl.ds(pl.multiple_of(base + j * 128, 128), 128)

    slots = [slice(F * s, F * s + F) for s in range(SLOT)]

    def temporal_probs(j, _):
        made = []
        for rows in slots:
            k = (proj[rows, cols_of(j, D)].astype(F32) * SCALE).astype(BF16)
            st = dot(k, two_heads(proj[rows, cols_of(j, 0)]), 1, 1) + bias[...]
            e = jnp.exp(st - jnp.max(st, axis=0, keepdims=True))
            made.append((e * (1.0 / jnp.sum(e, axis=0, keepdims=True))).astype(BF16))
        for rows, p in zip(slots, made):
            tprobs[j, rows] = p
        return 0

    lax.fori_loop(0, 8, temporal_probs, 0)

    out_u.land()

    @pl.when(owner)
    def _():
        out_l[1].wait()

    loads[2].wait()

    uv[...] = arrived(recv_u)

    def project_g(c, _):
        cols = pl.ds(pl.multiple_of(c * 512, 512), 512)
        g[:, cols] = dot(uv[...], wp[cols, :], 1, 1).astype(BF16)
        return 0

    lax.fori_loop(0, 2, project_g, 0)

    def pair(j, _):
        held = []
        for rows in slots:
            k, v = proj[rows, cols_of(j, D)], proj[rows, cols_of(j, 2 * D)]
            q, gr = two_heads(proj[rows, cols_of(j, 0)]), two_heads(g[rows, cols_of(j, 0)])
            pb = tprobs[j, rows]
            p = pb.astype(F32)
            dp = dot((v.astype(F32) * SCALE).astype(BF16), gr, 1, 1)
            ds = (p * (dp - jnp.sum(p * dp, axis=0, keepdims=True))).astype(BF16)
            held.append((q, k, v, gr, pb, ds))
        made = [
            (dot(pb, v, 0, 0), dot(ds, k, 0, 0), dot(ds, q, 1, 0), dot(pb, gr, 1, 0))
            for q, k, v, gr, pb, ds in held
        ]
        for rows, (out, dq, dk, dv) in zip(slots, made):
            o[rows, cols_of(j, 0)] = jnp.where(low_t, out[0:F], out[F : 2 * F]).astype(BF16)
            dqkv[rows, cols_of(j, 0)] = jnp.where(low_t, dq[0:F], dq[F : 2 * F]).astype(BF16)
            dqkv[rows, cols_of(j, D)] = dk.astype(BF16)
            dqkv[rows, cols_of(j, 2 * D)] = dv.astype(BF16)
        return 0

    lax.fori_loop(0, 8, pair, 0)

    back = dot(order, dot(dqkv[...], wqkv[...], 1, 1).astype(BF16), 0, 0).reshape(NF, 8, D)
    gn[...] = jnp.concatenate([back[:, :, 0:512], back[:, :, 512:1024]], axis=1).astype(BF16)
    back_x = Exchange(gn, recv_gn, (ssem_n, rsem_n), True, (lambda d: owner, from_all), to_owners)
    back_x.start()
    back_l = pltpu.make_async_copy(gn.at[me_f], recv_gn.at[me_f], lsem.at[2])

    @pl.when(owner)
    def _():
        back_l.start()

    ot[...] = o[...].T
    z, y_hi, core, x, y_lo = place()

    def weights(cx):
        r = dot(nt[...], dqkv[:, pl.ds(pl.multiple_of(cx * 768, 128), 768)], 1, 0)
        s = dot(ot[...], uv[:, pl.ds(pl.multiple_of(cx * 256, 128), 256)], 1, 0)
        for cy in range(2):
            q = r[:, 384 * cy : 384 * cy + 384].reshape(8, 2, 2, 32, 384)
            t = s[:, 128 * cy : 128 * cy + 128].reshape(8, 2, 2, 32, 128)
            term_a[:, :, :, cx, cy, :, 0:384] = q[:, :, :, 0:16].astype(BF16)
            term_a[:, :, :, cx, cy, :, 384:512] = t[:, :, :, 0:16].astype(BF16)
            sum_a.core_copy(cx, cy).start()
            term_b[:, :, :, cx, cy] = q[:, :, :, 16:32].astype(BF16)
            sum_b.core_copy(cx, cy).start()
            term_c[:, :, :, cx, cy] = t[:, :, :, 16:32].astype(BF16)
            sum_c.core_copy(cx, cy).start()

    def cores(cx):
        for cy in range(2):
            sum_a.core_add(cx, cy)
            sum_b.core_add(cx, cy)
            sum_c.core_add(cx, cy)

    turns = [lax.rem(x + dx, 4) for dx in (2, 1, 3, 0)]
    for n, turn in enumerate(turns):
        weights(turn)
        if n >= 1:
            cores(turns[n - 1])
        if n == 1:
            sum_a.start(sum_a.first(1))
    cores(turns[-1])
    sum_a.start(sum_a.plain(1))
    sum_b.start(sum_b.first(1) + sum_b.plain(1))

    head_x.land()
    low = lax.broadcasted_iota(jnp.int32, (SP, 128), 1) < E
    dead = lax.rem(lax.broadcasted_iota(jnp.int32, (SP, 128), 0), PAD) >= TOK
    dead_bias = jnp.where(dead, NEG, 0.0).astype(F32)
    for f in range(2):
        x = recv_s[:, f].reshape(SP, 128).astype(F32)
        kq[...] = jnp.where(low, pltpu.roll(x, E, 1) * SCALE, 0.0).astype(BF16)
        for b in range(SP // 128):
            rows = slice(b * 128, b * 128 + 128)
            st = dot(kq[...], x[rows].astype(BF16), 1, 1) + dead_bias
            e = jnp.exp(st - jnp.max(st, axis=0, keepdims=True))
            probs[f, :, rows] = (e * (1.0 / jnp.sum(e, axis=0, keepdims=True))).astype(BF16)
    loads[3].wait()

    back_x.land()
    sum_c.start(sum_c.along_z())

    @pl.when(owner)
    def _():
        back_l.wait()

    came = recv_gn[0:BUSY].astype(F32)
    scaled = jnp.concatenate([came[:, 0:8], came[:, 8:16]], axis=2).reshape(TR, D) * gain()
    x = xbuf[...]
    inverse = inverse_of(x)
    inner = jnp.mean(x * scaled, axis=-1, keepdims=True)
    gs = (ubuf[...] + inverse * scaled - x * (inverse * inverse * inverse) * inner).astype(BF16)
    gs_out[...] = gs
    gos = dot(gs, wps[...], 1, 1)
    for j in range(4):
        gosbuf[j] = gos[:, 128 * j : 128 * j + 128]
    for j in range(4):
        m0, m1 = swap_lanes(gosbuf[j, pl.ds(0, PAD, stride=2)], gosbuf[j, pl.ds(1, PAD, stride=2)])
        send_g[2 * j] = m0.astype(BF16)
        send_g[2 * j + 1] = m1.astype(BF16)
    cot_x = Exchange(send_g, recv_g, (ssem_g, rsem_g), False)
    cot_x.start()
    recv_g[me_p] = send_g[me_p]
    tp = dot(sopad[...], gs, 0, 0)
    for p in range(NP):
        term_p[:, :, :, p // 2, p % 2] = tp[:, 128 * p : 128 * p + 128].reshape(8, 2, 2, 16, 128).astype(BF16)
        sum_p.core_copy(p // 2, p % 2).start()

    sum_a.relay(1)
    sum_b.relay(1)

    for p in range(NP):
        sum_p.core_add(p // 2, p % 2)
    sum_p.start(sum_p.along_z())

    cot_x.land()

    g_all = recv_g[...].reshape(SP, 128)
    v_all = recv_s[:, 2].reshape(SP, 128).astype(F32)

    def spatial(f):
        dv = dot(probs[f], g_all, 1, 0)
        qk = recv_s[:, f].reshape(SP, 128)
        kq[...] = jnp.where(low if f == 0 else jnp.logical_not(low), v_all * SCALE, 0.0).astype(BF16)
        for b in range(SP // 128):
            rows = slice(b * 128, b * 128 + 128)
            p = probs[f, :, rows].astype(F32)
            dp = dot(kq[...], g_all[rows], 1, 1)
            ds = p * (dp - jnp.sum(p * dp, axis=0, keepdims=True))
            probs[f, :, rows] = ds.astype(BF16)
        dk = dot(probs[f], qk, 1, 0)
        dq = dot(probs[f], qk, 0, 0)
        return jnp.where(low, dk, dq).astype(BF16).reshape(NP, PAD, 128), dv

    send_b0[...], dv0 = spatial(0)
    token0 = Exchange(send_b0, recv_b0, (ssem_b0, rsem_b0), False)
    token0.start()
    recv_b0[me_p] = send_b0[me_p]

    send_b1[:, 0], dv1 = spatial(1)
    send_b1[:, 1] = jnp.where(low, dv0, dv1).astype(BF16).reshape(NP, PAD, 128)

    sum_b.ring_add(1)
    sum_b.start(sum_b.first(2) + sum_b.plain(2))

    sum_a.ring_add(1)
    sum_a.start(sum_a.first(2) + sum_a.plain(2))
    token1 = Exchange(send_b1, recv_b1, (ssem_b1, rsem_b1), False)
    token1.start()
    recv_b1[me_p] = send_b1[me_p]

    sum_b.relay(2)
    sum_a.relay(2)

    sum_c.z_add()
    sum_c.plane(lambda c: c.start())

    for s in (sum_b, sum_a):
        s.ring_add(2)
        s.start(s.last())

    sum_p.z_add()
    sum_p.plane(lambda c: c.start())

    token0.land()
    token1.land()
    tot_a[...] = sum_a.total()
    tot_b[...] = sum_b.total()
    tot_c[...] = sum_c.total()
    tot_p[...] = sum_p.total()

    for e in (out_u, back_x, head_x, cot_x, token0, token1):
        e.gone()
    for s in (sum_a, sum_b, sum_p, sum_c):
        s.gone()


def finish_kernel(gs, back0, back1, tot_a, tot_b, tot_c, tot_p, gs_out, out, out_s, out_q, out_t):
    gs_out[...] = gs[0 : 2 * TOK].astype(F32).reshape(TOK, 2, D).astype(BF16)
    out_q[0:16] = tot_a[:, 0:384]
    out_q[16:32] = tot_b[...]
    out_t[0:16] = tot_a[:, 384:512]
    out_t[16:32] = tot_c[...]
    out_s[...] = tot_p[...]
    for j in range(4):
        c = 128 * j
        for f in range(2):
            part = back0 if f == 0 else back1.at[:, 0]
            k, q = swap_lanes(part[2 * j].astype(F32), part[2 * j + 1].astype(F32))
            out[:, f, c : c + 128] = q[0:TOK].astype(BF16)
            out[:, f, 512 + c : 640 + c] = k[0:TOK].astype(BF16)
        v = swap_lanes(back1[2 * j, 1].astype(F32), back1[2 * j + 1, 1].astype(F32))
        for f in range(2):
            out[:, f, 1024 + c : 1152 + c] = v[f][0:TOK].astype(BF16)


def shards(
    stream,
    spatial_out,
    spatial_qkv,
    upstream,
    proj_spatial,
    qkv_temporal,
    proj_temporal,
    mod_weight,
    noise_steps,
    positions,
    memory,
):
    vmem = pl.BlockSpec(memory_space=pltpu.VMEM)
    smem = pl.BlockSpec(memory_space=pltpu.SMEM)
    hbm = pl.BlockSpec(memory_space=pl.ANY)

    def arr(*shape, dtype=BF16):
        return pltpu.VMEM(shape, dtype)

    def pair_of(n):
        return [pltpu.SemaphoreType.DMA((n,)), pltpu.SemaphoreType.DMA((n,))]

    def shapes(outs):
        return [jax.ShapeDtypeStruct(s, t) for s, t in outs]

    def by_token(tensor):
        return jnp.transpose(tensor, (1, 0, 2))

    scratch = (
        [
            arr(TOK, 2, 512),
            arr(TOK, 2, 1536),
            arr(D, 3 * D),
            arr(D, D),
            arr(512, D),
            pltpu.SemaphoreType.DMA((5,)),
            arr(TR, D, dtype=F32),
            arr(TR, D, dtype=F32),
            arr(TR, D, dtype=F32),
            arr(8, D, dtype=F32),
            arr(NF, 16, 512),
            arr(NF, 16, 512),
            arr(NF, 16, 512),
            arr(NF, 16, 512),
        ]
        + pair_of(1)
        + pair_of(1)
        + [pltpu.SemaphoreType.DMA((3,)), arr(NP, 3, PAD, 128), arr(NP, 3, PAD, 128)]
        + pair_of(1)
        + [
            arr(F, 128, dtype=F32),
            arr(ROWS, D),
            arr(ROWS, D),
            arr(D, ROWS),
            arr(ROWS, 3 * D),
            arr(ROWS, D),
            arr(ROWS, D),
            arr(ROWS, 3 * D),
            arr(D, ROWS),
            arr(8, ROWS, 128),
            arr(NF, 16, 512),
            arr(NF, 16, 512),
        ]
        + pair_of(1)
        + [arr(TR, 512), arr(4, TR, 128, dtype=F32), arr(NP, PAD, 128), arr(NP, PAD, 128)]
        + pair_of(1)
        + [arr(SP, 128), arr(2, SP, SP), arr(NP, PAD, 128)]
        + pair_of(1)
        + [arr(NP, 2, PAD, 128)]
        + pair_of(1)
        + [arr(8, 2, 2, 4, 2, 16, 512), arr(8, 2, 2, 4, 2, 16, 384)]
        + [arr(8, 2, 2, 4, 2, 16, 128), arr(8, 2, 2, 4, 2, 16, 128)]
        + sum_scratch(512, True)
        + sum_scratch(384, False)
        + small_scratch(128)
        + small_scratch(128)
    )
    made = pl.pallas_call(
        whole_kernel,
        out_shape=shapes(
            [
                ((TR, D), BF16),
                ((NP, PAD, 128), BF16),
                ((NP, 2, PAD, 128), BF16),
                ((16, 512), F32),
                ((16, 384), F32),
                ((16, 128), F32),
                ((16, 128), F32),
            ]
        ),
        in_specs=[vmem] * 2 + [smem] + [vmem] * 3 + [hbm] * 5,
        out_specs=[vmem] * 7,
        scratch_shapes=scratch,
        compiler_params=pltpu.CompilerParams(vmem_limit_bytes=VLIMIT, collective_id=0, has_side_effects=True),
    )(
        by_token(stream),
        by_token(upstream),
        noise_steps,
        mod_weight,
        positions.reshape(1, F),
        memory.T,
        by_token(spatial_out),
        by_token(spatial_qkv),
        qkv_temporal,
        proj_temporal,
        proj_spatial,
    )
    grad_stream, grad_spatial_qkv, grad_s, grad_q, grad_t = pl.pallas_call(
        finish_kernel,
        out_shape=shapes(
            [
                ((TOK, 2, D), BF16),
                ((TOK, 2, 1536), BF16),
                ((16, 128), F32),
                ((32, 384), F32),
                ((32, 128), F32),
            ]
        ),
        in_specs=[vmem] * 7,
        out_specs=[vmem] * 5,
    )(*made)
    return (by_token(grad_stream), by_token(grad_spatial_qkv), grad_s, grad_q, grad_t)


def solution(mesh):
    in_specs = (
        P("frame", "patch", None),
        P("frame", "patch", None),
        P("frame", "patch", None),
        P("frame", "patch", None),
        P(),
        P(),
        P(),
        P(),
        P("frame"),
        P(),
        P(),
    )
    out_specs = (
        P("frame", "patch", None),
        P("frame", "patch", None),
        P("frame", "patch"),
        P("frame", "patch"),
        P("frame", "patch"),
    )
    return jax.shard_map(shards, mesh=mesh, in_specs=in_specs, out_specs=out_specs, check_vma=False)
```

```python
import functools

import jax
import jax.numpy as jnp
from jax import lax
from jax.experimental import pallas as pl
from jax.experimental.pallas import tpu as pltpu
from jax.sharding import PartitionSpec as P

MESH = pl.DeviceIdType.MESH
F32 = jnp.float32
BF16 = jnp.bfloat16
D = 1024
E = 64
F = 64
NF = 32
NP = 8
TOK = 110
PAD = 112
SLOT = 4
BUSY = 28
ROWS = F * SLOT
SP = NP * PAD
SCALE = E ** (-0.5)
NEG = -1e30
VLIMIT = 61 * 1024 * 1024


def rcopy(src, dst, ssem, rsem, f, p):
    return pltpu.make_async_remote_copy(
        src_ref=src, dst_ref=dst, send_sem=ssem, recv_sem=rsem, device_id=(f, p), device_id_type=MESH
    )


def swap_halves(a, b):
    axis = a.ndim - 2
    low = lax.broadcasted_iota(jnp.int32, a.shape, axis) < 4
    return jnp.where(low, a, pltpu.roll(b, 4, axis)), jnp.where(low, pltpu.roll(a, 4, axis), b)


def swap_lanes(a, b):
    low = lax.broadcasted_iota(jnp.int32, a.shape, 1) < E
    return jnp.where(low, a, pltpu.roll(b, E, 1)), jnp.where(low, pltpu.roll(a, E, 1), b)


def dot(a, b, da, db):
    return lax.dot_general(a, b, (((da,), (db,)), ((), ())), preferred_element_type=F32)


def place():
    me_f, me_p = lax.axis_index("frame"), lax.axis_index("patch")
    z, y_hi, core = me_f // 4, lax.rem(me_f // 2, 2), lax.rem(me_f, 2)
    x, y_lo = me_p // 2, lax.rem(me_p, 2)
    return z, y_hi, core, x, y_lo


def device(z, y, core, x):
    return z * 4 + (y // 2) * 2 + core, x * 2 + lax.rem(y, 2)


def barrier():
    me_f, me_p = lax.axis_index("frame"), lax.axis_index("patch")
    z, y_hi, core, x, y_lo = place()
    sem = pltpu.get_barrier_semaphore()

    def greet(f, p):
        pl.semaphore_signal(sem, inc=1, device_id=(f, p), device_id_type=MESH)

    def frames(k, _):
        greet(lax.rem(me_f + k, NF), me_p)
        return 0

    lax.fori_loop(1, NF, frames, 0)

    def patches(k, _):
        greet(me_f, lax.rem(me_p + k, NP))
        return 0

    lax.fori_loop(1, NP, patches, 0)

    def across(k, _):
        greet(*device(z, (1 - y_hi) * 2 + lax.rem(k, 2), core, k // 2))
        return 0

    lax.fori_loop(0, NP, across, 0)
    pl.semaphore_wait(sem, NF - 1 + 2 * NP - 1)


class Exchange:
    def __init__(self, src, dst, sems, along_frame, sends=None, takes=None):
        self.src, self.dst, (self.ssem, self.rsem) = src, dst, sems
        self.along_frame, self.sends, self.takes = along_frame, sends, takes
        self.me_f, self.me_p = lax.axis_index("frame"), lax.axis_index("patch")
        self.me = self.me_f if along_frame else self.me_p
        self.n = NF if along_frame else NP

    def copy(self, to, src, dst):
        where = (to, self.me_p) if self.along_frame else (self.me_f, to)
        return rcopy(src, dst, self.ssem.at[0], self.rsem.at[0], *where)

    def start(self):
        def body(k, _):
            to = lax.rem(self.me + k, self.n)

            def go():
                self.copy(to, self.src.at[to], self.dst.at[self.me]).start()

            if self.sends is None:
                go()
            else:
                pl.when(self.sends[0](to))(go)
            return 0

        lax.fori_loop(1, self.n, body, 0)

    def all_of(self, cases, act):
        for condition, count in cases or [(None, self.n - 1)]:

            def go(count=count):
                to = lax.rem(self.me + 1, self.n)
                act(self.copy(to, self.src.at[0:count], self.dst.at[0:count]))

            if condition is None:
                go()
            else:
                pl.when(condition)(go)

    def land(self):
        self.all_of(self.takes, lambda c: c.wait_recv())

    def gone(self):
        self.all_of(self.sends and self.sends[1], lambda c: c.wait_send())


class Sum:
    def __init__(self, term, bufs, x_first):
        self.term, self.x_first = term, x_first
        (self.r0, self.t2, self.t3, self.in1, self.up1, self.full1, self.in2, self.up2, self.full2, self.r3,
         self.ssem, self.rsem) = bufs
        self.z, self.y_hi, self.core, self.x, self.y_lo = place()
        self.y = self.y_hi * 2 + self.y_lo
        self.cols = term.shape[-1]

    def chunk(self, stage, j):
        if stage == 1:
            if self.x_first:
                return self.term.at[:, :, self.core, j]
            return self.term.at[:, j // 2, self.core, :, lax.rem(j, 2)]
        if self.x_first:
            return self.t2.at[:, j // 2, lax.rem(j, 2)]
        return self.t2.at[:, j]

    def ring(self, stage):
        if (stage == 1) == self.x_first:
            return self.x, lambda j: device(self.z, self.y, self.core, j)
        return self.y, lambda j: device(self.z, j, self.core, self.x)

    def core_copy(self, x, y_lo):
        other = 1 - self.core
        s = x * 2 + y_lo
        return rcopy(
            self.term.at[:, :, other, x, y_lo], self.r0.at[:, :, x, y_lo], self.ssem.at[s], self.rsem.at[s],
            *device(self.z, self.y, other, self.x),
        )

    def core_add(self, x, y_lo):
        self.core_copy(x, y_lo).wait_recv()

        for z in range(0, 8, 4):
            rows = slice(z, z + 4)
            mine = self.term[rows, :, self.core, x, y_lo].astype(F32)
            self.term[rows, :, self.core, x, y_lo] = (mine + self.r0[rows, :, x, y_lo].astype(F32)).astype(BF16)

    def first(self, stage):
        me, at = self.ring(stage)
        far = lax.rem(me + 2, 4)
        into = self.in1 if stage == 1 else self.in2
        s = 8 if stage == 1 else 14
        return [
            rcopy(
                self.chunk(stage, far).at[4 * h : 4 * h + 4], into.at[h], self.ssem.at[s + h], self.rsem.at[s + h],
                *at(lax.rem(me + (1, 3)[h], 4)),
            )
            for h in range(2)
        ]

    def plain(self, stage):
        me, at = self.ring(stage)
        full = self.full1 if stage == 1 else self.full2
        s = 10 if stage == 1 else 16
        out = []
        for h in range(2):
            to = lax.rem(me + (1, 3)[h], 4)
            rows = slice(4 - 4 * h, 8 - 4 * h)
            out.append(
                rcopy(
                    self.chunk(stage, to).at[rows], full.at[h, rows], self.ssem.at[s + h], self.rsem.at[s + h], *at(to)
                )
            )
        return out

    def second(self, stage):
        me, at = self.ring(stage)
        up = self.up1 if stage == 1 else self.up2
        full = self.full1 if stage == 1 else self.full2
        s = 12 if stage == 1 else 18
        return [
            rcopy(
                up.at[h], full.at[h, 4 * h : 4 * h + 4], self.ssem.at[s + h], self.rsem.at[s + h],
                *at(lax.rem(me + (1, 3)[h], 4)),
            )
            for h in range(2)
        ]

    def relay(self, stage):
        me, _ = self.ring(stage)
        into = self.in1 if stage == 1 else self.in2
        up = self.up1 if stage == 1 else self.up2
        firsts, seconds = self.first(stage), self.second(stage)
        for h in range(2):
            mine = self.chunk(stage, lax.rem(me + (1, 3)[h], 4))
            firsts[h].wait_recv()
            up[h] = (mine[4 * h : 4 * h + 4].astype(F32) + into[h].astype(F32)).astype(BF16)
            seconds[h].start()

    def ring_add(self, stage):
        me, _ = self.ring(stage)
        full = self.full1 if stage == 1 else self.full2
        out = self.t2 if stage == 1 else self.t3
        mine = self.chunk(stage, me)
        for c in self.plain(stage) + self.second(stage):
            c.wait_recv()

        def body(z, _):
            total = mine[z].astype(F32) + full[0, z].astype(F32) + full[1, z].astype(F32)
            out[z] = total.astype(BF16)
            return 0

        lax.fori_loop(0, 8, body, 0)

    def last(self):
        out = []
        for k in range(1, 8):
            to = lax.rem(self.z + k, 8)
            out.append(
                rcopy(
                    self.t3.at[to], self.r3.at[k - 1], self.ssem.at[19 + k], self.rsem.at[19 + k],
                    *device(to, self.y, self.core, self.x),
                )
            )
        return out

    def total(self):
        total = self.t3[self.z].astype(F32)
        for c in self.last():
            c.wait_recv()
        for k in range(7):
            total = total + self.r3[k].astype(F32)
        return total

    def start(self, copies):
        for c in copies:
            c.start()

    def gone(self):
        for x in range(4):
            for y_lo in range(2):
                self.core_copy(x, y_lo).wait_send()
        for stage in (1, 2):
            for c in self.first(stage) + self.plain(stage) + self.second(stage):
                c.wait_send()
        for c in self.last():
            c.wait_send()


class SmallSum(Sum):
    def __init__(self, term, bufs):
        self.term = term
        self.r0, self.zin, self.t3, self.pin, self.ssem, self.rsem, self.psem, self.qsem = bufs
        self.z, self.y_hi, self.core, self.x, self.y_lo = place()
        self.y = self.y_hi * 2 + self.y_lo

    def along_z(self):
        out = []
        for k in range(1, 8):
            to = lax.rem(self.z + k, 8)
            out.append(
                rcopy(
                    self.term.at[to, :, self.core], self.zin.at[k - 1], self.ssem.at[7 + k], self.rsem.at[7 + k],
                    *device(to, self.y, self.core, self.x),
                )
            )
        return out

    def z_add(self):
        total = self.term[self.z, :, self.core].astype(F32)
        for c in self.along_z():
            c.wait_recv()
        for k in range(7):
            total = total + self.zin[k].astype(F32)
        self.t3[...] = total.astype(BF16)

    def plane(self, act):
        def body(k, _):
            to = lax.rem(self.x * 4 + self.y + k, 16)
            x, y = to // 4, lax.rem(to, 4)
            act(
                rcopy(
                    self.t3.at[y // 2, x, lax.rem(y, 2)], self.pin.at[k - 1],
                    self.psem.at[k - 1], self.qsem.at[k - 1], *device(self.z, y, self.core, x),
                )
            )
            return 0

        lax.fori_loop(1, 16, body, 0)

    def total(self):
        total = self.t3[self.y_hi, self.x, self.y_lo].astype(F32)
        self.plane(lambda c: c.wait_recv())
        for k in range(15):
            total = total + self.pin[k].astype(F32)
        return total

    def gone(self):
        for x in range(4):
            for y_lo in range(2):
                self.core_copy(x, y_lo).wait_send()
        for c in self.along_z():
            c.wait_send()
        self.plane(lambda c: c.wait_send())


class PlaneSum(Sum):
    def __init__(self, term, bufs):
        self.term = term
        self.r0, self.t3, self.inp, self.r3, self.ssem, self.rsem, self.psem, self.qsem = bufs
        self.z, self.y_hi, self.core, self.x, self.y_lo = place()
        self.y = self.y_hi * 2 + self.y_lo

    def plane(self, act):
        def body(k, _):
            to = lax.rem(self.x * 4 + self.y + k, 16)
            x, y = to // 4, lax.rem(to, 4)
            act(
                rcopy(
                    self.term.at[:, y // 2, self.core, x, lax.rem(y, 2)], self.inp.at[k - 1],
                    self.psem.at[k - 1], self.qsem.at[k - 1], *device(self.z, y, self.core, x),
                )
            )
            return 0

        lax.fori_loop(1, 16, body, 0)

    def plane_add(self):
        self.plane(lambda c: c.wait_recv())

        def body(z, _):
            total = self.term[z, self.y_hi, self.core, self.x, self.y_lo].astype(F32)
            for k in range(15):
                total = total + self.inp[k, z].astype(F32)
            self.t3[z] = total.astype(BF16)
            return 0

        lax.fori_loop(0, 8, body, 0)

    def gone(self):
        for x in range(4):
            for y_lo in range(2):
                self.core_copy(x, y_lo).wait_send()
        self.plane(lambda c: c.wait_send())
        for c in self.last():
            c.wait_send()


def sum_scratch(cols, x_first):
    mid = (2, 2) if x_first else (4,)
    tile = (16, cols)
    return [
        pltpu.VMEM((8, 2, 4, 2) + tile, BF16),
        pltpu.VMEM((8,) + mid + tile, BF16),
        pltpu.VMEM((8,) + tile, BF16),
        pltpu.VMEM((2, 4) + mid + tile, BF16),
        pltpu.VMEM((2, 4) + mid + tile, BF16),
        pltpu.VMEM((2, 8) + mid + tile, BF16),
        pltpu.VMEM((2, 4) + tile, BF16),
        pltpu.VMEM((2, 4) + tile, BF16),
        pltpu.VMEM((2, 8) + tile, BF16),
        pltpu.VMEM((7,) + tile, BF16),
        pltpu.SemaphoreType.DMA((27,)),
        pltpu.SemaphoreType.DMA((27,)),
    ]


def small_scratch(cols):
    tile = (16, cols)
    return [
        pltpu.VMEM((8, 2, 4, 2) + tile, BF16),
        pltpu.VMEM((7, 2, 4, 2) + tile, BF16),
        pltpu.VMEM((2, 4, 2) + tile, BF16),
        pltpu.VMEM((15,) + tile, BF16),
        pltpu.SemaphoreType.DMA((15,)),
        pltpu.SemaphoreType.DMA((15,)),
        pltpu.SemaphoreType.DMA((15,)),
        pltpu.SemaphoreType.DMA((15,)),
    ]


def plane_scratch(cols):
    tile = (16, cols)
    return [
        pltpu.VMEM((8, 2, 4, 2) + tile, BF16),
        pltpu.VMEM((8,) + tile, BF16),
        pltpu.VMEM((15, 8) + tile, BF16),
        pltpu.VMEM((7,) + tile, BF16),
        pltpu.SemaphoreType.DMA((27,)),
        pltpu.SemaphoreType.DMA((27,)),
        pltpu.SemaphoreType.DMA((15,)),
        pltpu.SemaphoreType.DMA((15,)),
    ]


NSUM, NSMALL = 12, 8
TR = 2 * PAD


def whole_kernel(
    stream, upstream, noise, mod, pos, memo, so_hbm, sqkv_hbm, wqkv_hbm, wp_hbm, wps_hbm,
    gs_out, recv_b0, recv_b1, tot_a, tot_b, tot_c, tot_p,
    so, sqkv, wqkv, wp, wps, wsem,
    xbuf, ubuf, nbuf, gainbuf, send_n, recv_n, send_u, recv_u, ssem, rsem, ssem_u, rsem_u, lsem,
    send_s, recv_s, ssem_s, rsem_s,
    bias, nv, uv, nt, proj, g, o, dqkv, ot, tprobs,
    gn, recv_gn, ssem_n, rsem_n,
    sopad, gosbuf, send_g, recv_g, ssem_g, rsem_g,
    kq, probs, send_b0, ssem_b0, rsem_b0, send_b1, ssem_b1, rsem_b1,
    term_a, term_b, term_p, term_c, *sum_bufs,
):
    me_f, me_p = lax.axis_index("frame"), lax.axis_index("patch")
    owner = me_f < BUSY
    loads = [
        pltpu.make_async_copy(src, dst, wsem.at[i])
        for i, (src, dst) in enumerate(
            ((sqkv_hbm, sqkv), (wqkv_hbm, wqkv), (wp_hbm, wp), (wps_hbm, wps), (so_hbm, so))
        )
    ]
    for c in loads:
        c.start()
    sum_a = Sum(term_a, sum_bufs[0:NSUM], True)
    sum_b = Sum(term_b, sum_bufs[NSUM : 2 * NSUM], False)
    sum_p = PlaneSum(term_p, sum_bufs[2 * NSUM : 2 * NSUM + NSMALL])
    sum_c = SmallSum(term_c, sum_bufs[2 * NSUM + NSMALL :])

    counter = lax.broadcasted_iota(jnp.int32, (1, 128), 1).astype(F32)
    frequency = jnp.exp(-jnp.log(10000.0) * counter / 128)
    waves = []
    for f in range(2):
        angles = noise[f].astype(F32) * frequency
        waves.append(jnp.concatenate([jnp.cos(angles), jnp.sin(angles)], axis=1))
    embedding = jnp.concatenate(waves * 4, axis=0).astype(BF16)
    gainbuf[...] = 1.0 + dot(embedding, mod[...], 1, 0)

    def gain():
        return jnp.broadcast_to(gainbuf[...].reshape(1, 8, D), (TR // 8, 8, D)).reshape(TR, D)

    def inverse_of(x):
        return lax.rsqrt(jnp.mean(x * x, axis=-1, keepdims=True) + 1e-06)

    xbuf[216:TR] = jnp.zeros((8, D), F32)
    ubuf[216:TR] = jnp.zeros((8, D), F32)
    xbuf[0 : 2 * TOK] = stream[...].astype(F32).reshape(2 * TOK, D)
    ubuf[0 : 2 * TOK] = upstream[...].astype(F32).reshape(2 * TOK, D)
    x = xbuf[...]
    nbuf[...] = x * inverse_of(x) * gain()

    def pack(i, _):
        rows = pl.ds(pl.multiple_of(i * 8, 8), 8)
        for buf, to in ((nbuf, send_n), (ubuf, send_u)):
            part = buf[rows]
            to[i] = jnp.concatenate([part[:, 0:512], part[:, 512:1024]], axis=0).astype(BF16)
        return 0

    lax.fori_loop(0, BUSY, pack, 0)

    @pl.when(jnp.logical_not(owner))
    def _():
        recv_n[...] = jnp.zeros(recv_n.shape, BF16)
        recv_u[...] = jnp.zeros(recv_u.shape, BF16)

    barrier()
    to_owners = [(owner, BUSY - 1), (jnp.logical_not(owner), BUSY)]
    from_all = [(owner, NF - 1)]
    out_n = Exchange(send_n, recv_n, (ssem, rsem), True, (lambda d: d < BUSY, to_owners), from_all)
    out_u = Exchange(send_u, recv_u, (ssem_u, rsem_u), True, (lambda d: d < BUSY, to_owners), from_all)
    out_n.start()
    out_l = [
        pltpu.make_async_copy(send_n.at[me_f], recv_n.at[me_f], lsem.at[0]),
        pltpu.make_async_copy(send_u.at[me_f], recv_u.at[me_f], lsem.at[1]),
    ]

    @pl.when(owner)
    def _():
        out_l[0].start()
        out_l[1].start()

    loads[0].wait()
    send_s[:, :, 96:PAD] = jnp.zeros((NP, 3, 16, 128), BF16)
    for j in range(4):
        v = []
        for f in range(2):
            q0 = sqkv[:, f, 128 * j : 128 * j + 128].astype(F32)
            k0 = sqkv[:, f, 512 + 128 * j : 640 + 128 * j].astype(F32)
            m0, m1 = swap_lanes(q0, k0)
            send_s[2 * j, f, 0:TOK] = m0.astype(BF16)
            send_s[2 * j + 1, f, 0:TOK] = m1.astype(BF16)
            v.append(sqkv[:, f, 1024 + 128 * j : 1152 + 128 * j].astype(F32))
        m0, m1 = swap_lanes(v[0], v[1])
        send_s[2 * j, 2, 0:TOK] = m0.astype(BF16)
        send_s[2 * j + 1, 2, 0:TOK] = m1.astype(BF16)
    recv_s[me_p] = send_s[me_p]
    sopad[208:TR] = jnp.zeros((16, 512), BF16)
    loads[4].wait()
    sopad[0 : 2 * TOK] = so[...].astype(F32).reshape(2 * TOK, 512).astype(BF16)

    table = jnp.concatenate(
        [pos[...].astype(F32), memo[...].astype(F32), jnp.zeros((3, F), F32)], axis=0
    ).astype(BF16)
    frame_col = lax.rem(lax.broadcasted_iota(jnp.int32, (F, 128), 1), F)
    at_col = lax.broadcasted_iota(jnp.int32, (F, 128), 0) == frame_col
    at_row = lax.broadcasted_iota(jnp.int32, (F, F), 0) == lax.broadcasted_iota(jnp.int32, (F, F), 1)
    asked = dot(table, jnp.where(at_col, 1.0, 0.0).astype(BF16), 1, 0)
    held = dot(jnp.where(at_row, 1.0, 0.0).astype(BF16), table, 1, 1)
    key_frame = lax.broadcasted_iota(jnp.int32, (F, 128), 0).astype(F32)
    seen = held[:, 0:1] <= asked[0:1]
    for m in range(4):
        seen = jnp.logical_or(seen, key_frame == asked[1 + m : 2 + m])
    bias[...] = jnp.where(seen, 0.0, NEG).astype(F32)

    i = lax.broadcasted_iota(jnp.int32, (ROWS, ROWS), 1)
    wanted = lax.rem(i // 2, SLOT) * F + (i // 8) * 2 + lax.rem(i, 2)
    order = jnp.where(lax.broadcasted_iota(jnp.int32, (ROWS, ROWS), 0) == wanted, 1.0, 0.0).astype(BF16)

    def arrived(ref):
        x = ref[...].astype(F32)
        x = jnp.concatenate([x[:, 0:8], x[:, 8:16]], axis=2).reshape(ROWS, D).astype(BF16)
        return dot(order, x, 1, 0).astype(BF16)

    out_n.gone()
    out_u.start()
    head_x = Exchange(send_s, recv_s, (ssem_s, rsem_s), False)
    head_x.start()

    out_n.land()

    @pl.when(owner)
    def _():
        out_l[0].wait()

    loads[1].wait()

    nv[...] = arrived(recv_n)
    nt[...] = nv[...].T

    def project(c, _):
        cols = pl.ds(pl.multiple_of(c * 512, 512), 512)
        proj[:, cols] = dot(nv[...], wqkv[:, cols], 1, 0).astype(BF16)
        return 0

    lax.fori_loop(0, 6, project, 0)

    low_t = lax.broadcasted_iota(jnp.int32, (F, 128), 1) < E

    def two_heads(x):
        x = x.astype(F32)
        return jnp.concatenate([jnp.where(low_t, x, 0.0), jnp.where(low_t, 0.0, x)], axis=0).astype(BF16)

    def cols_of(j, base):
        return pl.ds(pl.multiple_of(base + j * 128, 128), 128)

    slots = [slice(F * s, F * s + F) for s in range(SLOT)]

    def temporal_probs(j, _):
        made = []
        for rows in slots:
            k = (proj[rows, cols_of(j, D)].astype(F32) * SCALE).astype(BF16)
            st = dot(k, two_heads(proj[rows, cols_of(j, 0)]), 1, 1) + bias[...]
            e = jnp.exp(st - jnp.max(st, axis=0, keepdims=True))
            made.append((e * (1.0 / jnp.sum(e, axis=0, keepdims=True))).astype(BF16))
        for rows, p in zip(slots, made):
            tprobs[j, rows] = p
        return 0

    lax.fori_loop(0, 8, temporal_probs, 0)

    out_u.land()

    @pl.when(owner)
    def _():
        out_l[1].wait()

    loads[2].wait()

    uv[...] = arrived(recv_u)

    def project_g(c, _):
        cols = pl.ds(pl.multiple_of(c * 512, 512), 512)
        g[:, cols] = dot(uv[...], wp[cols, :], 1, 1).astype(BF16)
        return 0

    lax.fori_loop(0, 2, project_g, 0)

    def pair(j, _):
        held = []
        for rows in slots:
            k, v = proj[rows, cols_of(j, D)], proj[rows, cols_of(j, 2 * D)]
            q, gr = two_heads(proj[rows, cols_of(j, 0)]), two_heads(g[rows, cols_of(j, 0)])
            pb = tprobs[j, rows]
            p = pb.astype(F32)
            dp = dot((v.astype(F32) * SCALE).astype(BF16), gr, 1, 1)
            ds = (p * (dp - jnp.sum(p * dp, axis=0, keepdims=True))).astype(BF16)
            held.append((q, k, v, gr, pb, ds))
        made = [
            (dot(pb, v, 0, 0), dot(ds, k, 0, 0), dot(ds, q, 1, 0), dot(pb, gr, 1, 0))
            for q, k, v, gr, pb, ds in held
        ]
        for rows, (out, dq, dk, dv) in zip(slots, made):
            o[rows, cols_of(j, 0)] = jnp.where(low_t, out[0:F], out[F : 2 * F]).astype(BF16)
            dqkv[rows, cols_of(j, 0)] = jnp.where(low_t, dq[0:F], dq[F : 2 * F]).astype(BF16)
            dqkv[rows, cols_of(j, D)] = dk.astype(BF16)
            dqkv[rows, cols_of(j, 2 * D)] = dv.astype(BF16)
        return 0

    lax.fori_loop(0, 8, pair, 0)

    back = dot(order, dot(dqkv[...], wqkv[...], 1, 1).astype(BF16), 0, 0).reshape(NF, 8, D)
    gn[...] = jnp.concatenate([back[:, :, 0:512], back[:, :, 512:1024]], axis=1).astype(BF16)
    back_x = Exchange(gn, recv_gn, (ssem_n, rsem_n), True, (lambda d: owner, from_all), to_owners)
    back_x.start()
    back_l = pltpu.make_async_copy(gn.at[me_f], recv_gn.at[me_f], lsem.at[2])

    @pl.when(owner)
    def _():
        back_l.start()

    ot[...] = o[...].T
    z, y_hi, core, x, y_lo = place()

    def weights(cx):
        r = dot(nt[...], dqkv[:, pl.ds(pl.multiple_of(cx * 768, 128), 768)], 1, 0)
        s = dot(ot[...], uv[:, pl.ds(pl.multiple_of(cx * 256, 128), 256)], 1, 0)
        for cy in range(2):
            q = r[:, 384 * cy : 384 * cy + 384].reshape(8, 2, 2, 32, 384)
            t = s[:, 128 * cy : 128 * cy + 128].reshape(8, 2, 2, 32, 128)
            term_a[:, :, :, cx, cy, :, 0:384] = q[:, :, :, 0:16].astype(BF16)
            term_a[:, :, :, cx, cy, :, 384:512] = t[:, :, :, 0:16].astype(BF16)
            sum_a.core_copy(cx, cy).start()
            term_b[:, :, :, cx, cy] = q[:, :, :, 16:32].astype(BF16)
            sum_b.core_copy(cx, cy).start()
            term_c[:, :, :, cx, cy] = t[:, :, :, 16:32].astype(BF16)
            sum_c.core_copy(cx, cy).start()

    def cores(cx):
        for cy in range(2):
            sum_a.core_add(cx, cy)
            sum_b.core_add(cx, cy)
            sum_c.core_add(cx, cy)

    turns = [lax.rem(x + dx, 4) for dx in (2, 1, 3, 0)]
    for n, turn in enumerate(turns):
        weights(turn)
        if n >= 1:
            cores(turns[n - 1])
        if n == 1:
            sum_a.start(sum_a.first(1))
    cores(turns[-1])
    sum_a.start(sum_a.plain(1))
    sum_b.start(sum_b.first(1) + sum_b.plain(1))

    head_x.land()
    low = lax.broadcasted_iota(jnp.int32, (SP, 128), 1) < E
    dead = lax.rem(lax.broadcasted_iota(jnp.int32, (SP, 128), 0), PAD) >= TOK
    dead_bias = jnp.where(dead, NEG, 0.0).astype(F32)
    for f in range(2):
        x = recv_s[:, f].reshape(SP, 128).astype(F32)
        kq[...] = jnp.where(low, pltpu.roll(x, E, 1) * SCALE, 0.0).astype(BF16)
        for b in range(SP // 128):
            rows = slice(b * 128, b * 128 + 128)
            st = dot(kq[...], x[rows].astype(BF16), 1, 1) + dead_bias
            e = jnp.exp(st - jnp.max(st, axis=0, keepdims=True))
            probs[f, :, rows] = (e * (1.0 / jnp.sum(e, axis=0, keepdims=True))).astype(BF16)
    loads[3].wait()

    back_x.land()
    sum_c.start(sum_c.along_z())

    @pl.when(owner)
    def _():
        back_l.wait()

    came = recv_gn[0:BUSY].astype(F32)
    scaled = jnp.concatenate([came[:, 0:8], came[:, 8:16]], axis=2).reshape(TR, D) * gain()
    x = xbuf[...]
    inverse = inverse_of(x)
    inner = jnp.mean(x * scaled, axis=-1, keepdims=True)
    gs = (ubuf[...] + inverse * scaled - x * (inverse * inverse * inverse) * inner).astype(BF16)
    gs_out[...] = gs
    gos = dot(gs, wps[...], 1, 1)
    for j in range(4):
        gosbuf[j] = gos[:, 128 * j : 128 * j + 128]
    for j in range(4):
        m0, m1 = swap_lanes(gosbuf[j, pl.ds(0, PAD, stride=2)], gosbuf[j, pl.ds(1, PAD, stride=2)])
        send_g[2 * j] = m0.astype(BF16)
        send_g[2 * j + 1] = m1.astype(BF16)
    cot_x = Exchange(send_g, recv_g, (ssem_g, rsem_g), False)
    cot_x.start()
    recv_g[me_p] = send_g[me_p]
    tp = dot(sopad[...], gs, 0, 0)
    for p in range(NP):
        term_p[:, :, :, p // 2, p % 2] = tp[:, 128 * p : 128 * p + 128].reshape(8, 2, 2, 16, 128).astype(BF16)
        sum_p.core_copy(p // 2, p % 2).start()

    sum_a.relay(1)
    sum_b.relay(1)

    for p in range(NP):
        sum_p.core_add(p // 2, p % 2)
    sum_p.plane(lambda c: c.start())

    cot_x.land()

    g_all = recv_g[...].reshape(SP, 128)
    v_all = recv_s[:, 2].reshape(SP, 128).astype(F32)

    def spatial(f):
        dv = dot(probs[f], g_all, 1, 0)
        qk = recv_s[:, f].reshape(SP, 128)
        kq[...] = jnp.where(low if f == 0 else jnp.logical_not(low), v_all * SCALE, 0.0).astype(BF16)
        for b in range(SP // 128):
            rows = slice(b * 128, b * 128 + 128)
            p = probs[f, :, rows].astype(F32)
            dp = dot(kq[...], g_all[rows], 1, 1)
            ds = p * (dp - jnp.sum(p * dp, axis=0, keepdims=True))
            probs[f, :, rows] = ds.astype(BF16)
        dk = dot(probs[f], qk, 1, 0)
        dq = dot(probs[f], qk, 0, 0)
        return jnp.where(low, dk, dq).astype(BF16).reshape(NP, PAD, 128), dv

    send_b0[...], dv0 = spatial(0)
    token0 = Exchange(send_b0, recv_b0, (ssem_b0, rsem_b0), False)
    token0.start()
    recv_b0[me_p] = send_b0[me_p]

    sum_b.ring_add(1)
    sum_b.start(sum_b.first(2) + sum_b.plain(2))

    sum_a.ring_add(1)
    sum_a.start(sum_a.first(2) + sum_a.plain(2))

    send_b1[:, 0], dv1 = spatial(1)
    send_b1[:, 1] = jnp.where(low, dv0, dv1).astype(BF16).reshape(NP, PAD, 128)

    sum_b.relay(2)
    sum_a.relay(2)
    token1 = Exchange(send_b1, recv_b1, (ssem_b1, rsem_b1), False)
    token1.start()
    recv_b1[me_p] = send_b1[me_p]

    sum_c.z_add()
    sum_c.plane(lambda c: c.start())
    sum_p.plane_add()
    sum_p.start(sum_p.last())

    for s in (sum_b, sum_a):
        s.ring_add(2)
        s.start(s.last())

    token0.land()
    token1.land()
    tot_a[...] = sum_a.total()
    tot_b[...] = sum_b.total()
    tot_c[...] = sum_c.total()
    tot_p[...] = sum_p.total()

    for e in (out_u, back_x, head_x, cot_x, token0, token1):
        e.gone()
    for s in (sum_a, sum_b, sum_p, sum_c):
        s.gone()


def finish_kernel(gs, back0, back1, tot_a, tot_b, tot_c, tot_p, gs_out, out, out_s, out_q, out_t):
    gs_out[...] = gs[0 : 2 * TOK].astype(F32).reshape(TOK, 2, D).astype(BF16)
    out_q[0:16] = tot_a[:, 0:384]
    out_q[16:32] = tot_b[...]
    out_t[0:16] = tot_a[:, 384:512]
    out_t[16:32] = tot_c[...]
    out_s[...] = tot_p[...]
    for j in range(4):
        c = 128 * j
        for f in range(2):
            part = back0 if f == 0 else back1.at[:, 0]
            k, q = swap_lanes(part[2 * j].astype(F32), part[2 * j + 1].astype(F32))
            out[:, f, c : c + 128] = q[0:TOK].astype(BF16)
            out[:, f, 512 + c : 640 + c] = k[0:TOK].astype(BF16)
        v = swap_lanes(back1[2 * j, 1].astype(F32), back1[2 * j + 1, 1].astype(F32))
        for f in range(2):
            out[:, f, 1024 + c : 1152 + c] = v[f][0:TOK].astype(BF16)


def shards(
    stream,
    spatial_out,
    spatial_qkv,
    upstream,
    proj_spatial,
    qkv_temporal,
    proj_temporal,
    mod_weight,
    noise_steps,
    positions,
    memory,
):
    vmem = pl.BlockSpec(memory_space=pltpu.VMEM)
    smem = pl.BlockSpec(memory_space=pltpu.SMEM)
    hbm = pl.BlockSpec(memory_space=pl.ANY)

    def arr(*shape, dtype=BF16):
        return pltpu.VMEM(shape, dtype)

    def pair_of(n):
        return [pltpu.SemaphoreType.DMA((n,)), pltpu.SemaphoreType.DMA((n,))]

    def shapes(outs):
        return [jax.ShapeDtypeStruct(s, t) for s, t in outs]

    def by_token(tensor):
        return jnp.transpose(tensor, (1, 0, 2))

    scratch = (
        [
            arr(TOK, 2, 512),
            arr(TOK, 2, 1536),
            arr(D, 3 * D),
            arr(D, D),
            arr(512, D),
            pltpu.SemaphoreType.DMA((5,)),
            arr(TR, D, dtype=F32),
            arr(TR, D, dtype=F32),
            arr(TR, D, dtype=F32),
            arr(8, D, dtype=F32),
            arr(NF, 16, 512),
            arr(NF, 16, 512),
            arr(NF, 16, 512),
            arr(NF, 16, 512),
        ]
        + pair_of(1)
        + pair_of(1)
        + [pltpu.SemaphoreType.DMA((3,)), arr(NP, 3, PAD, 128), arr(NP, 3, PAD, 128)]
        + pair_of(1)
        + [
            arr(F, 128, dtype=F32),
            arr(ROWS, D),
            arr(ROWS, D),
            arr(D, ROWS),
            arr(ROWS, 3 * D),
            arr(ROWS, D),
            arr(ROWS, D),
            arr(ROWS, 3 * D),
            arr(D, ROWS),
            arr(8, ROWS, 128),
            arr(NF, 16, 512),
            arr(NF, 16, 512),
        ]
        + pair_of(1)
        + [arr(TR, 512), arr(4, TR, 128, dtype=F32), arr(NP, PAD, 128), arr(NP, PAD, 128)]
        + pair_of(1)
        + [arr(SP, 128), arr(2, SP, SP), arr(NP, PAD, 128)]
        + pair_of(1)
        + [arr(NP, 2, PAD, 128)]
        + pair_of(1)
        + [arr(8, 2, 2, 4, 2, 16, 512), arr(8, 2, 2, 4, 2, 16, 384)]
        + [arr(8, 2, 2, 4, 2, 16, 128), arr(8, 2, 2, 4, 2, 16, 128)]
        + sum_scratch(512, True)
        + sum_scratch(384, False)
        + plane_scratch(128)
        + small_scratch(128)
    )
    made = pl.pallas_call(
        whole_kernel,
        out_shape=shapes(
            [
                ((TR, D), BF16),
                ((NP, PAD, 128), BF16),
                ((NP, 2, PAD, 128), BF16),
                ((16, 512), F32),
                ((16, 384), F32),
                ((16, 128), F32),
                ((16, 128), F32),
            ]
        ),
        in_specs=[vmem] * 2 + [smem] + [vmem] * 3 + [hbm] * 5,
        out_specs=[vmem] * 7,
        scratch_shapes=scratch,
        compiler_params=pltpu.CompilerParams(vmem_limit_bytes=VLIMIT, collective_id=0, has_side_effects=True),
    )(
        by_token(stream),
        by_token(upstream),
        noise_steps,
        mod_weight,
        positions.reshape(1, F),
        memory.T,
        by_token(spatial_out),
        by_token(spatial_qkv),
        qkv_temporal,
        proj_temporal,
        proj_spatial,
    )
    grad_stream, grad_spatial_qkv, grad_s, grad_q, grad_t = pl.pallas_call(
        finish_kernel,
        out_shape=shapes(
            [
                ((TOK, 2, D), BF16),
                ((TOK, 2, 1536), BF16),
                ((16, 128), F32),
                ((32, 384), F32),
                ((32, 128), F32),
            ]
        ),
        in_specs=[vmem] * 7,
        out_specs=[vmem] * 5,
    )(*made)
    return (by_token(grad_stream), by_token(grad_spatial_qkv), grad_s, grad_q, grad_t)


def solution(mesh):
    in_specs = (
        P("frame", "patch", None),
        P("frame", "patch", None),
        P("frame", "patch", None),
        P("frame", "patch", None),
        P(),
        P(),
        P(),
        P(),
        P("frame"),
        P(),
        P(),
    )
    out_specs = (
        P("frame", "patch", None),
        P("frame", "patch", None),
        P("frame", "patch"),
        P("frame", "patch"),
        P("frame", "patch"),
    )
    return jax.shard_map(shards, mesh=mesh, in_specs=in_specs, out_specs=out_specs, check_vma=False)
```

```python
import functools

import jax
import jax.numpy as jnp
from jax import lax
from jax.experimental import pallas as pl
from jax.experimental.pallas import tpu as pltpu
from jax.sharding import PartitionSpec as P

MESH = pl.DeviceIdType.MESH
F32 = jnp.float32
BF16 = jnp.bfloat16
D = 1024
E = 64
F = 64
NF = 32
NP = 8
TOK = 110
PAD = 112
SLOT = 4
BUSY = 28
ROWS = F * SLOT
SP = NP * PAD
SCALE = E ** (-0.5)
NEG = -1e30
VLIMIT = 61 * 1024 * 1024


def rcopy(src, dst, ssem, rsem, f, p):
    return pltpu.make_async_remote_copy(
        src_ref=src, dst_ref=dst, send_sem=ssem, recv_sem=rsem, device_id=(f, p), device_id_type=MESH
    )


def swap_halves(a, b):
    axis = a.ndim - 2
    low = lax.broadcasted_iota(jnp.int32, a.shape, axis) < 4
    return jnp.where(low, a, pltpu.roll(b, 4, axis)), jnp.where(low, pltpu.roll(a, 4, axis), b)


def swap_lanes(a, b):
    low = lax.broadcasted_iota(jnp.int32, a.shape, 1) < E
    return jnp.where(low, a, pltpu.roll(b, E, 1)), jnp.where(low, pltpu.roll(a, E, 1), b)


def dot(a, b, da, db):
    return lax.dot_general(a, b, (((da,), (db,)), ((), ())), preferred_element_type=F32)


def place():
    me_f, me_p = lax.axis_index("frame"), lax.axis_index("patch")
    z, y_hi, core = me_f // 4, lax.rem(me_f // 2, 2), lax.rem(me_f, 2)
    x, y_lo = me_p // 2, lax.rem(me_p, 2)
    return z, y_hi, core, x, y_lo


def device(z, y, core, x):
    return z * 4 + (y // 2) * 2 + core, x * 2 + lax.rem(y, 2)


def barrier():
    me_f, me_p = lax.axis_index("frame"), lax.axis_index("patch")
    z, y_hi, core, x, y_lo = place()
    sem = pltpu.get_barrier_semaphore()

    def greet(f, p):
        pl.semaphore_signal(sem, inc=1, device_id=(f, p), device_id_type=MESH)

    def frames(k, _):
        greet(lax.rem(me_f + k, NF), me_p)
        return 0

    lax.fori_loop(1, NF, frames, 0)

    def patches(k, _):
        greet(me_f, lax.rem(me_p + k, NP))
        return 0

    lax.fori_loop(1, NP, patches, 0)

    def across(k, _):
        greet(*device(z, (1 - y_hi) * 2 + lax.rem(k, 2), core, k // 2))
        return 0

    lax.fori_loop(0, NP, across, 0)
    pl.semaphore_wait(sem, NF - 1 + 2 * NP - 1)


class Exchange:
    def __init__(self, src, dst, sems, along_frame, sends=None, takes=None):
        self.src, self.dst, (self.ssem, self.rsem) = src, dst, sems
        self.along_frame, self.sends, self.takes = along_frame, sends, takes
        self.me_f, self.me_p = lax.axis_index("frame"), lax.axis_index("patch")
        self.me = self.me_f if along_frame else self.me_p
        self.n = NF if along_frame else NP

    def copy(self, to, src, dst):
        where = (to, self.me_p) if self.along_frame else (self.me_f, to)
        return rcopy(src, dst, self.ssem.at[0], self.rsem.at[0], *where)

    def start(self):
        def body(k, _):
            to = lax.rem(self.me + k, self.n)

            def go():
                self.copy(to, self.src.at[to], self.dst.at[self.me]).start()

            if self.sends is None:
                go()
            else:
                pl.when(self.sends[0](to))(go)
            return 0

        lax.fori_loop(1, self.n, body, 0)

    def all_of(self, cases, act):
        for condition, count in cases or [(None, self.n - 1)]:

            def go(count=count):
                to = lax.rem(self.me + 1, self.n)
                act(self.copy(to, self.src.at[0:count], self.dst.at[0:count]))

            if condition is None:
                go()
            else:
                pl.when(condition)(go)

    def land(self):
        self.all_of(self.takes, lambda c: c.wait_recv())

    def gone(self):
        self.all_of(self.sends and self.sends[1], lambda c: c.wait_send())


class Sum:
    def __init__(self, term, bufs, x_first):
        self.term, self.x_first = term, x_first
        (self.r0, self.t2, self.t3, self.in1, self.up1, self.full1, self.in2, self.up2, self.full2, self.r3,
         self.ssem, self.rsem) = bufs
        self.z, self.y_hi, self.core, self.x, self.y_lo = place()
        self.y = self.y_hi * 2 + self.y_lo
        self.cols = term.shape[-1]

    def chunk(self, stage, j):
        if stage == 1:
            if self.x_first:
                return self.term.at[:, :, self.core, j]
            return self.term.at[:, j // 2, self.core, :, lax.rem(j, 2)]
        if self.x_first:
            return self.t2.at[:, j // 2, lax.rem(j, 2)]
        return self.t2.at[:, j]

    def ring(self, stage):
        if (stage == 1) == self.x_first:
            return self.x, lambda j: device(self.z, self.y, self.core, j)
        return self.y, lambda j: device(self.z, j, self.core, self.x)

    def core_copy(self, x, y_lo):
        other = 1 - self.core
        s = x * 2 + y_lo
        return rcopy(
            self.term.at[:, :, other, x, y_lo], self.r0.at[:, :, x, y_lo], self.ssem.at[s], self.rsem.at[s],
            *device(self.z, self.y, other, self.x),
        )

    def core_add(self, x, y_lo):
        self.core_copy(x, y_lo).wait_recv()

        for z in range(0, 8, 4):
            rows = slice(z, z + 4)
            mine = self.term[rows, :, self.core, x, y_lo].astype(F32)
            self.term[rows, :, self.core, x, y_lo] = (mine + self.r0[rows, :, x, y_lo].astype(F32)).astype(BF16)

    def first(self, stage):
        me, at = self.ring(stage)
        far = lax.rem(me + 2, 4)
        into = self.in1 if stage == 1 else self.in2
        s = 8 if stage == 1 else 14
        return [
            rcopy(
                self.chunk(stage, far).at[4 * h : 4 * h + 4], into.at[h], self.ssem.at[s + h], self.rsem.at[s + h],
                *at(lax.rem(me + (1, 3)[h], 4)),
            )
            for h in range(2)
        ]

    def plain(self, stage):
        me, at = self.ring(stage)
        full = self.full1 if stage == 1 else self.full2
        s = 10 if stage == 1 else 16
        out = []
        for h in range(2):
            to = lax.rem(me + (1, 3)[h], 4)
            rows = slice(4 - 4 * h, 8 - 4 * h)
            out.append(
                rcopy(
                    self.chunk(stage, to).at[rows], full.at[h, rows], self.ssem.at[s + h], self.rsem.at[s + h], *at(to)
                )
            )
        return out

    def second(self, stage):
        me, at = self.ring(stage)
        up = self.up1 if stage == 1 else self.up2
        full = self.full1 if stage == 1 else self.full2
        s = 12 if stage == 1 else 18
        return [
            rcopy(
                up.at[h], full.at[h, 4 * h : 4 * h + 4], self.ssem.at[s + h], self.rsem.at[s + h],
                *at(lax.rem(me + (1, 3)[h], 4)),
            )
            for h in range(2)
        ]

    def relay(self, stage):
        me, _ = self.ring(stage)
        into = self.in1 if stage == 1 else self.in2
        up = self.up1 if stage == 1 else self.up2
        firsts, seconds = self.first(stage), self.second(stage)
        for h in range(2):
            mine = self.chunk(stage, lax.rem(me + (1, 3)[h], 4))
            firsts[h].wait_recv()
            up[h] = (mine[4 * h : 4 * h + 4].astype(F32) + into[h].astype(F32)).astype(BF16)
            seconds[h].start()

    def ring_add(self, stage):
        me, _ = self.ring(stage)
        full = self.full1 if stage == 1 else self.full2
        out = self.t2 if stage == 1 else self.t3
        mine = self.chunk(stage, me)
        for c in self.plain(stage) + self.second(stage):
            c.wait_recv()

        def body(z, _):
            total = mine[z].astype(F32) + full[0, z].astype(F32) + full[1, z].astype(F32)
            out[z] = total.astype(BF16)
            return 0

        lax.fori_loop(0, 8, body, 0)

    def last(self):
        out = []
        for k in range(1, 8):
            to = lax.rem(self.z + k, 8)
            out.append(
                rcopy(
                    self.t3.at[to], self.r3.at[k - 1], self.ssem.at[19 + k], self.rsem.at[19 + k],
                    *device(to, self.y, self.core, self.x),
                )
            )
        return out

    def total(self):
        total = self.t3[self.z].astype(F32)
        for c in self.last():
            c.wait_recv()
        for k in range(7):
            total = total + self.r3[k].astype(F32)
        return total

    def start(self, copies):
        for c in copies:
            c.start()

    def gone(self):
        for x in range(4):
            for y_lo in range(2):
                self.core_copy(x, y_lo).wait_send()
        for stage in (1, 2):
            for c in self.first(stage) + self.plain(stage) + self.second(stage):
                c.wait_send()
        for c in self.last():
            c.wait_send()


class SmallSum(Sum):
    def __init__(self, term, bufs):
        self.term = term
        self.r0, self.zin, self.t3, self.pin, self.ssem, self.rsem, self.psem, self.qsem = bufs
        self.z, self.y_hi, self.core, self.x, self.y_lo = place()
        self.y = self.y_hi * 2 + self.y_lo

    def along_z(self):
        out = []
        for k in range(1, 8):
            to = lax.rem(self.z + k, 8)
            out.append(
                rcopy(
                    self.term.at[to, :, self.core], self.zin.at[k - 1], self.ssem.at[7 + k], self.rsem.at[7 + k],
                    *device(to, self.y, self.core, self.x),
                )
            )
        return out

    def z_add(self):
        total = self.term[self.z, :, self.core].astype(F32)
        for c in self.along_z():
            c.wait_recv()
        for k in range(7):
            total = total + self.zin[k].astype(F32)
        self.t3[...] = total.astype(BF16)

    def plane(self, act):
        def body(k, _):
            to = lax.rem(self.x * 4 + self.y + k, 16)
            x, y = to // 4, lax.rem(to, 4)
            act(
                rcopy(
                    self.t3.at[y // 2, x, lax.rem(y, 2)], self.pin.at[k - 1],
                    self.psem.at[k - 1], self.qsem.at[k - 1], *device(self.z, y, self.core, x),
                )
            )
            return 0

        lax.fori_loop(1, 16, body, 0)

    def total(self):
        total = self.t3[self.y_hi, self.x, self.y_lo].astype(F32)
        self.plane(lambda c: c.wait_recv())
        for k in range(15):
            total = total + self.pin[k].astype(F32)
        return total

    def gone(self):
        for x in range(4):
            for y_lo in range(2):
                self.core_copy(x, y_lo).wait_send()
        for c in self.along_z():
            c.wait_send()
        self.plane(lambda c: c.wait_send())


def sum_scratch(cols, x_first):
    mid = (2, 2) if x_first else (4,)
    tile = (16, cols)
    return [
        pltpu.VMEM((8, 2, 4, 2) + tile, BF16),
        pltpu.VMEM((8,) + mid + tile, BF16),
        pltpu.VMEM((8,) + tile, BF16),
        pltpu.VMEM((2, 4) + mid + tile, BF16),
        pltpu.VMEM((2, 4) + mid + tile, BF16),
        pltpu.VMEM((2, 8) + mid + tile, BF16),
        pltpu.VMEM((2, 4) + tile, BF16),
        pltpu.VMEM((2, 4) + tile, BF16),
        pltpu.VMEM((2, 8) + tile, BF16),
        pltpu.VMEM((7,) + tile, BF16),
        pltpu.SemaphoreType.DMA((27,)),
        pltpu.SemaphoreType.DMA((27,)),
    ]


def small_scratch(cols):
    tile = (16, cols)
    return [
        pltpu.VMEM((8, 2, 4, 2) + tile, BF16),
        pltpu.VMEM((7, 2, 4, 2) + tile, BF16),
        pltpu.VMEM((2, 4, 2) + tile, BF16),
        pltpu.VMEM((15,) + tile, BF16),
        pltpu.SemaphoreType.DMA((15,)),
        pltpu.SemaphoreType.DMA((15,)),
        pltpu.SemaphoreType.DMA((15,)),
        pltpu.SemaphoreType.DMA((15,)),
    ]


NSUM = 12
TR = 2 * PAD


def whole_kernel(
    stream, upstream, noise, mod, pos, memo, so_hbm, sqkv_hbm, wqkv_hbm, wp_hbm, wps_hbm,
    gs_out, recv_b0, recv_b1, tot_a, tot_b, tot_p,
    so, sqkv, wqkv, wp, wps, wsem,
    xbuf, ubuf, nbuf, gainbuf, send_n, recv_n, send_u, recv_u, ssem, rsem, ssem_u, rsem_u, lsem,
    send_s, recv_s, ssem_s, rsem_s,
    bias, nv, uv, nt, proj, g, o, dqkv, ot, tprobs,
    gn, recv_gn, ssem_n, rsem_n,
    sopad, gosbuf, send_g, recv_g, ssem_g, rsem_g,
    kq, probs, send_b0, ssem_b0, rsem_b0, send_b1, ssem_b1, rsem_b1,
    term_a, term_b, term_p, *sum_bufs,
):
    me_f, me_p = lax.axis_index("frame"), lax.axis_index("patch")
    owner = me_f < BUSY
    loads = [
        pltpu.make_async_copy(src, dst, wsem.at[i])
        for i, (src, dst) in enumerate(
            ((sqkv_hbm, sqkv), (wqkv_hbm, wqkv), (wp_hbm, wp), (wps_hbm, wps), (so_hbm, so))
        )
    ]
    for c in loads:
        c.start()
    sum_a = Sum(term_a, sum_bufs[0:NSUM], True)
    sum_b = Sum(term_b, sum_bufs[NSUM : 2 * NSUM], False)
    sum_p = SmallSum(term_p, sum_bufs[2 * NSUM :])

    counter = lax.broadcasted_iota(jnp.int32, (1, 128), 1).astype(F32)
    frequency = jnp.exp(-jnp.log(10000.0) * counter / 128)
    waves = []
    for f in range(2):
        angles = noise[f].astype(F32) * frequency
        waves.append(jnp.concatenate([jnp.cos(angles), jnp.sin(angles)], axis=1))
    embedding = jnp.concatenate(waves * 4, axis=0).astype(BF16)
    gainbuf[...] = 1.0 + dot(embedding, mod[...], 1, 0)

    def gain():
        return jnp.broadcast_to(gainbuf[...].reshape(1, 8, D), (TR // 8, 8, D)).reshape(TR, D)

    def inverse_of(x):
        return lax.rsqrt(jnp.mean(x * x, axis=-1, keepdims=True) + 1e-06)

    xbuf[216:TR] = jnp.zeros((8, D), F32)
    ubuf[216:TR] = jnp.zeros((8, D), F32)
    xbuf[0 : 2 * TOK] = stream[...].astype(F32).reshape(2 * TOK, D)
    ubuf[0 : 2 * TOK] = upstream[...].astype(F32).reshape(2 * TOK, D)
    x = xbuf[...]
    nbuf[...] = x * inverse_of(x) * gain()

    def pack(i, _):
        rows = pl.ds(pl.multiple_of(i * 8, 8), 8)
        for buf, to in ((nbuf, send_n), (ubuf, send_u)):
            part = buf[rows]
            to[i] = jnp.concatenate([part[:, 0:512], part[:, 512:1024]], axis=0).astype(BF16)
        return 0

    lax.fori_loop(0, BUSY, pack, 0)

    @pl.when(jnp.logical_not(owner))
    def _():
        recv_n[...] = jnp.zeros(recv_n.shape, BF16)
        recv_u[...] = jnp.zeros(recv_u.shape, BF16)

    barrier()
    to_owners = [(owner, BUSY - 1), (jnp.logical_not(owner), BUSY)]
    from_all = [(owner, NF - 1)]
    out_n = Exchange(send_n, recv_n, (ssem, rsem), True, (lambda d: d < BUSY, to_owners), from_all)
    out_u = Exchange(send_u, recv_u, (ssem_u, rsem_u), True, (lambda d: d < BUSY, to_owners), from_all)
    out_n.start()
    out_l = [
        pltpu.make_async_copy(send_n.at[me_f], recv_n.at[me_f], lsem.at[0]),
        pltpu.make_async_copy(send_u.at[me_f], recv_u.at[me_f], lsem.at[1]),
    ]

    @pl.when(owner)
    def _():
        out_l[0].start()
        out_l[1].start()

    loads[0].wait()
    send_s[:, :, 96:PAD] = jnp.zeros((NP, 3, 16, 128), BF16)
    for j in range(4):
        v = []
        for f in range(2):
            q0 = sqkv[:, f, 128 * j : 128 * j + 128].astype(F32)
            k0 = sqkv[:, f, 512 + 128 * j : 640 + 128 * j].astype(F32)
            m0, m1 = swap_lanes(q0, k0)
            send_s[2 * j, f, 0:TOK] = m0.astype(BF16)
            send_s[2 * j + 1, f, 0:TOK] = m1.astype(BF16)
            v.append(sqkv[:, f, 1024 + 128 * j : 1152 + 128 * j].astype(F32))
        m0, m1 = swap_lanes(v[0], v[1])
        send_s[2 * j, 2, 0:TOK] = m0.astype(BF16)
        send_s[2 * j + 1, 2, 0:TOK] = m1.astype(BF16)
    recv_s[me_p] = send_s[me_p]
    sopad[208:TR] = jnp.zeros((16, 512), BF16)
    loads[4].wait()
    sopad[0 : 2 * TOK] = so[...].astype(F32).reshape(2 * TOK, 512).astype(BF16)

    table = jnp.concatenate(
        [pos[...].astype(F32), memo[...].astype(F32), jnp.zeros((3, F), F32)], axis=0
    ).astype(BF16)
    frame_col = lax.rem(lax.broadcasted_iota(jnp.int32, (F, 128), 1), F)
    at_col = lax.broadcasted_iota(jnp.int32, (F, 128), 0) == frame_col
    at_row = lax.broadcasted_iota(jnp.int32, (F, F), 0) == lax.broadcasted_iota(jnp.int32, (F, F), 1)
    asked = dot(table, jnp.where(at_col, 1.0, 0.0).astype(BF16), 1, 0)
    held = dot(jnp.where(at_row, 1.0, 0.0).astype(BF16), table, 1, 1)
    key_frame = lax.broadcasted_iota(jnp.int32, (F, 128), 0).astype(F32)
    seen = held[:, 0:1] <= asked[0:1]
    for m in range(4):
        seen = jnp.logical_or(seen, key_frame == asked[1 + m : 2 + m])
    bias[...] = jnp.where(seen, 0.0, NEG).astype(F32)

    i = lax.broadcasted_iota(jnp.int32, (ROWS, ROWS), 1)
    wanted = lax.rem(i // 2, SLOT) * F + (i // 8) * 2 + lax.rem(i, 2)
    order = jnp.where(lax.broadcasted_iota(jnp.int32, (ROWS, ROWS), 0) == wanted, 1.0, 0.0).astype(BF16)

    def arrived(ref):
        x = ref[...].astype(F32)
        x = jnp.concatenate([x[:, 0:8], x[:, 8:16]], axis=2).reshape(ROWS, D).astype(BF16)
        return dot(order, x, 1, 0).astype(BF16)

    out_n.gone()
    out_u.start()
    head_x = Exchange(send_s, recv_s, (ssem_s, rsem_s), False)
    head_x.start()

    out_n.land()

    @pl.when(owner)
    def _():
        out_l[0].wait()

    loads[1].wait()

    nv[...] = arrived(recv_n)
    nt[...] = nv[...].T

    def project(c, _):
        cols = pl.ds(pl.multiple_of(c * 512, 512), 512)
        proj[:, cols] = dot(nv[...], wqkv[:, cols], 1, 0).astype(BF16)
        return 0

    lax.fori_loop(0, 6, project, 0)

    low_t = lax.broadcasted_iota(jnp.int32, (F, 128), 1) < E

    def two_heads(x):
        x = x.astype(F32)
        return jnp.concatenate([jnp.where(low_t, x, 0.0), jnp.where(low_t, 0.0, x)], axis=0).astype(BF16)

    def cols_of(j, base):
        return pl.ds(pl.multiple_of(base + j * 128, 128), 128)

    slots = [slice(F * s, F * s + F) for s in range(SLOT)]

    def temporal_probs(j, _):
        made = []
        for rows in slots:
            k = (proj[rows, cols_of(j, D)].astype(F32) * SCALE).astype(BF16)
            st = dot(k, two_heads(proj[rows, cols_of(j, 0)]), 1, 1) + bias[...]
            e = jnp.exp(st - jnp.max(st, axis=0, keepdims=True))
            made.append((e * (1.0 / jnp.sum(e, axis=0, keepdims=True))).astype(BF16))
        for rows, p in zip(slots, made):
            tprobs[j, rows] = p
        return 0

    lax.fori_loop(0, 8, temporal_probs, 0)

    out_u.land()

    @pl.when(owner)
    def _():
        out_l[1].wait()

    loads[2].wait()

    uv[...] = arrived(recv_u)

    def project_g(c, _):
        cols = pl.ds(pl.multiple_of(c * 512, 512), 512)
        g[:, cols] = dot(uv[...], wp[cols, :], 1, 1).astype(BF16)
        return 0

    lax.fori_loop(0, 2, project_g, 0)

    def pair(j, _):
        held = []
        for rows in slots:
            k, v = proj[rows, cols_of(j, D)], proj[rows, cols_of(j, 2 * D)]
            q, gr = two_heads(proj[rows, cols_of(j, 0)]), two_heads(g[rows, cols_of(j, 0)])
            pb = tprobs[j, rows]
            p = pb.astype(F32)
            dp = dot((v.astype(F32) * SCALE).astype(BF16), gr, 1, 1)
            ds = (p * (dp - jnp.sum(p * dp, axis=0, keepdims=True))).astype(BF16)
            held.append((q, k, v, gr, pb, ds))
        made = [
            (dot(pb, v, 0, 0), dot(ds, k, 0, 0), dot(ds, q, 1, 0), dot(pb, gr, 1, 0))
            for q, k, v, gr, pb, ds in held
        ]
        for rows, (out, dq, dk, dv) in zip(slots, made):
            o[rows, cols_of(j, 0)] = jnp.where(low_t, out[0:F], out[F : 2 * F]).astype(BF16)
            dqkv[rows, cols_of(j, 0)] = jnp.where(low_t, dq[0:F], dq[F : 2 * F]).astype(BF16)
            dqkv[rows, cols_of(j, D)] = dk.astype(BF16)
            dqkv[rows, cols_of(j, 2 * D)] = dv.astype(BF16)
        return 0

    lax.fori_loop(0, 8, pair, 0)

    back = dot(order, dot(dqkv[...], wqkv[...], 1, 1).astype(BF16), 0, 0).reshape(NF, 8, D)
    gn[...] = jnp.concatenate([back[:, :, 0:512], back[:, :, 512:1024]], axis=1).astype(BF16)
    back_x = Exchange(gn, recv_gn, (ssem_n, rsem_n), True, (lambda d: owner, from_all), to_owners)
    back_x.start()
    back_l = pltpu.make_async_copy(gn.at[me_f], recv_gn.at[me_f], lsem.at[2])

    @pl.when(owner)
    def _():
        back_l.start()

    ot[...] = o[...].T
    z, y_hi, core, x, y_lo = place()

    def weights(cx):
        r = dot(nt[...], dqkv[:, pl.ds(pl.multiple_of(cx * 768, 128), 768)], 1, 0)
        s = dot(ot[...], uv[:, pl.ds(pl.multiple_of(cx * 256, 128), 256)], 1, 0)
        for cy in range(2):
            q = r[:, 384 * cy : 384 * cy + 384].reshape(8, 2, 2, 32, 384)
            t = s[:, 128 * cy : 128 * cy + 128].reshape(8, 2, 2, 32, 128)
            term_a[:, :, :, cx, cy, :, 0:384] = q[:, :, :, 0:16].astype(BF16)
            term_a[:, :, :, cx, cy, :, 384:512] = t[:, :, :, 0:16].astype(BF16)
            sum_a.core_copy(cx, cy).start()
            term_b[:, :, :, cx, cy, :, 0:384] = q[:, :, :, 16:32].astype(BF16)
            term_b[:, :, :, cx, cy, :, 384:512] = t[:, :, :, 16:32].astype(BF16)
            sum_b.core_copy(cx, cy).start()

    def cores(cx):
        for cy in range(2):
            sum_a.core_add(cx, cy)
            sum_b.core_add(cx, cy)

    turns = [lax.rem(x + dx, 4) for dx in (2, 1, 3, 0)]
    for n, turn in enumerate(turns):
        weights(turn)
        if n >= 1:
            cores(turns[n - 1])
        if n == 1:
            sum_a.start(sum_a.first(1))
    cores(turns[-1])
    sum_a.start(sum_a.plain(1))
    sum_b.start(sum_b.first(1) + sum_b.plain(1))

    head_x.land()
    low = lax.broadcasted_iota(jnp.int32, (SP, 128), 1) < E
    dead = lax.rem(lax.broadcasted_iota(jnp.int32, (SP, 128), 0), PAD) >= TOK
    dead_bias = jnp.where(dead, NEG, 0.0).astype(F32)
    for f in range(2):
        x = recv_s[:, f].reshape(SP, 128).astype(F32)
        kq[...] = jnp.where(low, pltpu.roll(x, E, 1) * SCALE, 0.0).astype(BF16)
        for b in range(SP // 128):
            rows = slice(b * 128, b * 128 + 128)
            st = dot(kq[...], x[rows].astype(BF16), 1, 1) + dead_bias
            e = jnp.exp(st - jnp.max(st, axis=0, keepdims=True))
            probs[f, :, rows] = (e * (1.0 / jnp.sum(e, axis=0, keepdims=True))).astype(BF16)
    loads[3].wait()

    back_x.land()

    @pl.when(owner)
    def _():
        back_l.wait()

    came = recv_gn[0:BUSY].astype(F32)
    scaled = jnp.concatenate([came[:, 0:8], came[:, 8:16]], axis=2).reshape(TR, D) * gain()
    x = xbuf[...]
    inverse = inverse_of(x)
    inner = jnp.mean(x * scaled, axis=-1, keepdims=True)
    gs = (ubuf[...] + inverse * scaled - x * (inverse * inverse * inverse) * inner).astype(BF16)
    gs_out[...] = gs
    gos = dot(gs, wps[...], 1, 1)
    for j in range(4):
        gosbuf[j] = gos[:, 128 * j : 128 * j + 128]
    for j in range(4):
        m0, m1 = swap_lanes(gosbuf[j, pl.ds(0, PAD, stride=2)], gosbuf[j, pl.ds(1, PAD, stride=2)])
        send_g[2 * j] = m0.astype(BF16)
        send_g[2 * j + 1] = m1.astype(BF16)
    cot_x = Exchange(send_g, recv_g, (ssem_g, rsem_g), False)
    cot_x.start()
    recv_g[me_p] = send_g[me_p]
    tp = dot(sopad[...], gs, 0, 0)
    for p in range(NP):
        term_p[:, :, :, p // 2, p % 2] = tp[:, 128 * p : 128 * p + 128].reshape(8, 2, 2, 16, 128).astype(BF16)
        sum_p.core_copy(p // 2, p % 2).start()

    sum_a.relay(1)
    sum_b.relay(1)

    for p in range(NP):
        sum_p.core_add(p // 2, p % 2)
    sum_p.start(sum_p.along_z())

    cot_x.land()

    g_all = recv_g[...].reshape(SP, 128)
    v_all = recv_s[:, 2].reshape(SP, 128).astype(F32)

    def spatial(f):
        dv = dot(probs[f], g_all, 1, 0)
        qk = recv_s[:, f].reshape(SP, 128)
        kq[...] = jnp.where(low if f == 0 else jnp.logical_not(low), v_all * SCALE, 0.0).astype(BF16)
        for b in range(SP // 128):
            rows = slice(b * 128, b * 128 + 128)
            p = probs[f, :, rows].astype(F32)
            dp = dot(kq[...], g_all[rows], 1, 1)
            ds = p * (dp - jnp.sum(p * dp, axis=0, keepdims=True))
            probs[f, :, rows] = ds.astype(BF16)
        dk = dot(probs[f], qk, 1, 0)
        dq = dot(probs[f], qk, 0, 0)
        return jnp.where(low, dk, dq).astype(BF16).reshape(NP, PAD, 128), dv

    send_b0[...], dv0 = spatial(0)
    token0 = Exchange(send_b0, recv_b0, (ssem_b0, rsem_b0), False)
    token0.start()
    recv_b0[me_p] = send_b0[me_p]

    send_b1[:, 0], dv1 = spatial(1)
    send_b1[:, 1] = jnp.where(low, dv0, dv1).astype(BF16).reshape(NP, PAD, 128)

    sum_b.ring_add(1)
    sum_b.start(sum_b.first(2) + sum_b.plain(2))

    sum_a.ring_add(1)
    sum_a.start(sum_a.first(2) + sum_a.plain(2))

    sum_b.relay(2)
    sum_a.relay(2)
    token1 = Exchange(send_b1, recv_b1, (ssem_b1, rsem_b1), False)
    token1.start()
    recv_b1[me_p] = send_b1[me_p]

    for s in (sum_b, sum_a):
        s.ring_add(2)
        s.start(s.last())

    sum_p.z_add()
    sum_p.plane(lambda c: c.start())

    token0.land()
    token1.land()
    tot_a[...] = sum_a.total()
    tot_b[...] = sum_b.total()
    tot_p[...] = sum_p.total()

    for e in (out_u, back_x, head_x, cot_x, token0, token1):
        e.gone()
    for s in (sum_a, sum_b, sum_p):
        s.gone()


def finish_kernel(gs, back0, back1, tot_a, tot_b, tot_p, gs_out, out, out_s, out_q, out_t):
    gs_out[...] = gs[0 : 2 * TOK].astype(F32).reshape(TOK, 2, D).astype(BF16)
    out_q[0:16] = tot_a[:, 0:384]
    out_q[16:32] = tot_b[:, 0:384]
    out_t[0:16] = tot_a[:, 384:512]
    out_t[16:32] = tot_b[:, 384:512]
    out_s[...] = tot_p[...]
    for j in range(4):
        c = 128 * j
        for f in range(2):
            part = back0 if f == 0 else back1.at[:, 0]
            k, q = swap_lanes(part[2 * j].astype(F32), part[2 * j + 1].astype(F32))
            out[:, f, c : c + 128] = q[0:TOK].astype(BF16)
            out[:, f, 512 + c : 640 + c] = k[0:TOK].astype(BF16)
        v = swap_lanes(back1[2 * j, 1].astype(F32), back1[2 * j + 1, 1].astype(F32))
        for f in range(2):
            out[:, f, 1024 + c : 1152 + c] = v[f][0:TOK].astype(BF16)


def shards(
    stream,
    spatial_out,
    spatial_qkv,
    upstream,
    proj_spatial,
    qkv_temporal,
    proj_temporal,
    mod_weight,
    noise_steps,
    positions,
    memory,
):
    vmem = pl.BlockSpec(memory_space=pltpu.VMEM)
    smem = pl.BlockSpec(memory_space=pltpu.SMEM)
    hbm = pl.BlockSpec(memory_space=pl.ANY)

    def arr(*shape, dtype=BF16):
        return pltpu.VMEM(shape, dtype)

    def pair_of(n):
        return [pltpu.SemaphoreType.DMA((n,)), pltpu.SemaphoreType.DMA((n,))]

    def shapes(outs):
        return [jax.ShapeDtypeStruct(s, t) for s, t in outs]

    def by_token(tensor):
        return jnp.transpose(tensor, (1, 0, 2))

    scratch = (
        [
            arr(TOK, 2, 512),
            arr(TOK, 2, 1536),
            arr(D, 3 * D),
            arr(D, D),
            arr(512, D),
            pltpu.SemaphoreType.DMA((5,)),
            arr(TR, D, dtype=F32),
            arr(TR, D, dtype=F32),
            arr(TR, D, dtype=F32),
            arr(8, D, dtype=F32),
            arr(NF, 16, 512),
            arr(NF, 16, 512),
            arr(NF, 16, 512),
            arr(NF, 16, 512),
        ]
        + pair_of(1)
        + pair_of(1)
        + [pltpu.SemaphoreType.DMA((3,)), arr(NP, 3, PAD, 128), arr(NP, 3, PAD, 128)]
        + pair_of(1)
        + [
            arr(F, 128, dtype=F32),
            arr(ROWS, D),
            arr(ROWS, D),
            arr(D, ROWS),
            arr(ROWS, 3 * D),
            arr(ROWS, D),
            arr(ROWS, D),
            arr(ROWS, 3 * D),
            arr(D, ROWS),
            arr(8, ROWS, 128),
            arr(NF, 16, 512),
            arr(NF, 16, 512),
        ]
        + pair_of(1)
        + [arr(TR, 512), arr(4, TR, 128, dtype=F32), arr(NP, PAD, 128), arr(NP, PAD, 128)]
        + pair_of(1)
        + [arr(SP, 128), arr(2, SP, SP), arr(NP, PAD, 128)]
        + pair_of(1)
        + [arr(NP, 2, PAD, 128)]
        + pair_of(1)
        + [arr(8, 2, 2, 4, 2, 16, 512), arr(8, 2, 2, 4, 2, 16, 512)]
        + [arr(8, 2, 2, 4, 2, 16, 128)]
        + sum_scratch(512, True)
        + sum_scratch(512, False)
        + small_scratch(128)
    )
    made = pl.pallas_call(
        whole_kernel,
        out_shape=shapes(
            [
                ((TR, D), BF16),
                ((NP, PAD, 128), BF16),
                ((NP, 2, PAD, 128), BF16),
                ((16, 512), F32),
                ((16, 512), F32),
                ((16, 128), F32),
            ]
        ),
        in_specs=[vmem] * 2 + [smem] + [vmem] * 3 + [hbm] * 5,
        out_specs=[vmem] * 6,
        scratch_shapes=scratch,
        compiler_params=pltpu.CompilerParams(vmem_limit_bytes=VLIMIT, collective_id=0, has_side_effects=True),
    )(
        by_token(stream),
        by_token(upstream),
        noise_steps,
        mod_weight,
        positions.reshape(1, F),
        memory.T,
        by_token(spatial_out),
        by_token(spatial_qkv),
        qkv_temporal,
        proj_temporal,
        proj_spatial,
    )
    grad_stream, grad_spatial_qkv, grad_s, grad_q, grad_t = pl.pallas_call(
        finish_kernel,
        out_shape=shapes(
            [
                ((TOK, 2, D), BF16),
                ((TOK, 2, 1536), BF16),
                ((16, 128), F32),
                ((32, 384), F32),
                ((32, 128), F32),
            ]
        ),
        in_specs=[vmem] * 6,
        out_specs=[vmem] * 5,
    )(*made)
    return (by_token(grad_stream), by_token(grad_spatial_qkv), grad_s, grad_q, grad_t)


def solution(mesh):
    in_specs = (
        P("frame", "patch", None),
        P("frame", "patch", None),
        P("frame", "patch", None),
        P("frame", "patch", None),
        P(),
        P(),
        P(),
        P(),
        P("frame"),
        P(),
        P(),
    )
    out_specs = (
        P("frame", "patch", None),
        P("frame", "patch", None),
        P("frame", "patch"),
        P("frame", "patch"),
        P("frame", "patch"),
    )
    return jax.shard_map(shards, mesh=mesh, in_specs=in_specs, out_specs=out_specs, check_vma=False)
```
